512 devices in a mesh: paths: 8 (over y, core), tm: 64 (over z, x).
Axes of the slice: x: 4, y: 4, z: 16, core: 2. Of those that a mesh axis runs over, the one named last changes fastest.
Arguments:
- independent_disturbances: bfloat16 [4096, 32, 1024], P('tm', 'paths'), may hold values from -6 to 6
- starting_driver_values: float32 [32, 1024], P('paths'), may hold values from -6 to 6
- correlation_mixer: bfloat16 [1024, 1024], P('paths'), may hold values from -0.1875 to 0.1875
- log_persistence: float32 [1024], replicated, may hold values from -0.034 to 0
- regime_multiplier: float32 [4096], P('tm'), may hold values from 0.5 to 1
- payoff_per_unit_table: bfloat16 [1024, 128], replicated, may hold values from -0.1875 to 0.1875
- short_yield_coefficients: bfloat16 [1024], replicated, may hold values from -0.1875 to 0.1875
Outputs:
- values: float32 [32, 128], P('paths')
The draws below stay inside these ranges and needn't reach their ends.
All inputs are finite; a program needn't handle non-finite values.
Results may differ from the reference program's by a relative error of at most 0.0004.
Values may be sent and summed in bfloat16 or wider, within the bound.
A program may use at most 64 MiB of HBM per device.

```python
import math
import jax
import jax.numpy as jnp
from jax import lax

F = 1024
K = 128
PG = 4
HORIZON = 4096
PATHS = 32
N_PATHS = 8


def draw_log_persistence(key, part):
    key_pick, key_slow, key_fast = jax.random.split(key, 3)
    share = 0.5
    slow_mask = jax.random.uniform(key_pick, (F,), jnp.float32) < share
    slow_low = math.log(min(0.05 / HORIZON, 0.5 / 30.0))
    slow_high = math.log(min(2.0 / HORIZON, 1.0 / 30.0))
    slow_rate = jnp.exp(jax.random.uniform(key_slow, (F,), jnp.float32, slow_low, slow_high))
    fast_rate = jnp.exp(jax.random.uniform(key_fast, (F,), jnp.float32, math.log(1.0 / 50.0), math.log(1.0 / 30.0)))
    return -jnp.where(slow_mask, slow_rate, fast_rate)


def draw_regime_multiplier(key, part):
    key_day, key_size = jax.random.split(key)
    days = jax.random.randint(key_day, (4,), 0, HORIZON)
    sizes = jax.random.uniform(key_size, (4,), jnp.float32, 0.5, 0.8)
    return jnp.ones((HORIZON,), jnp.float32).at[days].set(sizes)


def steps_of(key, shape, cuts, smallest, largest):
    level, own = 1.0, jax.random.fold_in(key, 6)
    for position, shards_of in cuts:
        heights = jnp.exp(jax.random.uniform(jax.random.fold_in(own, position), (shards_of,), jnp.float32, smallest / len(cuts), largest / len(cuts)))
        level = level * jnp.repeat(heights, shape[position] // shards_of).reshape([-1 if axis == position else 1 for axis in range(len(shape))])
    return level


def gaussian(rng, extent, spread, limit, shards=(), held_as=jnp.bfloat16):
    level = steps_of(rng, extent, shards, -0.22, 0.18) if shards else 1.0
    drawn = jax.random.normal(rng, extent, jnp.float32) * spread * level
    return jnp.minimum(jnp.maximum(drawn, -limit), limit).astype(held_as)


def setup_inputs(seed: int = 0) -> dict:
    key_of = jax.random.split(jax.random.key(seed), 8)
    return {
        "independent_disturbances": gaussian(key_of[0], (HORIZON, PATHS, F), 1.0, 6.0, ((0, 64), (1, 8))),
        "starting_driver_values": gaussian(key_of[1], (PATHS, F), 1.0, 6.0, ((0, 8),), jnp.float32),
        "correlation_mixer": gaussian(key_of[2], (F, F), F ** -0.5, 0.1875, ((0, 8),)),
        "log_persistence": draw_log_persistence(jax.random.fold_in(key_of[7], 71), 0),
        "regime_multiplier": draw_regime_multiplier(jax.random.fold_in(key_of[7], 71), 0),
        "payoff_per_unit_table": gaussian(key_of[5], (F, K), F ** -0.5, 0.1875),
        "short_yield_coefficients": gaussian(key_of[6], (F,), F ** -0.5, 0.1875),
    }


def reference(independent_disturbances, starting_driver_values, correlation_mixer, log_persistence, regime_multiplier, payoff_per_unit_table, short_yield_coefficients):
    persistence_multiplier = jnp.exp(log_persistence)
    vol = jnp.sqrt(-jnp.expm1(2.0 * log_persistence))

    def one_group(group):
        start = (group * PG).astype(jnp.int32)
        block = lax.dynamic_slice_in_dim(independent_disturbances, start, PG, 1)
        leading_element = lax.dynamic_slice_in_dim(starting_driver_values, start, PG, 0)
        correlated_disturbances = jnp.dot(block.reshape(-1, F), correlation_mixer, preferred_element_type=jnp.float32).reshape(HORIZON, PG, F)

        def propagate_one_day(state, operand_tensors):
            random_normal_sample, driver_value_now = operand_tensors
            state = persistence_multiplier * driver_value_now * state + vol * random_normal_sample
            return (state, state)
        ignored_placeholder, driver_trajectory = lax.scan(propagate_one_day, leading_element, (correlated_disturbances, regime_multiplier))
        scenario = driver_trajectory.astype(jnp.bfloat16).reshape(-1, F)
        cash = jnp.dot(scenario, payoff_per_unit_table, preferred_element_type=jnp.float32).reshape(HORIZON, PG, K)
        rate = 0.03 + 0.3 * jnp.dot(scenario, short_yield_coefficients, preferred_element_type=jnp.float32).reshape(HORIZON, PG)
        discount = jnp.exp(-(1.0 / 256.0) * jnp.cumsum(rate, axis=0))
        return lax.optimization_barrier(jnp.sum(discount[:, :, None] * cash, axis=0)) / HORIZON
    result = lax.map(one_group, jnp.arange(N_PATHS, dtype=jnp.int32))
    return result.reshape(PATHS, K)
```

```python
import functools

import jax
import jax.numpy as jnp
from jax import lax
from jax.experimental import pallas as pl
from jax.experimental.pallas import tpu as pltpu
from jax.sharding import Mesh
from jax.sharding import PartitionSpec as P

MESH_ID = pl.DeviceIdType.MESH
NY, NC, NZ, NX = 4, 2, 16, 4
DAYS, PATHS, F, K = 64, 4, 1024, 128
BLOCK = DAYS * NX
LANES = 128
FAR_FIRST = (8, 7, 9, 6, 10, 5, 11, 4, 12, 3, 13, 2, 14, 1, 15)
f32, bf16 = jnp.float32, jnp.bfloat16


def columns(k):
    return pl.ds(pl.multiple_of(k * LANES, LANES), LANES)


def expm1(v):
    total = jnp.ones_like(v)
    for n in range(10, 1, -1):
        total = 1.0 + total * v * (1.0 / n)
    return v * total


def remote(src, dst, send, recv, **where):
    return pltpu.make_async_remote_copy(
        src_ref=src, dst_ref=dst, send_sem=send, recv_sem=recv, device_id=where, device_id_type=MESH_ID
    )


def kernel(
    e_in, s0_in, m_in, lp_in, lpd_in, reg_in, pay_in, sc_in, out,
    ev, es, er, mb, bm, acc, dd, scen, res, rw, rb, lpv, lpd, s0v, regv, scv,
    dk, dx, dt, uu, vv, lrs, lrr, ebs, ebr, cbs, fs, fr, gs, gr,
    ld, msend, mrecv, esend, erecv, rsend, rrecv, lsend, lrecv, bsend, brecv, fsend, frecv, gsend, grecv,
):
    y, c, z, x = (lax.axis_index(a) for a in ("y", "c", "z", "x"))
    yp, ym, y2 = lax.rem(y + 1, NY), lax.rem(y + NY - 1, NY), lax.rem(y + 2, NY)
    mate = 1 - c

    def shard(yy, cc, half):
        return mb.at[pl.ds(pl.multiple_of((yy * 2 + cc) * 128 + half * 64, 64), 64), :]

    loads = [
        pltpu.make_async_copy(e_in, ev, ld.at[0]),
        pltpu.make_async_copy(reg_in, regv, ld.at[1]),
        pltpu.make_async_copy(lp_in, lpv, ld.at[2]),
        pltpu.make_async_copy(lpd_in, lpd, ld.at[3]),
        pltpu.make_async_copy(s0_in, s0v, ld.at[4]),
        pltpu.make_async_copy(sc_in, scv, ld.at[5]),
        pltpu.make_async_copy(pay_in, bm.at[:, pl.ds(0, K)], ld.at[6]),
        pltpu.make_async_copy(m_in, mb.at[pl.ds(pl.multiple_of((y * 2 + c) * 128, 128), 128), :], ld.at[7]),
    ]
    for copy in loads:
        copy.start()

    barrier = pltpu.get_barrier_semaphore()
    peers = [{"c": mate}, {"y": yp}, {"y": ym}]
    peers += [{"x": lax.rem(x + k, NX)} for k in range(1, NX)]
    for peer in peers:
        pl.semaphore_signal(barrier, inc=1, device_id=peer, device_id_type=MESH_ID)

    @pl.loop(1, NZ)
    def _(k):
        pl.semaphore_signal(barrier, inc=1, device_id={"z": lax.rem(z + k, NZ)}, device_id_type=MESH_ID)

    loads[0].wait()
    row = lax.broadcasted_iota(jnp.int32, (256, 256), 0)
    col = lax.broadcasted_iota(jnp.int32, (256, 256), 1)
    source = (((row & 7) * 8 + ((row >> 3) & 7)) << 2) + (row >> 6)
    order = (col == source).astype(f32).astype(bf16)
    for k in range(4):
        cols = pl.ds(k * 256, 256)
        flat = ev[:, :, cols].reshape(DAYS * PATHS, 256)
        moved = jnp.dot(order, flat, preferred_element_type=f32).astype(bf16)
        for p in range(PATHS):
            es[p, :, cols] = moved[p * DAYS : (p + 1) * DAYS]
    loads[1].wait()
    rw[pl.ds(x, 1)] = jnp.ones((1, 8, LANES), f32)
    rw[pl.ds(x, 1), :, pl.ds(0, DAYS)] = jnp.broadcast_to(regv[...][None], (1, 8, DAYS))

    pl.semaphore_wait(barrier, len(peers) + NZ - 1)

    def m_copy(n, src, dst, **where):
        return remote(src, dst, msend.at[n], mrecv.at[n], **where)

    def own(half):
        return m_in.at[pl.ds(half * 64, 64), :]

    up = [m_copy(h, own(h), shard(y, c, h), y=yp) for h in range(2)]
    down = [m_copy(2 + h, own(h), shard(y, c, h), y=ym) for h in range(2)]
    across = m_copy(4, m_in, mb.at[pl.ds(pl.multiple_of((y * 2 + c) * 128, 128), 128), :], c=mate)
    up[0].start()
    down[1].start()
    r_copies, e_copies = [], []
    for k in range(1, NX):
        xx = lax.rem(x + k, NX)
        r_copies.append(remote(rw.at[x], rw.at[x], rsend.at[k - 1], rrecv.at[x], x=xx))
        e_copies.append(remote(es.at[xx], er.at[x], esend.at[k - 1], erecv.at[x], x=xx))
    for copy in r_copies:
        copy.start()
    across.start()
    up[1].start()
    down[0].start()
    for copy in e_copies:
        copy.start()
    e_own = pltpu.make_async_copy(es.at[x], er.at[x], ld.at[8])
    e_own.start()
    for copy in loads[2:]:
        copy.wait()

    for k in range(F // LANES):
        block = jnp.broadcast_to(scv[:, k * LANES : (k + 1) * LANES].astype(f32), (LANES, LANES))
        bm[pl.ds(k * LANES, LANES), pl.ds(K, LANES)] = block.T.astype(bf16)

    def r_wait(k):
        xx = lax.rem(x + k, NX)
        remote(rw.at[x], rw.at[xx], rsend.at[k - 1], rrecv.at[xx], x=xx).wait_recv()

    for k in range(1, NX):
        r_wait(k)
    rows = lax.broadcasted_iota(jnp.int32, (DAYS, LANES), 0)
    lanes = lax.broadcasted_iota(jnp.int32, (DAYS, LANES), 1)
    pick = lanes == (rows & 7) * 8 + (rows >> 3)
    logs = jnp.zeros((8, LANES), f32)
    for j in range(NX):
        logs = logs + jnp.log(rw[j])
        spread = jnp.where(pick, jnp.broadcast_to(rw[j, 0:1], (DAYS, LANES)), 0.0)
        rb[pl.ds(j * DAYS, DAYS), :] = jnp.broadcast_to(jnp.sum(spread, axis=1, keepdims=True), (DAYS, LANES))
    lrs[...] = jnp.broadcast_to(jnp.sum(logs, axis=1, keepdims=True), (8, LANES))

    def later(k, copy):
        @pl.when(z + k < NZ)
        def _():
            copy(k)

    def lr_copy(k):
        return remote(lrs, lrr.at[z], lsend.at[k], lrecv.at[z], z=lax.rem(z + k, NZ))

    def eb_copy(k):
        return remote(ebs, ebr.at[z], bsend.at[k], brecv.at[z], z=lax.rem(z + k, NZ))

    for k in FAR_FIRST:
        later(k, lambda k: lr_copy(k).start())

    sub = lax.broadcasted_iota(jnp.int32, (8, LANES), 0)

    @pl.loop(0, F // LANES)
    def _(k):
        cols = columns(k)
        keep = jnp.broadcast_to(jnp.exp(lpv[:, cols]), (8, LANES))
        before = jnp.ones((8, LANES), f32)
        for j in range(NX):
            decay = None
            for i in range(8):
                r = pl.ds(j * DAYS + i * 8, 8)
                today = keep * rb[r, :]
                decay = today if i == 0 else decay * today
                dd[r, cols] = decay
            for n, shift in enumerate((1, 2, 4)):
                dk[n, j, :, cols] = jnp.where(sub >= shift, decay, 0.0)
                decay = jnp.where(sub >= shift, decay * pltpu.roll(decay, shift, 0), decay)
            first = jnp.where(sub >= 1, pltpu.roll(decay, 1, 0), 1.0)
            total = jnp.broadcast_to(decay[7:8], (8, LANES))
            dx[j, :, cols] = first
            dt[j, :, cols] = total
            vv[j, :, cols] = first * before
            before = before * total

    def hop(n, yy, half):
        return remote(shard(yy, c, half), shard(yy, c, half), msend.at[n], mrecv.at[n], y=yp)

    def relay(n, yy, half):
        return m_copy(7 + n, shard(yy, c, half), shard(yy, c, half), c=mate)

    def relayed(n, yy, half):
        remote(shard(yy, mate, half), shard(yy, mate, half), msend.at[7 + n], mrecv.at[7 + n], c=mate).wait_recv()

    relays = [relay(0, ym, 0), relay(1, yp, 1), relay(2, ym, 1), relay(3, yp, 0), relay(4, y2, 0), relay(5, y2, 1)]
    up2 = m_copy(5, shard(ym, c, 0), shard(ym, c, 0), y=yp)
    down2 = m_copy(6, shard(yp, c, 1), shard(yp, c, 1), y=ym)

    def product(yy, first):
        at = pl.ds(pl.multiple_of(yy * 256, 256), 256)
        left = jnp.concatenate([er[j, :, at] for j in range(NX)], axis=0)
        for k in range(4):
            cols = pl.ds(k * 256, 256)
            term = jnp.dot(left, mb[at, cols], preferred_element_type=f32)
            acc[:, cols] = term if first else acc[:, cols] + term

    hop(0, ym, 0).wait_recv()
    up2.start()
    relays[0].start()
    hop(3, yp, 1).wait_recv()
    down2.start()
    relays[1].start()
    e_own.wait()
    for k in range(1, NX):
        xx = lax.rem(x + k, NX)
        remote(es.at[xx], er.at[xx], esend.at[k - 1], erecv.at[xx], x=xx).wait_recv()
    remote(m_in, mb.at[pl.ds(pl.multiple_of((y * 2 + mate) * 128, 128), 128), :], msend.at[4], mrecv.at[4], c=mate).wait_recv()
    product(y, True)
    hop(1, ym, 1).wait_recv()
    relays[2].start()
    hop(2, yp, 0).wait_recv()
    relays[3].start()
    relayed(0, ym, 0)
    relayed(2, ym, 1)
    product(ym, False)
    hop(5, y2, 0).wait_recv()
    relays[4].start()
    hop(6, y2, 1).wait_recv()
    relays[5].start()
    relayed(1, yp, 1)
    relayed(3, yp, 0)
    product(yp, False)
    relayed(4, y2, 0)
    relayed(5, y2, 1)
    product(y2, False)

    @pl.loop(0, F // LANES)
    def _(k):
        cols = columns(k)
        log_keep = lpv[:, cols]
        keep = jnp.broadcast_to(jnp.exp(log_keep), (8, LANES))
        double = 2.0 * log_keep
        vol = jnp.broadcast_to(jnp.sqrt(-expm1(double)), (8, LANES))
        carried = jnp.zeros((8, LANES), f32)
        for j in range(NX):
            state = None
            for i in range(8):
                r = pl.ds(j * DAYS + i * 8, 8)
                shock = vol * acc[r, cols]
                state = shock if i == 0 else (keep * rb[r, :]) * state + shock
                acc[r, cols] = state
            for n, shift in enumerate((1, 2, 4)):
                state = state + dk[n, j, :, cols] * pltpu.roll(state, shift, 0)
            first = jnp.where(sub >= 1, pltpu.roll(state, 1, 0), 0.0)
            uu[j, :, cols] = first + dx[j, :, cols] * carried
            carried = dt[j, :, cols] * carried + jnp.broadcast_to(state[7:8], (8, LANES))
        ebs[pl.ds(k, 1), :] = carried[0:1]

    for k in FAR_FIRST:
        later(k, lambda k: eb_copy(k).start())

    @pl.loop(0, F // LANES)
    def _(k):
        cols = columns(k)
        paths = lax.broadcasted_iota(jnp.int32, (PATHS, LANES), 0)
        cbs[pl.ds(k, 1), :] = jnp.sum(jnp.where(paths == x, s0v[:, cols], 0.0), axis=0, keepdims=True)
        for j in range(NX):
            u, v = uu[j, :, cols], vv[j, :, cols]
            for i in range(8):
                r = pl.ds(j * DAYS + i * 8, 8)
                decay = dd[r, cols]
                acc[r, cols] = acc[r, cols] + decay * u
                dd[r, cols] = decay * v

    span = float(BLOCK) * lpd[...]

    @pl.loop(0, z)
    def _(u):
        remote(lrs, lrr.at[u], lsend.at[0], lrecv.at[u], z=u).wait_recv()
        lrr[pl.ds(u, 1)] = jnp.exp(span + lrr[u])[None]

    def entered(u, carry):
        remote(ebs, ebr.at[u], bsend.at[0], brecv.at[u], z=u).wait_recv()
        return lrr[u] * carry + ebr[u]

    cbs[...] = lax.fori_loop(0, z, entered, cbs[...])

    @pl.loop(0, F // LANES)
    def _(k):
        cols = columns(k)
        scen[:, cols] = (acc[:, cols] + dd[:, cols] * cbs[pl.ds(k, 1), :]).astype(bf16)

    res[...] = jnp.dot(scen[...], bm[...], preferred_element_type=f32)

    base = jnp.zeros((8, LANES), f32)
    exponent = []
    for j in range(NX):
        run = jnp.zeros((8, LANES), f32)
        sums = []
        for i in range(8):
            run = run + (0.03 + 0.3 * res[pl.ds(j * DAYS + i * 8, 8), pl.ds(K, LANES)])
            sums.append(run)
        total = run
        for shift in (1, 2, 4):
            total = total + jnp.where(sub >= shift, pltpu.roll(total, shift, 0), 0.0)
        start = base + jnp.where(sub >= 1, pltpu.roll(total, 1, 0), 0.0)
        base = base + jnp.broadcast_to(total[7:8], (8, LANES))
        exponent += [(-1.0 / 256.0) * (start + s) for s in sums]
    top = functools.reduce(jnp.maximum, exponent)
    top = jnp.max(top, axis=0, keepdims=True)
    worth = jnp.zeros((8, LANES), f32)
    for n, power in enumerate(exponent):
        worth = worth + jnp.exp(power - top) * res[pl.ds(n * 8, 8), pl.ds(0, K)]
    fs[0:1, :] = jnp.sum(worth, axis=0, keepdims=True)
    fs[1:2, :] = base[0:1]
    fs[2:3, :] = top
    fs[3:4, :] = top
    fr[pl.ds(z, 1)] = fs[...][None]

    def f_copy(k):
        return remote(fs, fr.at[z], fsend.at[k], frecv.at[z], z=lax.rem(z + k, NZ))

    for k in FAR_FIRST:
        f_copy(k).start()
    for k in reversed(FAR_FIRST):
        u = lax.rem(z + k, NZ)
        remote(fs, fr.at[u], fsend.at[k], frecv.at[u], z=u).wait_recv()

    passed = jnp.zeros((1, LANES), f32)
    value = jnp.zeros((1, LANES), f32)
    for u in range(NZ):
        value = value + jnp.exp(fr[u, 2:3] - (1.0 / 256.0) * passed) * fr[u, 0:1]
        passed = passed + fr[u, 1:2]
    gs[...] = jnp.broadcast_to(value * (1.0 / 4096.0), (8, LANES))
    g_copies = []
    for k in range(1, NX):
        xx = lax.rem(x + k, NX)
        g_copies.append(remote(gs, gr.at[x], gsend.at[k - 1], grecv.at[x], x=xx))
        g_copies[-1].start()
    gr[pl.ds(x, 1)] = gs[...][None]

    for copy in (*up, *down, across, up2, down2, *relays, *r_copies, *e_copies):
        copy.wait_send()
    for k in FAR_FIRST:
        later(k, lambda k: lr_copy(k).wait_send())
        later(k, lambda k: eb_copy(k).wait_send())
        f_copy(k).wait_send()
    for k in range(1, NX):
        xx = lax.rem(x + k, NX)
        remote(gs, gr.at[xx], gsend.at[k - 1], grecv.at[xx], x=xx).wait_recv()
    for j in range(NX):
        out[j : j + 1, :] = gr[j, 0:1]
    for copy in g_copies:
        copy.wait_send()


def local(e, s0, m, lp, reg, pay, sc):
    vmem, dma = pltpu.VMEM, pltpu.SemaphoreType.DMA
    return pl.pallas_call(
        kernel,
        out_shape=jax.ShapeDtypeStruct((PATHS, K), f32),
        in_specs=[pl.BlockSpec(memory_space=pl.ANY)] * 8,
        out_specs=pl.BlockSpec(memory_space=pltpu.VMEM),
        scratch_shapes=[
            vmem((DAYS, PATHS, F), bf16),
            vmem((PATHS, DAYS, F), bf16),
            vmem((NX, DAYS, F), bf16),
            vmem((F, F), bf16),
            vmem((F, 2 * K), bf16),
            vmem((BLOCK, F), f32),
            vmem((BLOCK, F), f32),
            vmem((BLOCK, F), bf16),
            vmem((BLOCK, 2 * K), f32),
            vmem((NX, 8, LANES), f32),
            vmem((BLOCK, LANES), f32),
            vmem((1, F), f32),
            vmem((8, LANES), f32),
            vmem((PATHS, F), f32),
            vmem((1, DAYS), f32),
            vmem((1, F), bf16),
            vmem((3, NX, 8, F), f32),
            vmem((NX, 8, F), f32),
            vmem((NX, 8, F), f32),
            vmem((NX, 8, F), f32),
            vmem((NX, 8, F), f32),
            vmem((8, LANES), f32),
            vmem((NZ, 8, LANES), f32),
            vmem((8, LANES), f32),
            vmem((NZ, 8, LANES), f32),
            vmem((8, LANES), f32),
            vmem((4, LANES), f32),
            vmem((NZ, 4, LANES), f32),
            vmem((8, LANES), f32),
            vmem((NX, 8, LANES), f32),
            dma((9,)),
            dma((13,)), dma((13,)),
            dma((NX,)), dma((NX,)),
            dma((NX,)), dma((NX,)),
            dma((NZ,)), dma((NZ,)),
            dma((NZ,)), dma((NZ,)),
            dma((NZ,)), dma((NZ,)),
            dma((NX,)), dma((NX,)),
        ],
        compiler_params=pltpu.CompilerParams(collective_id=0, has_side_effects=True, vmem_limit_bytes=48 << 20),
        name="scenarios",
    )(e, s0, m, lp.reshape(1, F), lp.reshape(8, LANES), reg.reshape(1, DAYS), pay, sc.reshape(1, F))


def solution(mesh):
    split = Mesh(mesh.devices.reshape(NY, NC, NZ, NX), ("y", "c", "z", "x"))
    paths, days = ("y", "c"), ("z", "x")
    placed = (P(days, paths, None), P(paths, None), P(paths, None), P(), P(days), P(), P())
    return jax.shard_map(local, mesh=split, in_specs=placed, out_specs=P(paths, None), check_vma=False)
```

```python
import functools

import jax
import jax.numpy as jnp
from jax import lax
from jax.experimental import pallas as pl
from jax.experimental.pallas import tpu as pltpu
from jax.sharding import Mesh
from jax.sharding import PartitionSpec as P

MESH_ID = pl.DeviceIdType.MESH
NY, NC, NZ, NX = 4, 2, 16, 4
DAYS, PATHS, F, K = 64, 4, 1024, 128
BLOCK = DAYS * NX
LANES = 128
FAR_FIRST = (8, 7, 9, 6, 10, 5, 11, 4, 12, 3, 13, 2, 14, 1, 15)
f32, bf16 = jnp.float32, jnp.bfloat16


def columns(k):
    return pl.ds(pl.multiple_of(k * LANES, LANES), LANES)


def expm1(v):
    total = jnp.ones_like(v)
    for n in range(10, 1, -1):
        total = 1.0 + total * v * (1.0 / n)
    return v * total


def remote(src, dst, send, recv, **where):
    return pltpu.make_async_remote_copy(
        src_ref=src, dst_ref=dst, send_sem=send, recv_sem=recv, device_id=where, device_id_type=MESH_ID
    )


def kernel(
    e_in, s0_in, m_in, lp_in, lpd_in, reg_in, pay_in, sc_in, out,
    ev, es, er, mb, bm, acc, dd, scen, res, rw, rb, lpv, lpd, s0v, regv, scv,
    dk, dx, dt, uu, vv, lrs, lrr, ebs, ebr, cbs, fs, fr, gs, gr,
    ld, msend, mrecv, esend, erecv, rsend, rrecv, lsend, lrecv, bsend, brecv, fsend, frecv, gsend, grecv, met,
):
    y, c, z, x = (lax.axis_index(a) for a in ("y", "c", "z", "x"))
    yp, ym, y2 = lax.rem(y + 1, NY), lax.rem(y + NY - 1, NY), lax.rem(y + 2, NY)
    mate = 1 - c

    def shard(yy, cc, half):
        return mb.at[pl.ds(pl.multiple_of((yy * 2 + cc) * 128 + half * 64, 64), 64), :]

    loads = [
        pltpu.make_async_copy(e_in, ev, ld.at[0]),
        pltpu.make_async_copy(reg_in, regv, ld.at[1]),
        pltpu.make_async_copy(lp_in, lpv, ld.at[2]),
        pltpu.make_async_copy(lpd_in, lpd, ld.at[3]),
        pltpu.make_async_copy(s0_in, s0v, ld.at[4]),
        pltpu.make_async_copy(sc_in, scv, ld.at[5]),
        pltpu.make_async_copy(pay_in, bm.at[:, pl.ds(0, K)], ld.at[6]),
        pltpu.make_async_copy(m_in, mb.at[pl.ds(pl.multiple_of((y * 2 + c) * 128, 128), 128), :], ld.at[7]),
    ]
    for copy in loads:
        copy.start()

    barrier = pltpu.get_barrier_semaphore()
    peers = [{"c": mate}, {"y": yp}, {"y": ym}]
    peers += [{"x": lax.rem(x + k, NX)} for k in range(1, NX)]
    for peer in peers:
        pl.semaphore_signal(barrier, inc=1, device_id=peer, device_id_type=MESH_ID)

    def along_z(semaphore, distance):
        for k in (distance, NZ - distance):
            pl.semaphore_signal(semaphore, inc=1, device_id={"z": lax.rem(z + k, NZ)}, device_id_type=MESH_ID)

    along_z(barrier, 1)

    loads[0].wait()
    row = lax.broadcasted_iota(jnp.int32, (256, 256), 0)
    col = lax.broadcasted_iota(jnp.int32, (256, 256), 1)
    source = (((row & 7) * 8 + ((row >> 3) & 7)) << 2) + (row >> 6)
    order = (col == source).astype(f32).astype(bf16)
    for k in range(4):
        cols = pl.ds(k * 256, 256)
        flat = ev[:, :, cols].reshape(DAYS * PATHS, 256)
        moved = jnp.dot(order, flat, preferred_element_type=f32).astype(bf16)
        for p in range(PATHS):
            es[p, :, cols] = moved[p * DAYS : (p + 1) * DAYS]
    loads[1].wait()
    rw[pl.ds(x, 1)] = jnp.ones((1, 8, LANES), f32)
    rw[pl.ds(x, 1), :, pl.ds(0, DAYS)] = jnp.broadcast_to(regv[...][None], (1, 8, DAYS))

    pl.semaphore_wait(barrier, len(peers) + 2)
    along_z(met.at[0], 1)

    def m_copy(n, src, dst, **where):
        return remote(src, dst, msend.at[n], mrecv.at[n], **where)

    def own(half):
        return m_in.at[pl.ds(half * 64, 64), :]

    up = [m_copy(h, own(h), shard(y, c, h), y=yp) for h in range(2)]
    down = [m_copy(2 + h, own(h), shard(y, c, h), y=ym) for h in range(2)]
    across = m_copy(4, m_in, mb.at[pl.ds(pl.multiple_of((y * 2 + c) * 128, 128), 128), :], c=mate)
    up[0].start()
    down[1].start()
    r_copies, e_copies = [], []
    for k in range(1, NX):
        xx = lax.rem(x + k, NX)
        r_copies.append(remote(rw.at[x], rw.at[x], rsend.at[k - 1], rrecv.at[x], x=xx))
        e_copies.append(remote(es.at[xx], er.at[x], esend.at[k - 1], erecv.at[x], x=xx))
    for copy in r_copies:
        copy.start()
    across.start()
    up[1].start()
    down[0].start()
    for copy in e_copies:
        copy.start()
    e_own = pltpu.make_async_copy(es.at[x], er.at[x], ld.at[8])
    e_own.start()
    for copy in loads[2:]:
        copy.wait()

    short = scv[...].astype(f32)
    for k in range(F // LANES):
        block = jnp.broadcast_to(short[k : k + 1], (LANES, LANES))
        bm[pl.ds(k * LANES, LANES), pl.ds(K, LANES)] = block.T.astype(bf16)

    def r_wait(k):
        xx = lax.rem(x + k, NX)
        remote(rw.at[x], rw.at[xx], rsend.at[k - 1], rrecv.at[xx], x=xx).wait_recv()

    for k in range(1, NX):
        r_wait(k)
    rows = lax.broadcasted_iota(jnp.int32, (DAYS, LANES), 0)
    lanes = lax.broadcasted_iota(jnp.int32, (DAYS, LANES), 1)
    pick = lanes == (rows & 7) * 8 + (rows >> 3)
    logs = jnp.zeros((8, LANES), f32)
    for j in range(NX):
        logs = logs + jnp.log(rw[j])
        spread = jnp.where(pick, jnp.broadcast_to(rw[j, 0:1], (DAYS, LANES)), 0.0)
        rb[pl.ds(j * DAYS, DAYS), :] = jnp.broadcast_to(jnp.sum(spread, axis=1, keepdims=True), (DAYS, LANES))
    lrs[...] = jnp.broadcast_to(jnp.sum(logs, axis=1, keepdims=True), (8, LANES))

    def later(k, copy):
        @pl.when(z + k < NZ)
        def _():
            copy(k)

    def lr_copy(k):
        return remote(lrs, lrr.at[z], lsend.at[k], lrecv.at[z], z=lax.rem(z + k, NZ))

    def eb_copy(k):
        return remote(ebs, ebr.at[z], bsend.at[k], brecv.at[z], z=lax.rem(z + k, NZ))

    sub = lax.broadcasted_iota(jnp.int32, (8, LANES), 0)

    @pl.loop(0, F // LANES)
    def _(k):
        cols = columns(k)
        keep = jnp.broadcast_to(jnp.exp(lpv[:, cols]), (8, LANES))
        before = jnp.ones((8, LANES), f32)
        for j in range(NX):
            decay = None
            for i in range(8):
                r = pl.ds(j * DAYS + i * 8, 8)
                today = keep * rb[r, :]
                decay = today if i == 0 else decay * today
                dd[r, cols] = decay
            for n, shift in enumerate((1, 2, 4)):
                dk[n, j, :, cols] = jnp.where(sub >= shift, decay, 0.0)
                decay = jnp.where(sub >= shift, decay * pltpu.roll(decay, shift, 0), decay)
            first = jnp.where(sub >= 1, pltpu.roll(decay, 1, 0), 1.0)
            total = jnp.broadcast_to(decay[7:8], (8, LANES))
            dx[j, :, cols] = first
            dt[j, :, cols] = total
            vv[j, :, cols] = first * before
            before = before * total

    def hop(n, yy, half):
        return remote(shard(yy, c, half), shard(yy, c, half), msend.at[n], mrecv.at[n], y=yp)

    def relay(n, yy, half):
        return m_copy(7 + n, shard(yy, c, half), shard(yy, c, half), c=mate)

    def relayed(n, yy, half):
        remote(shard(yy, mate, half), shard(yy, mate, half), msend.at[7 + n], mrecv.at[7 + n], c=mate).wait_recv()

    relays = [relay(0, ym, 0), relay(1, yp, 1), relay(2, ym, 1), relay(3, yp, 0), relay(4, y2, 0), relay(5, y2, 1)]
    up2 = m_copy(5, shard(ym, c, 0), shard(ym, c, 0), y=yp)
    down2 = m_copy(6, shard(yp, c, 1), shard(yp, c, 1), y=ym)

    def product(yy, first):
        at = pl.ds(pl.multiple_of(yy * 256, 256), 256)
        left = jnp.concatenate([er[j, :, at] for j in range(NX)], axis=0)
        for k in range(4):
            cols = pl.ds(k * 256, 256)
            term = jnp.dot(left, mb[at, cols], preferred_element_type=f32)
            acc[:, cols] = term if first else acc[:, cols] + term

    hop(0, ym, 0).wait_recv()
    up2.start()
    relays[0].start()
    hop(3, yp, 1).wait_recv()
    down2.start()
    relays[1].start()
    e_own.wait()
    for k in range(1, NX):
        xx = lax.rem(x + k, NX)
        remote(es.at[xx], er.at[xx], esend.at[k - 1], erecv.at[xx], x=xx).wait_recv()
    remote(m_in, mb.at[pl.ds(pl.multiple_of((y * 2 + mate) * 128, 128), 128), :], msend.at[4], mrecv.at[4], c=mate).wait_recv()
    product(y, True)
    pl.semaphore_wait(met.at[0], 2)
    along_z(met.at[1], 2)
    hop(1, ym, 1).wait_recv()
    relays[2].start()
    hop(2, yp, 0).wait_recv()
    relays[3].start()
    relayed(0, ym, 0)
    relayed(2, ym, 1)
    product(ym, False)
    pl.semaphore_wait(met.at[1], 2)
    along_z(met.at[2], 4)
    hop(5, y2, 0).wait_recv()
    relays[4].start()
    hop(6, y2, 1).wait_recv()
    relays[5].start()
    relayed(1, yp, 1)
    relayed(3, yp, 0)
    product(yp, False)
    pl.semaphore_wait(met.at[2], 2)
    for k in FAR_FIRST:
        later(k, lambda k: lr_copy(k).start())
    relayed(4, y2, 0)
    relayed(5, y2, 1)
    product(y2, False)

    @pl.loop(0, F // LANES)
    def _(k):
        cols = columns(k)
        log_keep = lpv[:, cols]
        keep = jnp.broadcast_to(jnp.exp(log_keep), (8, LANES))
        double = 2.0 * log_keep
        vol = jnp.broadcast_to(jnp.sqrt(-expm1(double)), (8, LANES))
        carried = jnp.zeros((8, LANES), f32)
        for j in range(NX):
            state = None
            for i in range(8):
                r = pl.ds(j * DAYS + i * 8, 8)
                shock = vol * acc[r, cols]
                state = shock if i == 0 else (keep * rb[r, :]) * state + shock
                acc[r, cols] = state
            for n, shift in enumerate((1, 2, 4)):
                state = state + dk[n, j, :, cols] * pltpu.roll(state, shift, 0)
            first = jnp.where(sub >= 1, pltpu.roll(state, 1, 0), 0.0)
            uu[j, :, cols] = first + dx[j, :, cols] * carried
            carried = dt[j, :, cols] * carried + jnp.broadcast_to(state[7:8], (8, LANES))
        ebs[pl.ds(k, 1), :] = carried[0:1]

    for k in FAR_FIRST:
        later(k, lambda k: eb_copy(k).start())

    @pl.loop(0, F // LANES)
    def _(k):
        cols = columns(k)
        paths = lax.broadcasted_iota(jnp.int32, (PATHS, LANES), 0)
        cbs[pl.ds(k, 1), :] = jnp.sum(jnp.where(paths == x, s0v[:, cols], 0.0), axis=0, keepdims=True)
        for j in range(NX):
            u, v = uu[j, :, cols], vv[j, :, cols]
            for i in range(8):
                r = pl.ds(j * DAYS + i * 8, 8)
                decay = dd[r, cols]
                acc[r, cols] = acc[r, cols] + decay * u
                dd[r, cols] = decay * v

    span = float(BLOCK) * lpd[...]

    @pl.loop(0, z)
    def _(u):
        remote(lrs, lrr.at[u], lsend.at[0], lrecv.at[u], z=u).wait_recv()
        lrr[pl.ds(u, 1)] = jnp.exp(span + lrr[u])[None]

    def entered(u, carry):
        remote(ebs, ebr.at[u], bsend.at[0], brecv.at[u], z=u).wait_recv()
        return lrr[u] * carry + ebr[u]

    cbs[...] = lax.fori_loop(0, z, entered, cbs[...])

    @pl.loop(0, F // LANES)
    def _(k):
        cols = columns(k)
        scen[:, cols] = (acc[:, cols] + dd[:, cols] * cbs[pl.ds(k, 1), :]).astype(bf16)

    res[...] = jnp.dot(scen[...], bm[...], preferred_element_type=f32)

    base = jnp.zeros((8, LANES), f32)
    exponent = []
    for j in range(NX):
        run = jnp.zeros((8, LANES), f32)
        sums = []
        for i in range(8):
            run = run + (0.03 + 0.3 * res[pl.ds(j * DAYS + i * 8, 8), pl.ds(K, LANES)])
            sums.append(run)
        total = run
        for shift in (1, 2, 4):
            total = total + jnp.where(sub >= shift, pltpu.roll(total, shift, 0), 0.0)
        start = base + jnp.where(sub >= 1, pltpu.roll(total, 1, 0), 0.0)
        base = base + jnp.broadcast_to(total[7:8], (8, LANES))
        exponent += [(-1.0 / 256.0) * (start + s) for s in sums]
    top = functools.reduce(jnp.maximum, exponent)
    top = jnp.max(top, axis=0, keepdims=True)
    worth = jnp.zeros((8, LANES), f32)
    for n, power in enumerate(exponent):
        worth = worth + jnp.exp(power - top) * res[pl.ds(n * 8, 8), pl.ds(0, K)]
    fs[0:1, :] = jnp.sum(worth, axis=0, keepdims=True)
    fs[1:2, :] = base[0:1]
    fs[2:3, :] = top
    fs[3:4, :] = top
    fr[pl.ds(z, 1)] = fs[...][None]

    def f_copy(k):
        return remote(fs, fr.at[z], fsend.at[k], frecv.at[z], z=lax.rem(z + k, NZ))

    for k in FAR_FIRST:
        f_copy(k).start()
    for k in reversed(FAR_FIRST):
        u = lax.rem(z + k, NZ)
        remote(fs, fr.at[u], fsend.at[k], frecv.at[u], z=u).wait_recv()

    passed = jnp.zeros((1, LANES), f32)
    value = jnp.zeros((1, LANES), f32)
    for u in range(NZ):
        value = value + jnp.exp(fr[u, 2:3] - (1.0 / 256.0) * passed) * fr[u, 0:1]
        passed = passed + fr[u, 1:2]
    gs[...] = jnp.broadcast_to(value * (1.0 / 4096.0), (8, LANES))
    g_copies = []
    for k in range(1, NX):
        xx = lax.rem(x + k, NX)
        g_copies.append(remote(gs, gr.at[x], gsend.at[k - 1], grecv.at[x], x=xx))
        g_copies[-1].start()
    gr[pl.ds(x, 1)] = gs[...][None]

    for copy in (*up, *down, across, up2, down2, *relays, *r_copies, *e_copies):
        copy.wait_send()
    for k in FAR_FIRST:
        later(k, lambda k: lr_copy(k).wait_send())
        later(k, lambda k: eb_copy(k).wait_send())
        f_copy(k).wait_send()
    for k in range(1, NX):
        xx = lax.rem(x + k, NX)
        remote(gs, gr.at[xx], gsend.at[k - 1], grecv.at[xx], x=xx).wait_recv()
    for j in range(NX):
        out[j : j + 1, :] = gr[j, 0:1]
    for copy in g_copies:
        copy.wait_send()


def local(e, s0, m, lp, reg, pay, sc):
    vmem, dma = pltpu.VMEM, pltpu.SemaphoreType.DMA
    return pl.pallas_call(
        kernel,
        out_shape=jax.ShapeDtypeStruct((PATHS, K), f32),
        in_specs=[pl.BlockSpec(memory_space=pl.ANY)] * 8,
        out_specs=pl.BlockSpec(memory_space=pltpu.VMEM),
        scratch_shapes=[
            vmem((DAYS, PATHS, F), bf16),
            vmem((PATHS, DAYS, F), bf16),
            vmem((NX, DAYS, F), bf16),
            vmem((F, F), bf16),
            vmem((F, 2 * K), bf16),
            vmem((BLOCK, F), f32),
            vmem((BLOCK, F), f32),
            vmem((BLOCK, F), bf16),
            vmem((BLOCK, 2 * K), f32),
            vmem((NX, 8, LANES), f32),
            vmem((BLOCK, LANES), f32),
            vmem((1, F), f32),
            vmem((8, LANES), f32),
            vmem((PATHS, F), f32),
            vmem((1, DAYS), f32),
            vmem((8, LANES), bf16),
            vmem((3, NX, 8, F), f32),
            vmem((NX, 8, F), f32),
            vmem((NX, 8, F), f32),
            vmem((NX, 8, F), f32),
            vmem((NX, 8, F), f32),
            vmem((8, LANES), f32),
            vmem((NZ, 8, LANES), f32),
            vmem((8, LANES), f32),
            vmem((NZ, 8, LANES), f32),
            vmem((8, LANES), f32),
            vmem((4, LANES), f32),
            vmem((NZ, 4, LANES), f32),
            vmem((8, LANES), f32),
            vmem((NX, 8, LANES), f32),
            dma((9,)),
            dma((13,)), dma((13,)),
            dma((NX,)), dma((NX,)),
            dma((NX,)), dma((NX,)),
            dma((NZ,)), dma((NZ,)),
            dma((NZ,)), dma((NZ,)),
            dma((NZ,)), dma((NZ,)),
            dma((NX,)), dma((NX,)),
            pltpu.SemaphoreType.REGULAR((3,)),
        ],
        compiler_params=pltpu.CompilerParams(collective_id=0, has_side_effects=True, vmem_limit_bytes=60 << 20),
        name="scenarios",
    )(e, s0, m, lp.reshape(1, F), lp.reshape(8, LANES), reg.reshape(1, DAYS), pay, sc.reshape(8, LANES))


def solution(mesh):
    split = Mesh(mesh.devices.reshape(NY, NC, NZ, NX), ("y", "c", "z", "x"))
    paths, days = ("y", "c"), ("z", "x")
    placed = (P(days, paths, None), P(paths, None), P(paths, None), P(), P(days), P(), P())
    return jax.shard_map(local, mesh=split, in_specs=placed, out_specs=P(paths, None), check_vma=False)
```

```python
import functools

import jax
import jax.numpy as jnp
from jax import lax
from jax.experimental import pallas as pl
from jax.experimental.pallas import tpu as pltpu
from jax.sharding import Mesh
from jax.sharding import PartitionSpec as P

MESH_ID = pl.DeviceIdType.MESH
NY, NC, NZ, NX = 4, 2, 16, 4
DAYS, PATHS, F, K = 64, 4, 1024, 128
BLOCK = DAYS * NX
PIECE = 32
LANES = 128
FAR_FIRST = (8, 7, 9, 6, 10, 5, 11, 4, 12, 3, 13, 2, 14, 1, 15)
f32, bf16 = jnp.float32, jnp.bfloat16


def columns(k):
    return pl.ds(pl.multiple_of(k * LANES, LANES), LANES)


def expm1(v):
    total = jnp.ones_like(v)
    for n in range(10, 1, -1):
        total = 1.0 + total * v * (1.0 / n)
    return v * total


def remote(src, dst, send, recv, **where):
    return pltpu.make_async_remote_copy(
        src_ref=src, dst_ref=dst, send_sem=send, recv_sem=recv, device_id=where, device_id_type=MESH_ID
    )


def kernel(
    e_in, s0_in, m_in, lp_in, lpd_in, reg_in, pay_in, sc_in, out,
    ev, es, er, mb, bm, acc, dd, scen, res, rw, rb, lpv, lpd, s0v, regv, scv,
    dk, dx, dt, uu, vv, lrs, lrr, ebs, ebr, cbs, fs, fr,
    ld, msend, mrecv, esend, erecv, rsend, rrecv, lsend, lrecv, bsend, brecv, fsend, frecv, met,
):
    y, c, z, x = (lax.axis_index(a) for a in ("y", "c", "z", "x"))
    yp, ym, y2 = lax.rem(y + 1, NY), lax.rem(y + NY - 1, NY), lax.rem(y + 2, NY)
    mate = 1 - c

    def shard(yy, cc, piece):
        return mb.at[pl.ds(pl.multiple_of((yy * 2 + cc) * 128 + piece * PIECE, PIECE), PIECE), :]

    loads = [
        pltpu.make_async_copy(e_in, ev, ld.at[0]),
        pltpu.make_async_copy(reg_in, regv, ld.at[1]),
        pltpu.make_async_copy(lp_in, lpv, ld.at[2]),
        pltpu.make_async_copy(lpd_in, lpd, ld.at[3]),
        pltpu.make_async_copy(s0_in, s0v, ld.at[4]),
        pltpu.make_async_copy(sc_in, scv, ld.at[5]),
        pltpu.make_async_copy(pay_in, bm.at[:, pl.ds(0, K)], ld.at[6]),
        pltpu.make_async_copy(m_in, mb.at[pl.ds(pl.multiple_of((y * 2 + c) * 128, 128), 128), :], ld.at[7]),
    ]
    for copy in loads:
        copy.start()

    barrier = pltpu.get_barrier_semaphore()
    peers = [{"c": mate}, {"y": yp}, {"y": ym}]
    peers += [{"x": lax.rem(x + k, NX)} for k in range(1, NX)]
    for peer in peers:
        pl.semaphore_signal(barrier, inc=1, device_id=peer, device_id_type=MESH_ID)

    def along_z(semaphore, distance):
        for k in (distance, NZ - distance):
            pl.semaphore_signal(semaphore, inc=1, device_id={"z": lax.rem(z + k, NZ)}, device_id_type=MESH_ID)

    along_z(barrier, 1)

    loads[0].wait()
    row = lax.broadcasted_iota(jnp.int32, (256, 256), 0)
    col = lax.broadcasted_iota(jnp.int32, (256, 256), 1)
    source = (((row & 7) * 8 + ((row >> 3) & 7)) << 2) + (row >> 6)
    order = (col == source).astype(f32).astype(bf16)
    for k in range(4):
        cols = pl.ds(k * 256, 256)
        flat = ev[:, :, cols].reshape(DAYS * PATHS, 256)
        moved = jnp.dot(order, flat, preferred_element_type=f32).astype(bf16)
        for p in range(PATHS):
            es[p, :, cols] = moved[p * DAYS : (p + 1) * DAYS]
    loads[1].wait()
    rw[pl.ds(x, 1)] = jnp.ones((1, 8, LANES), f32)
    rw[pl.ds(x, 1), :, pl.ds(0, DAYS)] = jnp.broadcast_to(regv[...][None], (1, 8, DAYS))

    pl.semaphore_wait(barrier, len(peers) + 2)
    along_z(met.at[0], 1)

    def m_copy(n, src, dst, **where):
        return remote(src, dst, msend.at[n], mrecv.at[n], **where)

    def own(piece):
        return m_in.at[pl.ds(piece * PIECE, PIECE), :]

    up = [m_copy(n, own(n), shard(y, c, n), y=yp) for n in range(4)]
    down = [m_copy(4 + n, own(n), shard(y, c, n), y=ym) for n in range(4)]
    across = m_copy(8, m_in, mb.at[pl.ds(pl.multiple_of((y * 2 + c) * 128, 128), 128), :], c=mate)
    r_copies, e_copies = [], []
    for k in range(1, NX):
        xx = lax.rem(x + k, NX)
        r_copies.append(remote(rw.at[x], rw.at[x], rsend.at[k - 1], rrecv.at[x], x=xx))
        e_copies.append(remote(es.at[xx], er.at[x], esend.at[k - 1], erecv.at[x], x=xx))
    up[0].start()
    down[3].start()
    for copy in r_copies:
        copy.start()
    for copy in e_copies:
        copy.start()
    for n in (1, 2, 3):
        up[n].start()
        down[3 - n].start()
    across.start()
    e_own = pltpu.make_async_copy(es.at[x], er.at[x], ld.at[8])
    e_own.start()

    pl.semaphore_wait(met.at[0], 2)
    along_z(met.at[1], 2)
    for copy in loads[2:]:
        copy.wait()

    short = scv[...].astype(f32)
    for k in range(F // LANES):
        block = jnp.broadcast_to(short[k : k + 1], (LANES, LANES))
        bm[pl.ds(k * LANES, LANES), pl.ds(K, LANES)] = block.T.astype(bf16)

    def hop(n, yy, piece):
        remote(shard(yy, c, piece), shard(yy, c, piece), msend.at[n], mrecv.at[n], y=yp).wait_recv()

    def relay(n, yy, piece):
        relays.append(m_copy(13 + n, shard(yy, c, piece), shard(yy, c, piece), c=mate))
        relays[-1].start()

    def relayed(n, yy, piece):
        remote(shard(yy, mate, piece), shard(yy, mate, piece), msend.at[13 + n], mrecv.at[13 + n], c=mate).wait_recv()

    relays, onward = [], []
    for n in range(2):
        hop(n, ym, n)
        onward.append(m_copy(9 + n, shard(ym, c, n), shard(ym, c, n), y=yp))
        onward[-1].start()
        relay(n, ym, n)
        hop(7 - n, yp, 3 - n)
        onward.append(m_copy(11 + n, shard(yp, c, 3 - n), shard(yp, c, 3 - n), y=ym))
        onward[-1].start()
        relay(7 - n, yp, 3 - n)

    def r_wait(k):
        xx = lax.rem(x + k, NX)
        remote(rw.at[x], rw.at[xx], rsend.at[k - 1], rrecv.at[xx], x=xx).wait_recv()

    for k in range(1, NX):
        r_wait(k)
    rows = lax.broadcasted_iota(jnp.int32, (DAYS, LANES), 0)
    lanes = lax.broadcasted_iota(jnp.int32, (DAYS, LANES), 1)
    pick = lanes == (rows & 7) * 8 + (rows >> 3)
    logs = jnp.zeros((8, LANES), f32)
    for j in range(NX):
        logs = logs + jnp.log(rw[j])
        spread = jnp.where(pick, jnp.broadcast_to(rw[j, 0:1], (DAYS, LANES)), 0.0)
        rb[pl.ds(j * DAYS, DAYS), :] = jnp.broadcast_to(jnp.sum(spread, axis=1, keepdims=True), (DAYS, LANES))
    lrs[...] = jnp.broadcast_to(jnp.sum(logs, axis=1, keepdims=True), (8, LANES))

    def later(k, copy):
        @pl.when(z + k < NZ)
        def _():
            copy(k)

    def lr_copy(k):
        return remote(lrs, lrr.at[z], lsend.at[k], lrecv.at[z], z=lax.rem(z + k, NZ))

    def eb_copy(k):
        return remote(ebs, ebr.at[z], bsend.at[k], brecv.at[z], z=lax.rem(z + k, NZ))

    sub = lax.broadcasted_iota(jnp.int32, (8, LANES), 0)

    @pl.loop(0, F // LANES)
    def _(k):
        cols = columns(k)
        keep = jnp.broadcast_to(jnp.exp(lpv[:, cols]), (8, LANES))
        before = jnp.ones((8, LANES), f32)
        for j in range(NX):
            decay = None
            for i in range(8):
                r = pl.ds(j * DAYS + i * 8, 8)
                today = keep * rb[r, :]
                decay = today if i == 0 else decay * today
                dd[r, cols] = decay
            for n, shift in enumerate((1, 2, 4)):
                dk[n, j, :, cols] = jnp.where(sub >= shift, decay, 0.0)
                decay = jnp.where(sub >= shift, decay * pltpu.roll(decay, shift, 0), decay)
            first = jnp.where(sub >= 1, pltpu.roll(decay, 1, 0), 1.0)
            total = jnp.broadcast_to(decay[7:8], (8, LANES))
            dx[j, :, cols] = first
            dt[j, :, cols] = total
            vv[j, :, cols] = first * before
            before = before * total

    pl.semaphore_wait(met.at[1], 2)
    along_z(met.at[2], 4)

    def product(row, depth, first=False):
        at = pl.ds(pl.multiple_of(row, depth), depth)
        left = jnp.concatenate([er[j, :, at] for j in range(NX)], axis=0)
        for k in range(4):
            cols = pl.ds(k * 256, 256)
            term = jnp.dot(left, mb[at, cols], preferred_element_type=f32)
            acc[:, cols] = term if first else acc[:, cols] + term

    for n in range(2, 4):
        hop(n, ym, n)
        relay(n, ym, n)
        hop(7 - n, yp, 3 - n)
        relay(7 - n, yp, 3 - n)
    e_own.wait()
    for k in range(1, NX):
        xx = lax.rem(x + k, NX)
        remote(es.at[xx], er.at[xx], esend.at[k - 1], erecv.at[xx], x=xx).wait_recv()
    remote(m_in, mb.at[pl.ds(pl.multiple_of((y * 2 + mate) * 128, 128), 128), :], msend.at[8], mrecv.at[8], c=mate).wait_recv()
    product(y * 256, 256, True)
    pl.semaphore_wait(met.at[2], 2)
    for k in range(1, NX):
        pl.semaphore_signal(met.at[3], inc=1, device_id={"x": lax.rem(x + k, NX)}, device_id_type=MESH_ID)
    for k in FAR_FIRST:
        later(k, lambda k: lr_copy(k).start())
    for n in range(2):
        hop(9 + n, y2, n)
        relay(8 + n, y2, n)
        hop(11 + n, y2, 3 - n)
        relay(11 - n, y2, 3 - n)
    for n in range(4):
        relayed(n, ym, n)
    product(ym * 256, 256)
    for n in range(4):
        relayed(4 + n, yp, n)
    product(yp * 256, 256)
    product((y2 * 2 + c) * 128, 128)
    for n in range(4):
        relayed(8 + n, y2, n)
    product((y2 * 2 + mate) * 128, 128)

    @pl.loop(0, F // LANES)
    def _(k):
        cols = columns(k)
        log_keep = lpv[:, cols]
        keep = jnp.broadcast_to(jnp.exp(log_keep), (8, LANES))
        double = 2.0 * log_keep
        vol = jnp.broadcast_to(jnp.sqrt(-expm1(double)), (8, LANES))
        carried = jnp.zeros((8, LANES), f32)
        for j in range(NX):
            state = None
            for i in range(8):
                r = pl.ds(j * DAYS + i * 8, 8)
                shock = vol * acc[r, cols]
                state = shock if i == 0 else (keep * rb[r, :]) * state + shock
                acc[r, cols] = state
            for n, shift in enumerate((1, 2, 4)):
                state = state + dk[n, j, :, cols] * pltpu.roll(state, shift, 0)
            first = jnp.where(sub >= 1, pltpu.roll(state, 1, 0), 0.0)
            uu[j, :, cols] = first + dx[j, :, cols] * carried
            carried = dt[j, :, cols] * carried + jnp.broadcast_to(state[7:8], (8, LANES))
        ebs[pl.ds(k, 1), :] = carried[0:1]

    for k in FAR_FIRST:
        later(k, lambda k: eb_copy(k).start())

    @pl.loop(0, F // LANES)
    def _(k):
        cols = columns(k)
        paths = lax.broadcasted_iota(jnp.int32, (PATHS, LANES), 0)
        cbs[pl.ds(k, 1), :] = jnp.sum(jnp.where(paths == x, s0v[:, cols], 0.0), axis=0, keepdims=True)
        for j in range(NX):
            u, v = uu[j, :, cols], vv[j, :, cols]
            for i in range(8):
                r = pl.ds(j * DAYS + i * 8, 8)
                decay = dd[r, cols]
                acc[r, cols] = acc[r, cols] + decay * u
                dd[r, cols] = decay * v

    span = float(BLOCK) * lpd[...]

    @pl.loop(0, z)
    def _(u):
        remote(lrs, lrr.at[u], lsend.at[0], lrecv.at[u], z=u).wait_recv()
        lrr[pl.ds(u, 1)] = jnp.exp(span + lrr[u])[None]

    def entered(u, carry):
        remote(ebs, ebr.at[u], bsend.at[0], brecv.at[u], z=u).wait_recv()
        return lrr[u] * carry + ebr[u]

    cbs[...] = lax.fori_loop(0, z, entered, cbs[...])

    @pl.loop(0, F // LANES)
    def _(k):
        cols = columns(k)
        scen[:, cols] = (acc[:, cols] + dd[:, cols] * cbs[pl.ds(k, 1), :]).astype(bf16)

    res[...] = jnp.dot(scen[...], bm[...], preferred_element_type=f32)

    base = jnp.zeros((8, LANES), f32)
    exponent = []
    for j in range(NX):
        run = jnp.zeros((8, LANES), f32)
        sums = []
        for i in range(8):
            run = run + (0.03 + 0.3 * res[pl.ds(j * DAYS + i * 8, 8), pl.ds(K, LANES)])
            sums.append(run)
        total = run
        for shift in (1, 2, 4):
            total = total + jnp.where(sub >= shift, pltpu.roll(total, shift, 0), 0.0)
        start = base + jnp.where(sub >= 1, pltpu.roll(total, 1, 0), 0.0)
        base = base + jnp.broadcast_to(total[7:8], (8, LANES))
        exponent += [(-1.0 / 256.0) * (start + s) for s in sums]
    top = functools.reduce(jnp.maximum, exponent)
    top = jnp.max(top, axis=0, keepdims=True)
    worth = jnp.zeros((8, LANES), f32)
    for n, power in enumerate(exponent):
        worth = worth + jnp.exp(power - top) * res[pl.ds(n * 8, 8), pl.ds(0, K)]
    fs[0:1, :] = jnp.sum(worth, axis=0, keepdims=True)
    fs[1:2, :] = base[0:1]
    fs[2:3, :] = top
    fs[3:4, :] = top
    mine = z * NX + x
    fr[pl.ds(mine, 1)] = fs[...][None]

    pl.semaphore_wait(met.at[3], NX - 1)
    for k in (*FAR_FIRST, 0):
        for n in (2, 1, 3, 0):
            if k or n:
                remote(
                    fs, fr.at[mine], fsend.at[0], frecv.at[0], z=lax.rem(z + k, NZ), x=lax.rem(x + n, NX)
                ).start()

    for copy in (*up, *down, across, *onward, *relays, *r_copies, *e_copies):
        copy.wait_send()
    for k in FAR_FIRST:
        later(k, lambda k: lr_copy(k).wait_send())
        later(k, lambda k: eb_copy(k).wait_send())
    others = fr.at[pl.ds(0, NZ * NX - 1)]
    everyone = remote(others, others, fsend.at[0], frecv.at[0], z=lax.rem(z + 1, NZ))
    everyone.wait_recv()
    passed = jnp.zeros((NX, LANES), f32)
    value = jnp.zeros((NX, LANES), f32)
    for u in range(NZ):
        part = [jnp.concatenate([fr[u * NX + j, r : r + 1] for j in range(NX)], axis=0) for r in range(3)]
        value = value + jnp.exp(part[2] - (1.0 / 256.0) * passed) * part[0]
        passed = passed + part[1]
    out[...] = value * (1.0 / 4096.0)
    everyone.wait_send()


def local(e, s0, m, lp, reg, pay, sc):
    vmem, dma = pltpu.VMEM, pltpu.SemaphoreType.DMA
    return pl.pallas_call(
        kernel,
        out_shape=jax.ShapeDtypeStruct((PATHS, K), f32),
        in_specs=[pl.BlockSpec(memory_space=pl.ANY)] * 8,
        out_specs=pl.BlockSpec(memory_space=pltpu.VMEM),
        scratch_shapes=[
            vmem((DAYS, PATHS, F), bf16),
            vmem((PATHS, DAYS, F), bf16),
            vmem((NX, DAYS, F), bf16),
            vmem((F, F), bf16),
            vmem((F, 2 * K), bf16),
            vmem((BLOCK, F), f32),
            vmem((BLOCK, F), f32),
            vmem((BLOCK, F), bf16),
            vmem((BLOCK, 2 * K), f32),
            vmem((NX, 8, LANES), f32),
            vmem((BLOCK, LANES), f32),
            vmem((1, F), f32),
            vmem((8, LANES), f32),
            vmem((PATHS, F), f32),
            vmem((1, DAYS), f32),
            vmem((8, LANES), bf16),
            vmem((3, NX, 8, F), f32),
            vmem((NX, 8, F), f32),
            vmem((NX, 8, F), f32),
            vmem((NX, 8, F), f32),
            vmem((NX, 8, F), f32),
            vmem((8, LANES), f32),
            vmem((NZ, 8, LANES), f32),
            vmem((8, LANES), f32),
            vmem((NZ, 8, LANES), f32),
            vmem((8, LANES), f32),
            vmem((4, LANES), f32),
            vmem((NZ * NX, 4, LANES), f32),
            dma((9,)),
            dma((25,)), dma((25,)),
            dma((NX,)), dma((NX,)),
            dma((NX,)), dma((NX,)),
            dma((NZ,)), dma((NZ,)),
            dma((NZ,)), dma((NZ,)),
            dma((1,)), dma((1,)),
            pltpu.SemaphoreType.REGULAR((4,)),
        ],
        compiler_params=pltpu.CompilerParams(collective_id=0, has_side_effects=True, vmem_limit_bytes=60 << 20),
        name="scenarios",
    )(e, s0, m, lp.reshape(1, F), lp.reshape(8, LANES), reg.reshape(1, DAYS), pay, sc.reshape(8, LANES))


def solution(mesh):
    split = Mesh(mesh.devices.reshape(NY, NC, NZ, NX), ("y", "c", "z", "x"))
    paths, days = ("y", "c"), ("z", "x")
    placed = (P(days, paths, None), P(paths, None), P(paths, None), P(), P(days), P(), P())
    return jax.shard_map(local, mesh=split, in_specs=placed, out_specs=P(paths, None), check_vma=False)
```

```python
import functools

import jax
import jax.numpy as jnp
from jax import lax
from jax.experimental import pallas as pl
from jax.experimental.pallas import tpu as pltpu
from jax.sharding import Mesh
from jax.sharding import PartitionSpec as P

MESH_ID = pl.DeviceIdType.MESH
NY, NC, NZ, NX = 4, 2, 16, 4
DAYS, PATHS, F, K = 64, 4, 1024, 128
BLOCK = DAYS * NX
PIECE = 32
LANES = 128
FAR_FIRST = (8, 7, 9, 6, 10, 5, 11, 4, 12, 3, 13, 2, 14, 1, 15)
f32, bf16 = jnp.float32, jnp.bfloat16


def columns(k):
    return pl.ds(pl.multiple_of(k * LANES, LANES), LANES)


def expm1(v):
    total = jnp.ones_like(v)
    for n in range(10, 1, -1):
        total = 1.0 + total * v * (1.0 / n)
    return v * total


def remote(src, dst, send, recv, **where):
    return pltpu.make_async_remote_copy(
        src_ref=src, dst_ref=dst, send_sem=send, recv_sem=recv, device_id=where, device_id_type=MESH_ID
    )


def kernel(
    e_in, s0_in, m_in, lp_in, lpd_in, reg_in, pay_in, sc_in, out,
    ev, es, er, mb, bm, acc, dd, scen, res, rw, rb, lpv, lpd, s0v, regv, scv,
    dk, dx, dt, uu, vv, lrs, lrr, ebs, ebr, cbs, fs, fr,
    ld, msend, mrecv, esend, erecv, rsend, rrecv, lsend, lrecv, bsend, brecv, fsend, frecv, met,
):
    y, c, z, x = (lax.axis_index(a) for a in ("y", "c", "z", "x"))
    yp, ym, y2 = lax.rem(y + 1, NY), lax.rem(y + NY - 1, NY), lax.rem(y + 2, NY)
    mate = 1 - c

    def shard(yy, cc, piece):
        return mb.at[pl.ds(pl.multiple_of((yy * 2 + cc) * 128 + piece * PIECE, PIECE), PIECE), :]

    turn = (y, ym, yp, y2)
    width = F // NY

    def quarter(yy):
        return pl.ds(pl.multiple_of(yy * width, width), width)

    shocks = [
        pltpu.make_async_copy(e_in.at[:, :, quarter(yy)], ev.at[:, :, quarter(yy)], ld.at[9 + n])
        for n, yy in enumerate(turn)
    ]
    loads = [
        pltpu.make_async_copy(reg_in, regv, ld.at[1]),
        pltpu.make_async_copy(lp_in, lpv, ld.at[2]),
        pltpu.make_async_copy(lpd_in, lpd, ld.at[3]),
        pltpu.make_async_copy(s0_in, s0v, ld.at[4]),
        pltpu.make_async_copy(sc_in, scv, ld.at[5]),
        pltpu.make_async_copy(pay_in, bm.at[:, pl.ds(0, K)], ld.at[6]),
        pltpu.make_async_copy(m_in, mb.at[pl.ds(pl.multiple_of((y * 2 + c) * 128, 128), 128), :], ld.at[7]),
    ]
    for copy in (*shocks, *loads):
        copy.start()

    barrier = pltpu.get_barrier_semaphore()
    peers = [{"c": mate}, {"y": yp}, {"y": ym}]
    peers += [{"x": lax.rem(x + k, NX)} for k in range(1, NX)]
    for peer in peers:
        pl.semaphore_signal(barrier, inc=1, device_id=peer, device_id_type=MESH_ID)

    def along_z(semaphore, distance):
        for k in (distance, NZ - distance):
            pl.semaphore_signal(semaphore, inc=1, device_id={"z": lax.rem(z + k, NZ)}, device_id_type=MESH_ID)

    along_z(barrier, 1)

    pl.semaphore_wait(barrier, len(peers) + 2)
    along_z(met.at[0], 1)

    def m_copy(n, src, dst, **where):
        return remote(src, dst, msend.at[n], mrecv.at[n], **where)

    def own(piece):
        return m_in.at[pl.ds(piece * PIECE, PIECE), :]

    up = [m_copy(n, own(n), shard(y, c, n), y=yp) for n in range(4)]
    down = [m_copy(4 + n, own(n), shard(y, c, n), y=ym) for n in range(4)]
    across = m_copy(8, m_in, mb.at[pl.ds(pl.multiple_of((y * 2 + c) * 128, 128), 128), :], c=mate)
    for n in range(4):
        up[n].start()
        down[3 - n].start()
    across.start()

    loads[0].wait()
    rw[pl.ds(x, 1)] = jnp.ones((1, 8, LANES), f32)
    rw[pl.ds(x, 1), :, pl.ds(0, DAYS)] = jnp.broadcast_to(regv[...][None], (1, 8, DAYS))
    r_copies, e_copies = [], []
    for k in range(1, NX):
        xx = lax.rem(x + k, NX)
        r_copies.append(remote(rw.at[x], rw.at[x], rsend.at[k - 1], rrecv.at[x], x=xx))
        r_copies[-1].start()

    row = lax.broadcasted_iota(jnp.int32, (256, 256), 0)
    col = lax.broadcasted_iota(jnp.int32, (256, 256), 1)
    source = (((row & 7) * 8 + ((row >> 3) & 7)) << 2) + (row >> 6)
    order = (col == source).astype(f32).astype(bf16)
    e_own = []
    for n, yy in enumerate(turn):
        cols = quarter(yy)
        shocks[n].wait()
        flat = ev[:, :, cols].reshape(DAYS * PATHS, width)
        moved = jnp.dot(order, flat, preferred_element_type=f32).astype(bf16)
        for p in range(PATHS):
            es[p, :, cols] = moved[p * DAYS : (p + 1) * DAYS]
        for k in (2, 1, 3):
            xx = lax.rem(x + k, NX)
            e_copies.append(
                remote(es.at[xx, :, cols], er.at[x, :, cols], esend.at[n, k - 1], erecv.at[n, x], x=xx)
            )
            e_copies[-1].start()
        e_own.append(pltpu.make_async_copy(es.at[x, :, cols], er.at[x, :, cols], ld.at[13 + n]))
        e_own[-1].start()

    def shocks_here(n):
        cols = quarter(turn[n])
        e_own[n].wait()
        for k in range(1, NX):
            xx = lax.rem(x + k, NX)
            remote(
                es.at[xx, :, cols], er.at[xx, :, cols], esend.at[n, k - 1], erecv.at[n, xx], x=xx
            ).wait_recv()

    pl.semaphore_wait(met.at[0], 2)
    along_z(met.at[1], 2)
    for copy in loads[1:]:
        copy.wait()

    short = scv[...].astype(f32)
    for k in range(F // LANES):
        block = jnp.broadcast_to(short[k : k + 1], (LANES, LANES))
        bm[pl.ds(k * LANES, LANES), pl.ds(K, LANES)] = block.T.astype(bf16)

    def hop(n, yy, piece):
        remote(shard(yy, c, piece), shard(yy, c, piece), msend.at[n], mrecv.at[n], y=yp).wait_recv()

    def relay(n, yy, piece):
        relays.append(m_copy(13 + n, shard(yy, c, piece), shard(yy, c, piece), c=mate))
        relays[-1].start()

    def relayed(n, yy, piece):
        remote(shard(yy, mate, piece), shard(yy, mate, piece), msend.at[13 + n], mrecv.at[13 + n], c=mate).wait_recv()

    relays, onward = [], []
    for n in range(2):
        hop(n, ym, n)
        onward.append(m_copy(9 + n, shard(ym, c, n), shard(ym, c, n), y=yp))
        onward[-1].start()
        relay(n, ym, n)
        hop(7 - n, yp, 3 - n)
        onward.append(m_copy(11 + n, shard(yp, c, 3 - n), shard(yp, c, 3 - n), y=ym))
        onward[-1].start()
        relay(7 - n, yp, 3 - n)

    def r_wait(k):
        xx = lax.rem(x + k, NX)
        remote(rw.at[x], rw.at[xx], rsend.at[k - 1], rrecv.at[xx], x=xx).wait_recv()

    for k in range(1, NX):
        r_wait(k)
    rows = lax.broadcasted_iota(jnp.int32, (DAYS, LANES), 0)
    lanes = lax.broadcasted_iota(jnp.int32, (DAYS, LANES), 1)
    pick = lanes == (rows & 7) * 8 + (rows >> 3)
    logs = jnp.zeros((8, LANES), f32)
    for j in range(NX):
        logs = logs + jnp.log(rw[j])
        spread = jnp.where(pick, jnp.broadcast_to(rw[j, 0:1], (DAYS, LANES)), 0.0)
        rb[pl.ds(j * DAYS, DAYS), :] = jnp.broadcast_to(jnp.sum(spread, axis=1, keepdims=True), (DAYS, LANES))
    lrs[...] = jnp.broadcast_to(jnp.sum(logs, axis=1, keepdims=True), (8, LANES))

    def later(k, copy):
        @pl.when(z + k < NZ)
        def _():
            copy(k)

    def lr_copy(k):
        return remote(lrs, lrr.at[z], lsend.at[k], lrecv.at[z], z=lax.rem(z + k, NZ))

    def eb_copy(k):
        return remote(ebs, ebr.at[z], bsend.at[k], brecv.at[z], z=lax.rem(z + k, NZ))

    sub = lax.broadcasted_iota(jnp.int32, (8, LANES), 0)

    @pl.loop(0, F // LANES)
    def _(k):
        cols = columns(k)
        keep = jnp.broadcast_to(jnp.exp(lpv[:, cols]), (8, LANES))
        before = jnp.ones((8, LANES), f32)
        for j in range(NX):
            decay = None
            for i in range(8):
                r = pl.ds(j * DAYS + i * 8, 8)
                today = keep * rb[r, :]
                decay = today if i == 0 else decay * today
                dd[r, cols] = decay
            for n, shift in enumerate((1, 2, 4)):
                dk[n, j, :, cols] = jnp.where(sub >= shift, decay, 0.0)
                decay = jnp.where(sub >= shift, decay * pltpu.roll(decay, shift, 0), decay)
            first = jnp.where(sub >= 1, pltpu.roll(decay, 1, 0), 1.0)
            total = jnp.broadcast_to(decay[7:8], (8, LANES))
            dx[j, :, cols] = first
            dt[j, :, cols] = total
            vv[j, :, cols] = first * before
            before = before * total

    pl.semaphore_wait(met.at[1], 2)
    along_z(met.at[2], 4)

    def product(row, depth, first=False):
        at = pl.ds(pl.multiple_of(row, depth), depth)
        left = jnp.concatenate([er[j, :, at] for j in range(NX)], axis=0)
        for k in range(4):
            cols = pl.ds(k * 256, 256)
            term = jnp.dot(left, mb[at, cols], preferred_element_type=f32)
            acc[:, cols] = term if first else acc[:, cols] + term

    for n in range(2, 4):
        hop(n, ym, n)
        relay(n, ym, n)
        hop(7 - n, yp, 3 - n)
        relay(7 - n, yp, 3 - n)
    remote(m_in, mb.at[pl.ds(pl.multiple_of((y * 2 + mate) * 128, 128), 128), :], msend.at[8], mrecv.at[8], c=mate).wait_recv()
    shocks_here(0)
    product(y * 256, 256, True)
    pl.semaphore_wait(met.at[2], 2)
    for k in range(1, NX):
        pl.semaphore_signal(met.at[3], inc=1, device_id={"x": lax.rem(x + k, NX)}, device_id_type=MESH_ID)
    for k in FAR_FIRST:
        later(k, lambda k: lr_copy(k).start())
    for n in range(2):
        hop(9 + n, y2, n)
        relay(8 + n, y2, n)
        hop(11 + n, y2, 3 - n)
        relay(11 - n, y2, 3 - n)
    for n in range(4):
        relayed(n, ym, n)
    shocks_here(1)
    product(ym * 256, 256)
    for n in range(4):
        relayed(4 + n, yp, n)
    shocks_here(2)
    product(yp * 256, 256)
    shocks_here(3)
    product((y2 * 2 + c) * 128, 128)
    for n in range(4):
        relayed(8 + n, y2, n)
    product((y2 * 2 + mate) * 128, 128)

    @pl.loop(0, F // LANES)
    def _(k):
        cols = columns(k)
        log_keep = lpv[:, cols]
        keep = jnp.broadcast_to(jnp.exp(log_keep), (8, LANES))
        double = 2.0 * log_keep
        vol = jnp.broadcast_to(jnp.sqrt(-expm1(double)), (8, LANES))
        carried = jnp.zeros((8, LANES), f32)
        for j in range(NX):
            state = None
            for i in range(8):
                r = pl.ds(j * DAYS + i * 8, 8)
                shock = vol * acc[r, cols]
                state = shock if i == 0 else (keep * rb[r, :]) * state + shock
                acc[r, cols] = state
            for n, shift in enumerate((1, 2, 4)):
                state = state + dk[n, j, :, cols] * pltpu.roll(state, shift, 0)
            first = jnp.where(sub >= 1, pltpu.roll(state, 1, 0), 0.0)
            uu[j, :, cols] = first + dx[j, :, cols] * carried
            carried = dt[j, :, cols] * carried + jnp.broadcast_to(state[7:8], (8, LANES))
        ebs[pl.ds(k, 1), :] = carried[0:1]

    for k in FAR_FIRST:
        later(k, lambda k: eb_copy(k).start())

    @pl.loop(0, F // LANES)
    def _(k):
        cols = columns(k)
        paths = lax.broadcasted_iota(jnp.int32, (PATHS, LANES), 0)
        cbs[pl.ds(k, 1), :] = jnp.sum(jnp.where(paths == x, s0v[:, cols], 0.0), axis=0, keepdims=True)
        for j in range(NX):
            u, v = uu[j, :, cols], vv[j, :, cols]
            for i in range(8):
                r = pl.ds(j * DAYS + i * 8, 8)
                decay = dd[r, cols]
                acc[r, cols] = acc[r, cols] + decay * u
                dd[r, cols] = decay * v

    span = float(BLOCK) * lpd[...]

    @pl.loop(0, z)
    def _(u):
        remote(lrs, lrr.at[u], lsend.at[0], lrecv.at[u], z=u).wait_recv()
        lrr[pl.ds(u, 1)] = jnp.exp(span + lrr[u])[None]

    def entered(u, carry):
        remote(ebs, ebr.at[u], bsend.at[0], brecv.at[u], z=u).wait_recv()
        return lrr[u] * carry + ebr[u]

    cbs[...] = lax.fori_loop(0, z, entered, cbs[...])

    @pl.loop(0, F // LANES)
    def _(k):
        cols = columns(k)
        scen[:, cols] = (acc[:, cols] + dd[:, cols] * cbs[pl.ds(k, 1), :]).astype(bf16)

    res[...] = jnp.dot(scen[...], bm[...], preferred_element_type=f32)

    base = jnp.zeros((8, LANES), f32)
    exponent = []
    for j in range(NX):
        run = jnp.zeros((8, LANES), f32)
        sums = []
        for i in range(8):
            run = run + (0.03 + 0.3 * res[pl.ds(j * DAYS + i * 8, 8), pl.ds(K, LANES)])
            sums.append(run)
        total = run
        for shift in (1, 2, 4):
            total = total + jnp.where(sub >= shift, pltpu.roll(total, shift, 0), 0.0)
        start = base + jnp.where(sub >= 1, pltpu.roll(total, 1, 0), 0.0)
        base = base + jnp.broadcast_to(total[7:8], (8, LANES))
        exponent += [(-1.0 / 256.0) * (start + s) for s in sums]
    top = functools.reduce(jnp.maximum, exponent)
    top = jnp.max(top, axis=0, keepdims=True)
    worth = jnp.zeros((8, LANES), f32)
    for n, power in enumerate(exponent):
        worth = worth + jnp.exp(power - top) * res[pl.ds(n * 8, 8), pl.ds(0, K)]
    fs[0:1, :] = jnp.sum(worth, axis=0, keepdims=True)
    low = lax.broadcasted_iota(jnp.int32, (1, LANES), 1) < LANES // 2
    fs[1:2, :] = jnp.where(low, base[0:1], top)
    mine = z * NX + x
    fr[pl.ds(mine, 1)] = fs[...][None]

    pl.semaphore_wait(met.at[3], NX - 1)
    for k in (*FAR_FIRST, 0):
        for n in (2, 1, 3, 0):
            if k or n:
                remote(
                    fs, fr.at[mine], fsend.at[0], frecv.at[0], z=lax.rem(z + k, NZ), x=lax.rem(x + n, NX)
                ).start()

    for copy in (*up, *down, across, *onward, *relays, *r_copies, *e_copies):
        copy.wait_send()
    for k in FAR_FIRST:
        later(k, lambda k: lr_copy(k).wait_send())
        later(k, lambda k: eb_copy(k).wait_send())
    others = fr.at[pl.ds(0, NZ * NX - 1)]
    everyone = remote(others, others, fsend.at[0], frecv.at[0], z=lax.rem(z + 1, NZ))
    everyone.wait_recv()
    passed = jnp.zeros((NX, LANES), f32)
    value = jnp.zeros((NX, LANES), f32)
    for u in range(NZ):
        part, both = (
            jnp.concatenate([fr[u * NX + j, r : r + 1] for j in range(NX)], axis=0) for r in range(2)
        )
        swapped = pltpu.roll(both, LANES // 2, 1)
        value = value + jnp.exp(jnp.where(low, swapped, both) - (1.0 / 256.0) * passed) * part
        passed = passed + jnp.where(low, both, swapped)
    out[...] = value * (1.0 / 4096.0)
    everyone.wait_send()


def local(e, s0, m, lp, reg, pay, sc):
    vmem, dma = pltpu.VMEM, pltpu.SemaphoreType.DMA
    return pl.pallas_call(
        kernel,
        out_shape=jax.ShapeDtypeStruct((PATHS, K), f32),
        in_specs=[pl.BlockSpec(memory_space=pl.ANY)] * 8,
        out_specs=pl.BlockSpec(memory_space=pltpu.VMEM),
        scratch_shapes=[
            vmem((DAYS, PATHS, F), bf16),
            vmem((PATHS, DAYS, F), bf16),
            vmem((NX, DAYS, F), bf16),
            vmem((F, F), bf16),
            vmem((F, 2 * K), bf16),
            vmem((BLOCK, F), f32),
            vmem((BLOCK, F), f32),
            vmem((BLOCK, F), bf16),
            vmem((BLOCK, 2 * K), f32),
            vmem((NX, 8, LANES), f32),
            vmem((BLOCK, LANES), f32),
            vmem((1, F), f32),
            vmem((8, LANES), f32),
            vmem((PATHS, F), f32),
            vmem((1, DAYS), f32),
            vmem((8, LANES), bf16),
            vmem((3, NX, 8, F), f32),
            vmem((NX, 8, F), f32),
            vmem((NX, 8, F), f32),
            vmem((NX, 8, F), f32),
            vmem((NX, 8, F), f32),
            vmem((8, LANES), f32),
            vmem((NZ, 8, LANES), f32),
            vmem((8, LANES), f32),
            vmem((NZ, 8, LANES), f32),
            vmem((8, LANES), f32),
            vmem((2, LANES), f32),
            vmem((NZ * NX, 2, LANES), f32),
            dma((17,)),
            dma((25,)), dma((25,)),
            dma((NY, NX)), dma((NY, NX)),
            dma((NX,)), dma((NX,)),
            dma((NZ,)), dma((NZ,)),
            dma((NZ,)), dma((NZ,)),
            dma((1,)), dma((1,)),
            pltpu.SemaphoreType.REGULAR((4,)),
        ],
        compiler_params=pltpu.CompilerParams(collective_id=0, has_side_effects=True, vmem_limit_bytes=32 << 20),
        name="scenarios",
    )(
        *(
            pltpu.with_memory_space_constraint(a, pltpu.HBM)
            for a in (e, s0, m, lp.reshape(1, F), lp.reshape(8, LANES), reg.reshape(1, DAYS), pay, sc.reshape(8, LANES))
        )
    )


def solution(mesh):
    split = Mesh(mesh.devices.reshape(NY, NC, NZ, NX), ("y", "c", "z", "x"))
    paths, days = ("y", "c"), ("z", "x")
    placed = (P(days, paths, None), P(paths, None), P(paths, None), P(), P(days), P(), P())
    return jax.shard_map(local, mesh=split, in_specs=placed, out_specs=P(paths, None), check_vma=False)
```

```python
import functools

import jax
import jax.numpy as jnp
from jax import lax
from jax.experimental import pallas as pl
from jax.experimental.pallas import tpu as pltpu
from jax.sharding import Mesh
from jax.sharding import PartitionSpec as P

MESH_ID = pl.DeviceIdType.MESH
NY, NC, NZ, NX = 4, 2, 16, 4
DAYS, PATHS, F, K = 64, 4, 1024, 128
BLOCK = DAYS * NX
PIECE = 32
LANES = 128
FAR_FIRST = (8, 7, 9, 6, 10, 5, 11, 4, 12, 3, 13, 2, 14, 1, 15)
f32, bf16 = jnp.float32, jnp.bfloat16


def columns(k):
    return pl.ds(pl.multiple_of(k * LANES, LANES), LANES)


def expm1(v):
    total = jnp.ones_like(v)
    for n in range(10, 1, -1):
        total = 1.0 + total * v * (1.0 / n)
    return v * total


def remote(src, dst, send, recv, **where):
    return pltpu.make_async_remote_copy(
        src_ref=src, dst_ref=dst, send_sem=send, recv_sem=recv, device_id=where, device_id_type=MESH_ID
    )


def kernel(
    e_in, s0_in, m_in, lp_in, lpd_in, reg_in, pay_in, sc_in, out,
    ev, es, er, mb, bm, acc, dd, scen, res, rw, rb, lpv, lpd, s0v, regv, scv,
    dk, dx, dt, uu, vv, lrs, lrr, ebs, ebr, cbs, fs, fr,
    ld, msend, mrecv, esend, erecv, rsend, rrecv, lsend, lrecv, bsend, brecv, fsend, frecv, met,
):
    y, c, z, x = (lax.axis_index(a) for a in ("y", "c", "z", "x"))
    yp, ym, y2 = lax.rem(y + 1, NY), lax.rem(y + NY - 1, NY), lax.rem(y + 2, NY)
    mate = 1 - c

    def shard(yy, cc, piece):
        return mb.at[pl.ds(pl.multiple_of((yy * 2 + cc) * 128 + piece * PIECE, PIECE), PIECE), :]

    turn = (y, ym, yp, y2)
    width = F // NY

    def quarter(yy):
        return pl.ds(pl.multiple_of(yy * width, width), width)

    shocks = [
        pltpu.make_async_copy(e_in.at[:, :, quarter(yy)], ev.at[:, :, quarter(yy)], ld.at[9 + n])
        for n, yy in enumerate(turn)
    ]
    loads = [
        pltpu.make_async_copy(reg_in, regv, ld.at[1]),
        pltpu.make_async_copy(lp_in, lpv, ld.at[2]),
        pltpu.make_async_copy(lpd_in, lpd, ld.at[3]),
        pltpu.make_async_copy(s0_in, s0v, ld.at[4]),
        pltpu.make_async_copy(sc_in, scv, ld.at[5]),
        pltpu.make_async_copy(pay_in, bm.at[:, pl.ds(0, K)], ld.at[6]),
        pltpu.make_async_copy(m_in, mb.at[pl.ds(pl.multiple_of((y * 2 + c) * 128, 128), 128), :], ld.at[7]),
    ]
    for copy in (*shocks, *loads):
        copy.start()

    barrier = pltpu.get_barrier_semaphore()
    beside = [{"x": lax.rem(x + k, NX)} for k in (1, NX - 1)]
    peers = [{"c": mate}, {"y": yp}, {"y": ym}, *beside]
    for peer in peers:
        pl.semaphore_signal(barrier, inc=1, device_id=peer, device_id_type=MESH_ID)

    def along_z(semaphore, distance):
        for k in (distance, NZ - distance):
            pl.semaphore_signal(semaphore, inc=1, device_id={"z": lax.rem(z + k, NZ)}, device_id_type=MESH_ID)

    along_z(barrier, 1)

    pl.semaphore_wait(barrier, len(peers) + 2)
    along_z(met.at[0], 1)

    for peer in beside:
        pl.semaphore_signal(met.at[4], inc=1, device_id=peer, device_id_type=MESH_ID)

    def m_copy(n, src, dst, **where):
        return remote(src, dst, msend.at[n], mrecv.at[n], **where)

    odd = lax.rem(z, 2)
    rising = [2 * odd, 2 * odd + 1]
    falling = [2 - 2 * odd, 3 - 2 * odd]

    def own(piece):
        return m_in.at[pl.ds(pl.multiple_of(piece * PIECE, PIECE), PIECE), :]

    straight = []
    for n in range(2):
        straight.append(m_copy(n, own(rising[n]), shard(y, c, rising[n]), y=yp))
        straight.append(m_copy(2 + n, own(falling[n]), shard(y, c, falling[n]), y=ym))
    straight.append(m_copy(4, m_in, mb.at[pl.ds(pl.multiple_of((y * 2 + c) * 128, 128), 128), :], c=mate))
    for copy in straight:
        copy.start()

    loads[0].wait()
    rw[pl.ds(x, 1)] = jnp.ones((1, 8, LANES), f32)
    rw[pl.ds(x, 1), :, pl.ds(0, DAYS)] = jnp.broadcast_to(regv[...][None], (1, 8, DAYS))
    r_copies, e_copies = [], []

    row = lax.broadcasted_iota(jnp.int32, (256, 256), 0)
    col = lax.broadcasted_iota(jnp.int32, (256, 256), 1)
    source = (((row & 7) * 8 + ((row >> 3) & 7)) << 2) + (row >> 6)
    order = (col == source).astype(f32).astype(bf16)
    e_own = []
    for n, yy in enumerate(turn):
        cols = quarter(yy)
        shocks[n].wait()
        flat = ev[:, :, cols].reshape(DAYS * PATHS, width)
        moved = jnp.dot(order, flat, preferred_element_type=f32).astype(bf16)
        for p in range(PATHS):
            es[p, :, cols] = moved[p * DAYS : (p + 1) * DAYS]
        if n == 0:
            pl.semaphore_wait(met.at[4], 2)
            for k in (2, 1, 3):
                xx = lax.rem(x + k, NX)
                r_copies.append(remote(rw.at[x], rw.at[x], rsend.at[k - 1], rrecv.at[x], x=xx))
                r_copies[-1].start()
        for k in (2, 1, 3):
            xx = lax.rem(x + k, NX)
            e_copies.append(
                remote(es.at[xx, :, cols], er.at[x, :, cols], esend.at[n, k - 1], erecv.at[n, x], x=xx)
            )
            e_copies[-1].start()
        e_own.append(pltpu.make_async_copy(es.at[x, :, cols], er.at[x, :, cols], ld.at[13 + n]))
        e_own[-1].start()

    def shocks_here(n):
        cols = quarter(turn[n])
        e_own[n].wait()
        for k in range(1, NX):
            xx = lax.rem(x + k, NX)
            remote(
                es.at[xx, :, cols], er.at[xx, :, cols], esend.at[n, k - 1], erecv.at[n, xx], x=xx
            ).wait_recv()

    def hop(n, yy, piece):
        remote(shard(yy, c, piece), shard(yy, c, piece), msend.at[n], mrecv.at[n], y=yp).wait_recv()

    def passed_on(n, yy, piece, **where):
        onward.append(m_copy(n, shard(yy, c, piece), shard(yy, c, piece), **where))
        onward[-1].start()

    def relayed(n, yy, piece):
        remote(shard(yy, mate, piece), shard(yy, mate, piece), msend.at[n], mrecv.at[n], c=mate).wait_recv()

    onward = []
    aside = [{"z": lax.rem(z + 1, NZ)}, {"z": lax.rem(z + NZ - 1, NZ)}]
    for n in range(2):
        hop(n, ym, rising[n])
        passed_on(5 + n, ym, rising[n], y=yp)
        passed_on(9 + n, ym, rising[n], **aside[n])
        passed_on(13 + n, ym, rising[n], c=mate)
        hop(2 + n, yp, falling[n])
        passed_on(7 + n, yp, falling[n], y=ym)
        passed_on(11 + n, yp, falling[n], **aside[n])
        passed_on(15 + n, yp, falling[n], c=mate)

    pl.semaphore_wait(met.at[0], 2)
    along_z(met.at[1], 2)
    for copy in loads[1:]:
        copy.wait()

    short = scv[...].astype(f32)
    for k in range(F // LANES):
        block = jnp.broadcast_to(short[k : k + 1], (LANES, LANES))
        bm[pl.ds(k * LANES, LANES), pl.ds(K, LANES)] = block.T.astype(bf16)

    def r_wait(k):
        xx = lax.rem(x + k, NX)
        remote(rw.at[x], rw.at[xx], rsend.at[k - 1], rrecv.at[xx], x=xx).wait_recv()

    for k in range(1, NX):
        r_wait(k)
    rows = lax.broadcasted_iota(jnp.int32, (DAYS, LANES), 0)
    lanes = lax.broadcasted_iota(jnp.int32, (DAYS, LANES), 1)
    pick = lanes == (rows & 7) * 8 + (rows >> 3)
    logs = jnp.zeros((8, LANES), f32)
    for j in range(NX):
        logs = logs + jnp.log(rw[j])
        spread = jnp.where(pick, jnp.broadcast_to(rw[j, 0:1], (DAYS, LANES)), 0.0)
        rb[pl.ds(j * DAYS, DAYS), :] = jnp.broadcast_to(jnp.sum(spread, axis=1, keepdims=True), (DAYS, LANES))
    lrs[...] = jnp.broadcast_to(jnp.sum(logs, axis=1, keepdims=True), (8, LANES))

    def later(k, copy):
        @pl.when(z + k < NZ)
        def _():
            copy(k)

    def lr_copy(k):
        return remote(lrs, lrr.at[z], lsend.at[k], lrecv.at[z], z=lax.rem(z + k, NZ))

    def eb_copy(k):
        return remote(ebs, ebr.at[z], bsend.at[k], brecv.at[z], z=lax.rem(z + k, NZ))

    sub = lax.broadcasted_iota(jnp.int32, (8, LANES), 0)

    @pl.loop(0, F // LANES)
    def _(k):
        cols = columns(k)
        keep = jnp.broadcast_to(jnp.exp(lpv[:, cols]), (8, LANES))
        before = jnp.ones((8, LANES), f32)
        for j in range(NX):
            decay = None
            for i in range(8):
                r = pl.ds(j * DAYS + i * 8, 8)
                today = keep * rb[r, :]
                decay = today if i == 0 else decay * today
                dd[r, cols] = decay
            for n, shift in enumerate((1, 2, 4)):
                dk[n, j, :, cols] = jnp.where(sub >= shift, decay, 0.0)
                decay = jnp.where(sub >= shift, decay * pltpu.roll(decay, shift, 0), decay)
            first = jnp.where(sub >= 1, pltpu.roll(decay, 1, 0), 1.0)
            total = jnp.broadcast_to(decay[7:8], (8, LANES))
            dx[j, :, cols] = first
            dt[j, :, cols] = total
            vv[j, :, cols] = first * before
            before = before * total

    pl.semaphore_wait(met.at[1], 2)
    along_z(met.at[2], 4)

    def product(row, depth, first=False):
        at = pl.ds(pl.multiple_of(row, depth), depth)
        left = jnp.concatenate([er[j, :, at] for j in range(NX)], axis=0)
        for k in range(4):
            cols = pl.ds(k * 256, 256)
            term = jnp.dot(left, mb[at, cols], preferred_element_type=f32)
            acc[:, cols] = term if first else acc[:, cols] + term

    for n in range(2):
        hop(9 + n, ym, falling[n])
        passed_on(17 + n, ym, falling[n], c=mate)
        hop(11 + n, yp, rising[n])
        passed_on(19 + n, yp, rising[n], c=mate)
    for n in range(2):
        hop(5 + n, y2, rising[n])
        passed_on(21 + n, y2, rising[n], c=mate)
        hop(7 + n, y2, falling[n])
        passed_on(23 + n, y2, falling[n], c=mate)
    pl.semaphore_wait(met.at[2], 2)
    for k in range(1, NX):
        pl.semaphore_signal(met.at[3], inc=1, device_id={"x": lax.rem(x + k, NX)}, device_id_type=MESH_ID)
    for k in FAR_FIRST:
        later(k, lambda k: lr_copy(k).start())
    remote(m_in, mb.at[pl.ds(pl.multiple_of((y * 2 + mate) * 128, 128), 128), :], msend.at[4], mrecv.at[4], c=mate).wait_recv()
    shocks_here(0)
    product(y * 256, 256, True)
    for n in range(2):
        relayed(13 + n, ym, rising[n])
        relayed(17 + n, ym, falling[n])
    shocks_here(1)
    product(ym * 256, 256)
    for n in range(2):
        relayed(15 + n, yp, falling[n])
        relayed(19 + n, yp, rising[n])
    shocks_here(2)
    product(yp * 256, 256)
    for n in range(2):
        relayed(21 + n, y2, rising[n])
        relayed(23 + n, y2, falling[n])
    shocks_here(3)
    product(y2 * 256, 256)

    @pl.loop(0, F // LANES)
    def _(k):
        cols = columns(k)
        log_keep = lpv[:, cols]
        keep = jnp.broadcast_to(jnp.exp(log_keep), (8, LANES))
        double = 2.0 * log_keep
        vol = jnp.broadcast_to(jnp.sqrt(-expm1(double)), (8, LANES))
        carried = jnp.zeros((8, LANES), f32)
        for j in range(NX):
            state = None
            for i in range(8):
                r = pl.ds(j * DAYS + i * 8, 8)
                shock = vol * acc[r, cols]
                state = shock if i == 0 else (keep * rb[r, :]) * state + shock
                acc[r, cols] = state
            for n, shift in enumerate((1, 2, 4)):
                state = state + dk[n, j, :, cols] * pltpu.roll(state, shift, 0)
            first = jnp.where(sub >= 1, pltpu.roll(state, 1, 0), 0.0)
            uu[j, :, cols] = first + dx[j, :, cols] * carried
            carried = dt[j, :, cols] * carried + jnp.broadcast_to(state[7:8], (8, LANES))
        ebs[pl.ds(k, 1), :] = carried[0:1]

    for k in FAR_FIRST:
        later(k, lambda k: eb_copy(k).start())

    @pl.loop(0, F // LANES)
    def _(k):
        cols = columns(k)
        paths = lax.broadcasted_iota(jnp.int32, (PATHS, LANES), 0)
        cbs[pl.ds(k, 1), :] = jnp.sum(jnp.where(paths == x, s0v[:, cols], 0.0), axis=0, keepdims=True)
        for j in range(NX):
            u, v = uu[j, :, cols], vv[j, :, cols]
            for i in range(8):
                r = pl.ds(j * DAYS + i * 8, 8)
                decay = dd[r, cols]
                acc[r, cols] = acc[r, cols] + decay * u
                dd[r, cols] = decay * v

    span = float(BLOCK) * lpd[...]

    @pl.loop(0, z)
    def _(u):
        remote(lrs, lrr.at[u], lsend.at[0], lrecv.at[u], z=u).wait_recv()
        lrr[pl.ds(u, 1)] = jnp.exp(span + lrr[u])[None]

    def entered(u, carry):
        remote(ebs, ebr.at[u], bsend.at[0], brecv.at[u], z=u).wait_recv()
        return lrr[u] * carry + ebr[u]

    cbs[...] = lax.fori_loop(0, z, entered, cbs[...])

    @pl.loop(0, F // LANES)
    def _(k):
        cols = columns(k)
        scen[:, cols] = (acc[:, cols] + dd[:, cols] * cbs[pl.ds(k, 1), :]).astype(bf16)

    res[...] = jnp.dot(scen[...], bm[...], preferred_element_type=f32)

    base = jnp.zeros((8, LANES), f32)
    exponent = []
    for j in range(NX):
        run = jnp.zeros((8, LANES), f32)
        sums = []
        for i in range(8):
            run = run + (0.03 + 0.3 * res[pl.ds(j * DAYS + i * 8, 8), pl.ds(K, LANES)])
            sums.append(run)
        total = run
        for shift in (1, 2, 4):
            total = total + jnp.where(sub >= shift, pltpu.roll(total, shift, 0), 0.0)
        start = base + jnp.where(sub >= 1, pltpu.roll(total, 1, 0), 0.0)
        base = base + jnp.broadcast_to(total[7:8], (8, LANES))
        exponent += [(-1.0 / 256.0) * (start + s) for s in sums]
    top = functools.reduce(jnp.maximum, exponent)
    top = jnp.max(top, axis=0, keepdims=True)
    worth = jnp.zeros((8, LANES), f32)
    for n, power in enumerate(exponent):
        worth = worth + jnp.exp(power - top) * res[pl.ds(n * 8, 8), pl.ds(0, K)]
    fs[0:1, :] = jnp.sum(worth, axis=0, keepdims=True)
    low = lax.broadcasted_iota(jnp.int32, (1, LANES), 1) < LANES // 2
    fs[1:2, :] = jnp.where(low, base[0:1], top)
    mine = z * NX + x
    fr[pl.ds(mine, 1)] = fs[...][None]

    pl.semaphore_wait(met.at[3], NX - 1)
    for k in (*FAR_FIRST, 0):
        for n in (2, 1, 3, 0):
            if k or n:
                remote(
                    fs, fr.at[mine], fsend.at[0], frecv.at[0], z=lax.rem(z + k, NZ), x=lax.rem(x + n, NX)
                ).start()

    for copy in (*straight, *onward, *r_copies, *e_copies):
        copy.wait_send()
    for k in FAR_FIRST:
        later(k, lambda k: lr_copy(k).wait_send())
        later(k, lambda k: eb_copy(k).wait_send())
    others = fr.at[pl.ds(0, NZ * NX - 1)]
    everyone = remote(others, others, fsend.at[0], frecv.at[0], z=lax.rem(z + 1, NZ))
    everyone.wait_recv()
    passed = jnp.zeros((NX, LANES), f32)
    value = jnp.zeros((NX, LANES), f32)
    for u in range(NZ):
        part, both = (
            jnp.concatenate([fr[u * NX + j, r : r + 1] for j in range(NX)], axis=0) for r in range(2)
        )
        swapped = pltpu.roll(both, LANES // 2, 1)
        value = value + jnp.exp(jnp.where(low, swapped, both) - (1.0 / 256.0) * passed) * part
        passed = passed + jnp.where(low, both, swapped)
    out[...] = value * (1.0 / 4096.0)
    everyone.wait_send()


def local(e, s0, m, lp, reg, pay, sc):
    vmem, dma = pltpu.VMEM, pltpu.SemaphoreType.DMA
    return pl.pallas_call(
        kernel,
        out_shape=jax.ShapeDtypeStruct((PATHS, K), f32),
        in_specs=[pl.BlockSpec(memory_space=pl.ANY)] * 8,
        out_specs=pl.BlockSpec(memory_space=pltpu.VMEM),
        scratch_shapes=[
            vmem((DAYS, PATHS, F), bf16),
            vmem((PATHS, DAYS, F), bf16),
            vmem((NX, DAYS, F), bf16),
            vmem((F, F), bf16),
            vmem((F, 2 * K), bf16),
            vmem((BLOCK, F), f32),
            vmem((BLOCK, F), f32),
            vmem((BLOCK, F), bf16),
            vmem((BLOCK, 2 * K), f32),
            vmem((NX, 8, LANES), f32),
            vmem((BLOCK, LANES), f32),
            vmem((1, F), f32),
            vmem((8, LANES), f32),
            vmem((PATHS, F), f32),
            vmem((1, DAYS), f32),
            vmem((8, LANES), bf16),
            vmem((3, NX, 8, F), f32),
            vmem((NX, 8, F), f32),
            vmem((NX, 8, F), f32),
            vmem((NX, 8, F), f32),
            vmem((NX, 8, F), f32),
            vmem((8, LANES), f32),
            vmem((NZ, 8, LANES), f32),
            vmem((8, LANES), f32),
            vmem((NZ, 8, LANES), f32),
            vmem((8, LANES), f32),
            vmem((2, LANES), f32),
            vmem((NZ * NX, 2, LANES), f32),
            dma((17,)),
            dma((25,)), dma((25,)),
            dma((NY, NX)), dma((NY, NX)),
            dma((NX,)), dma((NX,)),
            dma((NZ,)), dma((NZ,)),
            dma((NZ,)), dma((NZ,)),
            dma((1,)), dma((1,)),
            pltpu.SemaphoreType.REGULAR((5,)),
        ],
        compiler_params=pltpu.CompilerParams(collective_id=0, has_side_effects=True, vmem_limit_bytes=32 << 20),
        name="scenarios",
    )(
        *(
            pltpu.with_memory_space_constraint(a, pltpu.HBM)
            for a in (e, s0, m, lp.reshape(1, F), lp.reshape(8, LANES), reg.reshape(1, DAYS), pay, sc.reshape(8, LANES))
        )
    )


def solution(mesh):
    split = Mesh(mesh.devices.reshape(NY, NC, NZ, NX), ("y", "c", "z", "x"))
    paths, days = ("y", "c"), ("z", "x")
    placed = (P(days, paths, None), P(paths, None), P(paths, None), P(), P(days), P(), P())
    return jax.shard_map(local, mesh=split, in_specs=placed, out_specs=P(paths, None), check_vma=False)
```

```python
import functools

import jax
import jax.numpy as jnp
from jax import lax
from jax.experimental import pallas as pl
from jax.experimental.pallas import tpu as pltpu
from jax.sharding import Mesh
from jax.sharding import PartitionSpec as P

MESH_ID = pl.DeviceIdType.MESH
NY, NC, NZ, NX = 4, 2, 16, 4
DAYS, PATHS, F, K = 64, 4, 1024, 128
BLOCK = DAYS * NX
PIECE = 16
HALF = 64 // PIECE
LANES = 128
FAR_FIRST = (8, 7, 9, 6, 10, 5, 11, 4, 12, 3, 13, 2, 14, 1, 15)
f32, bf16 = jnp.float32, jnp.bfloat16


def columns(k):
    return pl.ds(pl.multiple_of(k * LANES, LANES), LANES)


def expm1(v):
    total = jnp.ones_like(v)
    for n in range(10, 1, -1):
        total = 1.0 + total * v * (1.0 / n)
    return v * total


def remote(src, dst, send, recv, **where):
    return pltpu.make_async_remote_copy(
        src_ref=src, dst_ref=dst, send_sem=send, recv_sem=recv, device_id=where, device_id_type=MESH_ID
    )


def kernel(
    e_in, s0_in, m_in, lp_in, lpd_in, reg_in, pay_in, sc_in, out,
    ev, es, er, mb, bm, acc, dd, res, rw, rb, lpv, lpd, s0v, regv, scv,
    dk, dx, dt, uu, vv, lrs, lrr, ebs, ebr, cbs, fs, fr,
    ld, msend, mrecv, esend, erecv, rsend, rrecv, lsend, lrecv, bsend, brecv, fsend, frecv, met,
):
    y, c, z, x = (lax.axis_index(a) for a in ("y", "c", "z", "x"))
    yp, ym, y2 = lax.rem(y + 1, NY), lax.rem(y + NY - 1, NY), lax.rem(y + 2, NY)
    mate = 1 - c

    barrier = pltpu.get_barrier_semaphore()
    beside = [{"x": lax.rem(x + k, NX)} for k in (1, NX - 1)]
    peers = [{"c": mate}, {"y": yp}, {"y": ym}, *beside]
    for peer in peers:
        pl.semaphore_signal(barrier, inc=1, device_id=peer, device_id_type=MESH_ID)

    def along_z(semaphore, distance):
        for k in (distance, NZ - distance):
            pl.semaphore_signal(semaphore, inc=1, device_id={"z": lax.rem(z + k, NZ)}, device_id_type=MESH_ID)

    along_z(barrier, 1)

    def shard(yy, cc, piece):
        return mb.at[pl.ds(pl.multiple_of((yy * 2 + cc) * 128 + piece * PIECE, PIECE), PIECE), :]

    turn = (y, ym, yp, y2)
    width = F // NY

    def quarter(yy):
        return pl.ds(pl.multiple_of(yy * width, width), width)

    shocks = [
        pltpu.make_async_copy(e_in.at[:, :, quarter(yy)], ev.at[:, :, quarter(yy)], ld.at[9 + n])
        for n, yy in enumerate(turn)
    ]
    loads = [
        pltpu.make_async_copy(reg_in, regv, ld.at[1]),
        pltpu.make_async_copy(lp_in, lpv, ld.at[2]),
        pltpu.make_async_copy(lpd_in, lpd, ld.at[3]),
        pltpu.make_async_copy(s0_in, s0v, ld.at[4]),
        pltpu.make_async_copy(sc_in, scv, ld.at[5]),
        pltpu.make_async_copy(pay_in, bm.at[:, pl.ds(0, K)], ld.at[6]),
        pltpu.make_async_copy(m_in, mb.at[pl.ds(pl.multiple_of((y * 2 + c) * 128, 128), 128), :], ld.at[7]),
    ]
    for copy in (*shocks, *loads):
        copy.start()

    pl.semaphore_wait(barrier, len(peers) + 2)
    along_z(met.at[0], 1)

    for peer in beside:
        pl.semaphore_signal(met.at[4], inc=1, device_id=peer, device_id_type=MESH_ID)

    def group(g, n):
        return g * HALF + n

    def m_copy(n, src, dst, **where):
        return remote(src, dst, msend.at[n], mrecv.at[n], **where)

    odd = lax.rem(z, 2)
    rising = [HALF * odd + n for n in range(HALF)]
    falling = [HALF * (1 - odd) + n for n in range(HALF)]

    def own(piece):
        return m_in.at[pl.ds(pl.multiple_of(piece * PIECE, PIECE), PIECE), :]

    straight = []
    for n in range(HALF):
        straight.append(m_copy(group(0, n), own(rising[n]), shard(y, c, rising[n]), y=yp))
        straight.append(m_copy(group(1, n), own(falling[n]), shard(y, c, falling[n]), y=ym))
    straight.append(m_copy(group(12, 0), m_in, mb.at[pl.ds(pl.multiple_of((y * 2 + c) * 128, 128), 128), :], c=mate))
    for copy in straight:
        copy.start()

    loads[0].wait()
    rw[pl.ds(x, 1)] = jnp.ones((1, 8, LANES), f32)
    rw[pl.ds(x, 1), :, pl.ds(0, DAYS)] = jnp.broadcast_to(regv[...][None], (1, 8, DAYS))
    r_copies, e_copies = [], []

    row = lax.broadcasted_iota(jnp.int32, (256, 256), 0)
    col = lax.broadcasted_iota(jnp.int32, (256, 256), 1)
    source = (((row & 7) * 8 + ((row >> 3) & 7)) << 2) + (row >> 6)
    order = (col == source).astype(f32).astype(bf16)
    e_own = []
    for n, yy in enumerate(turn):
        cols = quarter(yy)
        shocks[n].wait()
        flat = ev[:, :, cols].reshape(DAYS * PATHS, width)
        moved = jnp.dot(order, flat, preferred_element_type=f32).astype(bf16)
        for p in range(PATHS):
            es[p, :, cols] = moved[p * DAYS : (p + 1) * DAYS]
        if n == 0:
            pl.semaphore_wait(met.at[0], 2)
            along_z(met.at[1], 2)
            pl.semaphore_wait(met.at[4], 2)
            for k in (2, 1, 3):
                xx = lax.rem(x + k, NX)
                r_copies.append(remote(rw.at[x], rw.at[x], rsend.at[k - 1], rrecv.at[x], x=xx))
                r_copies[-1].start()
        for k in (2, 1, 3):
            xx = lax.rem(x + k, NX)
            e_copies.append(
                remote(es.at[xx, :, cols], er.at[x, :, cols], esend.at[n, k - 1], erecv.at[n, x], x=xx)
            )
            e_copies[-1].start()
        e_own.append(pltpu.make_async_copy(es.at[x, :, cols], er.at[x, :, cols], ld.at[13 + n]))
        e_own[-1].start()

    pl.semaphore_wait(met.at[1], 2)
    along_z(met.at[2], 4)

    def shocks_here(n):
        cols = quarter(turn[n])
        e_own[n].wait()
        for k in range(1, NX):
            xx = lax.rem(x + k, NX)
            remote(
                es.at[xx, :, cols], er.at[xx, :, cols], esend.at[n, k - 1], erecv.at[n, xx], x=xx
            ).wait_recv()

    def hop(n, yy, piece):
        remote(shard(yy, c, piece), shard(yy, c, piece), msend.at[n], mrecv.at[n], y=yp).wait_recv()

    def passed_on(n, yy, piece, **where):
        onward.append(m_copy(n, shard(yy, c, piece), shard(yy, c, piece), **where))
        onward[-1].start()

    def relayed(n, yy, piece):
        remote(shard(yy, mate, piece), shard(yy, mate, piece), msend.at[n], mrecv.at[n], c=mate).wait_recv()

    onward = []
    aside = [{"z": lax.rem(z + 1, NZ)}, {"z": lax.rem(z + NZ - 1, NZ)}]
    for n in range(HALF):
        hop(group(0, n), ym, rising[n])
        passed_on(group(2, n), ym, rising[n], y=yp)
        passed_on(group(4, n), ym, rising[n], **aside[n % 2])
        passed_on(group(6, n), ym, rising[n], c=mate)
        hop(group(1, n), yp, falling[n])
        passed_on(group(3, n), yp, falling[n], y=ym)
        passed_on(group(5, n), yp, falling[n], **aside[n % 2])
        passed_on(group(7, n), yp, falling[n], c=mate)

    for copy in loads[1:]:
        copy.wait()

    short = scv[...].astype(f32)
    for k in range(F // LANES):
        block = jnp.broadcast_to(short[k : k + 1], (LANES, LANES))
        bm[pl.ds(k * LANES, LANES), pl.ds(K, LANES)] = block.T.astype(bf16)

    def r_wait(k):
        xx = lax.rem(x + k, NX)
        remote(rw.at[x], rw.at[xx], rsend.at[k - 1], rrecv.at[xx], x=xx).wait_recv()

    for k in range(1, NX):
        r_wait(k)
    rows = lax.broadcasted_iota(jnp.int32, (DAYS, LANES), 0)
    lanes = lax.broadcasted_iota(jnp.int32, (DAYS, LANES), 1)
    pick = lanes == (rows & 7) * 8 + (rows >> 3)
    logs = jnp.zeros((8, LANES), f32)
    for j in range(NX):
        logs = logs + jnp.log(rw[j])
        spread = jnp.where(pick, jnp.broadcast_to(rw[j, 0:1], (DAYS, LANES)), 0.0)
        rb[pl.ds(j * DAYS, DAYS), :] = jnp.broadcast_to(jnp.sum(spread, axis=1, keepdims=True), (DAYS, LANES))
    lrs[...] = jnp.broadcast_to(jnp.sum(logs, axis=1, keepdims=True), (8, LANES))

    def later(k, copy):
        @pl.when(z + k < NZ)
        def _():
            copy(k)

    def lr_copy(k):
        return remote(lrs, lrr.at[z], lsend.at[k], lrecv.at[z], z=lax.rem(z + k, NZ))

    def eb_copy(k):
        return remote(ebs, ebr.at[z], bsend.at[k], brecv.at[z], z=lax.rem(z + k, NZ))

    sub = lax.broadcasted_iota(jnp.int32, (8, LANES), 0)

    @pl.loop(0, F // LANES)
    def _(k):
        cols = columns(k)
        keep = jnp.broadcast_to(jnp.exp(lpv[:, cols]), (8, LANES))
        before = jnp.ones((8, LANES), f32)
        for j in range(NX):
            decay = None
            for i in range(8):
                r = pl.ds(j * DAYS + i * 8, 8)
                today = keep * rb[r, :]
                decay = today if i == 0 else decay * today
                dd[r, cols] = decay
            for n, shift in enumerate((1, 2, 4)):
                dk[n, j, :, cols] = jnp.where(sub >= shift, decay, 0.0)
                decay = jnp.where(sub >= shift, decay * pltpu.roll(decay, shift, 0), decay)
            first = jnp.where(sub >= 1, pltpu.roll(decay, 1, 0), 1.0)
            total = jnp.broadcast_to(decay[7:8], (8, LANES))
            dx[j, :, cols] = first
            dt[j, :, cols] = total
            vv[j, :, cols] = first * before
            before = before * total

    def product(row, depth, first=False):
        at = pl.ds(pl.multiple_of(row, depth), depth)
        left = jnp.concatenate([er[j, :, at] for j in range(NX)], axis=0)
        for k in range(4):
            cols = pl.ds(k * 256, 256)
            term = jnp.dot(left, mb[at, cols], preferred_element_type=f32)
            acc[:, cols] = term if first else acc[:, cols] + term

    for n in range(HALF):
        hop(group(4, n), ym, falling[n])
        passed_on(group(8, n), ym, falling[n], c=mate)
        hop(group(5, n), yp, rising[n])
        passed_on(group(9, n), yp, rising[n], c=mate)
    for n in range(HALF):
        hop(group(2, n), y2, rising[n])
        passed_on(group(10, n), y2, rising[n], c=mate)
        hop(group(3, n), y2, falling[n])
        passed_on(group(11, n), y2, falling[n], c=mate)
    pl.semaphore_wait(met.at[2], 2)
    for k in range(1, NX):
        pl.semaphore_signal(met.at[3], inc=1, device_id={"x": lax.rem(x + k, NX)}, device_id_type=MESH_ID)
    for k in FAR_FIRST:
        later(k, lambda k: lr_copy(k).start())
    remote(m_in, mb.at[pl.ds(pl.multiple_of((y * 2 + mate) * 128, 128), 128), :], msend.at[group(12, 0)], mrecv.at[group(12, 0)], c=mate).wait_recv()
    shocks_here(0)
    product(y * 256, 256, True)
    for n in range(HALF):
        relayed(group(6, n), ym, rising[n])
        relayed(group(8, n), ym, falling[n])
    shocks_here(1)
    product(ym * 256, 256)
    for n in range(HALF):
        relayed(group(7, n), yp, falling[n])
        relayed(group(9, n), yp, rising[n])
    shocks_here(2)
    product(yp * 256, 256)
    shocks_here(3)
    for n in range(HALF):
        relayed(group(10, n), y2, rising[n])
        relayed(group(11, n), y2, falling[n])

    last = quarter(y2)
    left = jnp.concatenate([er[j, :, last] for j in range(NX)], axis=0)
    for w in range(4):
        wide = pl.ds(w * 256, 256)
        acc[:, wide] = acc[:, wide] + jnp.dot(left, mb[last, wide], preferred_element_type=f32)
        for k in (2 * w, 2 * w + 1):
            cols = pl.ds(k * LANES, LANES)
            log_keep = lpv[:, cols]
            keep = jnp.broadcast_to(jnp.exp(log_keep), (8, LANES))
            double = 2.0 * log_keep
            vol = jnp.broadcast_to(jnp.sqrt(-expm1(double)), (8, LANES))
            carried = jnp.zeros((8, LANES), f32)
            for j in range(NX):
                state = None
                for i in range(8):
                    r = pl.ds(j * DAYS + i * 8, 8)
                    shock = vol * acc[r, cols]
                    state = shock if i == 0 else (keep * rb[r, :]) * state + shock
                    acc[r, cols] = state
                for n, shift in enumerate((1, 2, 4)):
                    state = state + dk[n, j, :, cols] * pltpu.roll(state, shift, 0)
                first = jnp.where(sub >= 1, pltpu.roll(state, 1, 0), 0.0)
                uu[j, :, cols] = first + dx[j, :, cols] * carried
                carried = dt[j, :, cols] * carried + jnp.broadcast_to(state[7:8], (8, LANES))
            ebs[k : k + 1, :] = carried[0:1]

    for k in FAR_FIRST:
        later(k, lambda k: eb_copy(k).start())

    @pl.loop(0, F // LANES)
    def _(k):
        cols = columns(k)
        paths = lax.broadcasted_iota(jnp.int32, (PATHS, LANES), 0)
        cbs[pl.ds(k, 1), :] = jnp.sum(jnp.where(paths == x, s0v[:, cols], 0.0), axis=0, keepdims=True)
        for j in range(NX):
            u, v = uu[j, :, cols], vv[j, :, cols]
            for i in range(8):
                r = pl.ds(j * DAYS + i * 8, 8)
                decay = dd[r, cols]
                acc[r, cols] = acc[r, cols] + decay * u
                dd[r, cols] = decay * v

    span = float(BLOCK) * lpd[...]

    @pl.loop(0, z)
    def _(u):
        remote(lrs, lrr.at[u], lsend.at[0], lrecv.at[u], z=u).wait_recv()
        lrr[pl.ds(u, 1)] = jnp.exp(span + lrr[u])[None]

    def entered(u, carry):
        remote(ebs, ebr.at[u], bsend.at[0], brecv.at[u], z=u).wait_recv()
        return lrr[u] * carry + ebr[u]

    cbs[...] = lax.fori_loop(0, z, entered, cbs[...])

    for w in range(4):
        wide = pl.ds(w * 256, 256)
        now = jnp.concatenate([cbs[k : k + 1, :] for k in (2 * w, 2 * w + 1)], axis=1)
        scenario = (acc[:, wide] + dd[:, wide] * now).astype(bf16)
        term = jnp.dot(scenario, bm[wide, :], preferred_element_type=f32)
        res[...] = term if w == 0 else res[...] + term

    base = jnp.zeros((8, LANES), f32)
    exponent = []
    for j in range(NX):
        run = jnp.zeros((8, LANES), f32)
        sums = []
        for i in range(8):
            run = run + (0.03 + 0.3 * res[pl.ds(j * DAYS + i * 8, 8), pl.ds(K, LANES)])
            sums.append(run)
        total = run
        for shift in (1, 2, 4):
            total = total + jnp.where(sub >= shift, pltpu.roll(total, shift, 0), 0.0)
        start = base + jnp.where(sub >= 1, pltpu.roll(total, 1, 0), 0.0)
        base = base + jnp.broadcast_to(total[7:8], (8, LANES))
        exponent += [(-1.0 / 256.0) * (start + s) for s in sums]
    top = functools.reduce(jnp.maximum, exponent)
    top = jnp.max(top, axis=0, keepdims=True)
    worth = jnp.zeros((8, LANES), f32)
    for n, power in enumerate(exponent):
        worth = worth + jnp.exp(power - top) * res[pl.ds(n * 8, 8), pl.ds(0, K)]
    fs[0:1, :] = jnp.sum(worth, axis=0, keepdims=True)
    low = lax.broadcasted_iota(jnp.int32, (1, LANES), 1) < LANES // 2
    fs[1:2, :] = jnp.where(low, base[0:1], top)
    mine = z * NX + x
    fr[pl.ds(mine, 1)] = fs[...][None]

    pl.semaphore_wait(met.at[3], NX - 1)
    for k in (*FAR_FIRST, 0):
        for n in (2, 1, 3, 0):
            if k or n:
                remote(
                    fs, fr.at[mine], fsend.at[0], frecv.at[0], z=lax.rem(z + k, NZ), x=lax.rem(x + n, NX)
                ).start()

    for copy in (*straight, *onward, *r_copies, *e_copies):
        copy.wait_send()
    for k in FAR_FIRST:
        later(k, lambda k: lr_copy(k).wait_send())
        later(k, lambda k: eb_copy(k).wait_send())
    others = fr.at[pl.ds(0, NZ * NX - 1)]
    everyone = remote(others, others, fsend.at[0], frecv.at[0], z=lax.rem(z + 1, NZ))
    everyone.wait_recv()
    passed = jnp.zeros((NX, LANES), f32)
    value = jnp.zeros((NX, LANES), f32)
    for u in range(NZ):
        part, both = (
            jnp.concatenate([fr[u * NX + j, r : r + 1] for j in range(NX)], axis=0) for r in range(2)
        )
        swapped = pltpu.roll(both, LANES // 2, 1)
        value = value + jnp.exp(jnp.where(low, swapped, both) - (1.0 / 256.0) * passed) * part
        passed = passed + jnp.where(low, both, swapped)
    out[...] = value * (1.0 / 4096.0)
    everyone.wait_send()


def local(e, s0, m, lp, reg, pay, sc):
    vmem, dma = pltpu.VMEM, pltpu.SemaphoreType.DMA
    return pl.pallas_call(
        kernel,
        out_shape=jax.ShapeDtypeStruct((PATHS, K), f32),
        in_specs=[pl.BlockSpec(memory_space=pl.ANY)] * 8,
        out_specs=pl.BlockSpec(memory_space=pltpu.VMEM),
        scratch_shapes=[
            vmem((DAYS, PATHS, F), bf16),
            vmem((PATHS, DAYS, F), bf16),
            vmem((NX, DAYS, F), bf16),
            vmem((F, F), bf16),
            vmem((F, 2 * K), bf16),
            vmem((BLOCK, F), f32),
            vmem((BLOCK, F), f32),
            vmem((BLOCK, 2 * K), f32),
            vmem((NX, 8, LANES), f32),
            vmem((BLOCK, LANES), f32),
            vmem((1, F), f32),
            vmem((8, LANES), f32),
            vmem((PATHS, F), f32),
            vmem((1, DAYS), f32),
            vmem((8, LANES), bf16),
            vmem((3, NX, 8, F), f32),
            vmem((NX, 8, F), f32),
            vmem((NX, 8, F), f32),
            vmem((NX, 8, F), f32),
            vmem((NX, 8, F), f32),
            vmem((8, LANES), f32),
            vmem((NZ, 8, LANES), f32),
            vmem((8, LANES), f32),
            vmem((NZ, 8, LANES), f32),
            vmem((8, LANES), f32),
            vmem((2, LANES), f32),
            vmem((NZ * NX, 2, LANES), f32),
            dma((17,)),
            dma((12 * HALF + 1,)), dma((12 * HALF + 1,)),
            dma((NY, NX)), dma((NY, NX)),
            dma((NX,)), dma((NX,)),
            dma((NZ,)), dma((NZ,)),
            dma((NZ,)), dma((NZ,)),
            dma((1,)), dma((1,)),
            pltpu.SemaphoreType.REGULAR((5,)),
        ],
        compiler_params=pltpu.CompilerParams(collective_id=0, has_side_effects=True, vmem_limit_bytes=32 << 20),
        name="scenarios",
    )(
        *(
            pltpu.with_memory_space_constraint(a, pltpu.HBM)
            for a in (e, s0, m, lp.reshape(1, F), lp.reshape(8, LANES), reg.reshape(1, DAYS), pay, sc.reshape(8, LANES))
        )
    )


def solution(mesh):
    split = Mesh(mesh.devices.reshape(NY, NC, NZ, NX), ("y", "c", "z", "x"))
    paths, days = ("y", "c"), ("z", "x")
    placed = (P(days, paths, None), P(paths, None), P(paths, None), P(), P(days), P(), P())
    return jax.shard_map(local, mesh=split, in_specs=placed, out_specs=P(paths, None), check_vma=False)
```

```python
import functools

import jax
import jax.numpy as jnp
from jax import lax
from jax.experimental import pallas as pl
from jax.experimental.pallas import tpu as pltpu
from jax.sharding import Mesh
from jax.sharding import PartitionSpec as P

MESH_ID = pl.DeviceIdType.MESH
NY, NC, NZ, NX = 4, 2, 16, 4
DAYS, PATHS, F, K = 64, 4, 1024, 128
BLOCK = DAYS * NX
PIECE = 128
HALF = F // 2 // PIECE
LANES = 128
FAR_FIRST = (8, 7, 9, 6, 10, 5, 11, 4, 12, 3, 13, 2, 14, 1, 15)
f32, bf16 = jnp.float32, jnp.bfloat16


def columns(k):
    return pl.ds(pl.multiple_of(k * LANES, LANES), LANES)


def expm1(v):
    total = jnp.ones_like(v)
    for n in range(10, 1, -1):
        total = 1.0 + total * v * (1.0 / n)
    return v * total


def remote(src, dst, send, recv, **where):
    return pltpu.make_async_remote_copy(
        src_ref=src, dst_ref=dst, send_sem=send, recv_sem=recv, device_id=where, device_id_type=MESH_ID
    )


def kernel(
    e_in, s0_in, m_in, lp_in, lpd_in, reg_in, pay_in, sc_in, out,
    ev, es, er, mb, bm, acc, dd, res, rw, rb, lpv, lpd, s0v, regv, scv,
    dk, dx, dt, uu, vv, lrs, lrr, ebs, ebr, cbs, fs, fr,
    ld, msend, mrecv, esend, erecv, rsend, rrecv, lsend, lrecv, bsend, brecv, fsend, frecv, met,
):
    y, c, z, x = (lax.axis_index(a) for a in ("y", "c", "z", "x"))
    yp, ym, y2 = lax.rem(y + 1, NY), lax.rem(y + NY - 1, NY), lax.rem(y + 2, NY)
    mate = 1 - c

    barrier = pltpu.get_barrier_semaphore()
    beside = [{"x": lax.rem(x + k, NX)} for k in (1, NX - 1)]
    peers = [{"c": mate}, {"y": yp}, {"y": ym}, *beside]
    for peer in peers:
        pl.semaphore_signal(barrier, inc=1, device_id=peer, device_id_type=MESH_ID)

    def along_z(semaphore, distance):
        for k in (distance, NZ - distance):
            pl.semaphore_signal(semaphore, inc=1, device_id={"z": lax.rem(z + k, NZ)}, device_id_type=MESH_ID)

    along_z(barrier, 1)

    def shard(yy, cc, piece):
        return mb.at[
            pl.ds(pl.multiple_of((yy * 2 + cc) * 128, 128), 128), pl.ds(pl.multiple_of(piece * PIECE, PIECE), PIECE)
        ]

    turn = (y, ym, yp, y2)
    width = F // NY

    def quarter(yy):
        return pl.ds(pl.multiple_of(yy * width, width), width)

    shocks = [
        pltpu.make_async_copy(e_in.at[:, :, quarter(yy)], ev.at[:, :, quarter(yy)], ld.at[9 + n])
        for n, yy in enumerate(turn)
    ]
    loads = [
        pltpu.make_async_copy(reg_in, regv, ld.at[1]),
        pltpu.make_async_copy(lp_in, lpv, ld.at[2]),
        pltpu.make_async_copy(lpd_in, lpd, ld.at[3]),
        pltpu.make_async_copy(s0_in, s0v, ld.at[4]),
        pltpu.make_async_copy(sc_in, scv, ld.at[5]),
        pltpu.make_async_copy(pay_in, bm.at[:, pl.ds(0, K)], ld.at[6]),
        pltpu.make_async_copy(m_in, mb.at[pl.ds(pl.multiple_of((y * 2 + c) * 128, 128), 128), :], ld.at[7]),
    ]
    for copy in (*shocks, *loads):
        copy.start()

    pl.semaphore_wait(barrier, len(peers) + 2)
    along_z(met.at[0], 1)

    for peer in beside:
        pl.semaphore_signal(met.at[4], inc=1, device_id=peer, device_id_type=MESH_ID)

    def group(g, n):
        return g * HALF + n

    def m_copy(n, src, dst, **where):
        return remote(src, dst, msend.at[n], mrecv.at[n], **where)

    odd = lax.rem(z, 2)
    rising = [HALF * odd + n for n in range(HALF)]
    falling = [HALF * (1 - odd) + n for n in range(HALF)]

    def own(piece):
        return m_in.at[:, pl.ds(pl.multiple_of(piece * PIECE, PIECE), PIECE)]

    straight = []
    for n in range(HALF):
        straight.append(m_copy(group(0, n), own(rising[n]), shard(y, c, rising[n]), y=yp))
        straight.append(m_copy(group(1, n), own(falling[n]), shard(y, c, falling[n]), y=ym))
    straight.append(m_copy(group(12, 0), m_in, mb.at[pl.ds(pl.multiple_of((y * 2 + c) * 128, 128), 128), :], c=mate))
    for copy in straight:
        copy.start()

    loads[0].wait()
    rw[pl.ds(x, 1)] = jnp.ones((1, 8, LANES), f32)
    rw[pl.ds(x, 1), :, pl.ds(0, DAYS)] = jnp.broadcast_to(regv[...][None], (1, 8, DAYS))
    r_copies, e_copies = [], []

    row = lax.broadcasted_iota(jnp.int32, (256, 256), 0)
    col = lax.broadcasted_iota(jnp.int32, (256, 256), 1)
    source = (((row & 7) * 8 + ((row >> 3) & 7)) << 2) + (row >> 6)
    order = (col == source).astype(f32).astype(bf16)
    e_own = []
    for n, yy in enumerate(turn):
        cols = quarter(yy)
        shocks[n].wait()
        flat = ev[:, :, cols].reshape(DAYS * PATHS, width)
        moved = jnp.dot(order, flat, preferred_element_type=f32).astype(bf16)
        for p in range(PATHS):
            es[p, :, cols] = moved[p * DAYS : (p + 1) * DAYS]
        if n == 0:
            pl.semaphore_wait(met.at[0], 2)
            along_z(met.at[1], 2)
            pl.semaphore_wait(met.at[4], 2)
            for k in (2, 1, 3):
                xx = lax.rem(x + k, NX)
                r_copies.append(remote(rw.at[x], rw.at[x], rsend.at[k - 1], rrecv.at[x], x=xx))
                r_copies[-1].start()
        for k in (2, 1, 3):
            xx = lax.rem(x + k, NX)
            e_copies.append(
                remote(es.at[xx, :, cols], er.at[x, :, cols], esend.at[n, k - 1], erecv.at[n, x], x=xx)
            )
            e_copies[-1].start()
        e_own.append(pltpu.make_async_copy(es.at[x, :, cols], er.at[x, :, cols], ld.at[13 + n]))
        e_own[-1].start()

    pl.semaphore_wait(met.at[1], 2)
    along_z(met.at[2], 4)

    def shocks_here(n):
        cols = quarter(turn[n])
        e_own[n].wait()
        for k in range(1, NX):
            xx = lax.rem(x + k, NX)
            remote(
                es.at[xx, :, cols], er.at[xx, :, cols], esend.at[n, k - 1], erecv.at[n, xx], x=xx
            ).wait_recv()

    def hop(n, yy, piece):
        remote(shard(yy, c, piece), shard(yy, c, piece), msend.at[n], mrecv.at[n], y=yp).wait_recv()

    def passed_on(n, yy, piece, **where):
        onward.append(m_copy(n, shard(yy, c, piece), shard(yy, c, piece), **where))
        onward[-1].start()

    def relayed(n, yy, piece):
        remote(shard(yy, mate, piece), shard(yy, mate, piece), msend.at[n], mrecv.at[n], c=mate).wait_recv()

    onward = []
    aside = [{"z": lax.rem(z + 1, NZ)}, {"z": lax.rem(z + NZ - 1, NZ)}]
    for n in range(HALF):
        hop(group(0, n), ym, rising[n])
        passed_on(group(2, n), ym, rising[n], y=yp)
        passed_on(group(4, n), ym, rising[n], **aside[n % 2])
        hop(group(1, n), yp, falling[n])
        passed_on(group(3, n), yp, falling[n], y=ym)
        passed_on(group(5, n), yp, falling[n], **aside[n % 2])
    for n in range(HALF):
        passed_on(group(6, n), ym, rising[n], c=mate)
        passed_on(group(7, n), yp, falling[n], c=mate)

    for copy in loads[1:]:
        copy.wait()

    def r_wait(k):
        xx = lax.rem(x + k, NX)
        remote(rw.at[x], rw.at[xx], rsend.at[k - 1], rrecv.at[xx], x=xx).wait_recv()

    for k in range(1, NX):
        r_wait(k)
    rows = lax.broadcasted_iota(jnp.int32, (DAYS, LANES), 0)
    lanes = lax.broadcasted_iota(jnp.int32, (DAYS, LANES), 1)
    pick = lanes == (rows & 7) * 8 + (rows >> 3)
    logs = jnp.zeros((8, LANES), f32)
    for j in range(NX):
        logs = logs + jnp.log(rw[j])
        spread = jnp.where(pick, jnp.broadcast_to(rw[j, 0:1], (DAYS, LANES)), 0.0)
        rb[pl.ds(j * DAYS, DAYS), :] = jnp.broadcast_to(jnp.sum(spread, axis=1, keepdims=True), (DAYS, LANES))
    lrs[...] = jnp.broadcast_to(jnp.sum(logs, axis=1, keepdims=True), (8, LANES))

    def later(k, copy):
        @pl.when(z + k < NZ)
        def _():
            copy(k)

    def lr_copy(k):
        return remote(lrs, lrr.at[z], lsend.at[k], lrecv.at[z], z=lax.rem(z + k, NZ))

    def eb_copy(k):
        return remote(ebs, ebr.at[z], bsend.at[k], brecv.at[z], z=lax.rem(z + k, NZ))

    sub = lax.broadcasted_iota(jnp.int32, (8, LANES), 0)

    @pl.loop(0, F // LANES)
    def _(k):
        cols = columns(k)
        keep = jnp.broadcast_to(jnp.exp(lpv[:, cols]), (8, LANES))
        before = jnp.ones((8, LANES), f32)
        for j in range(NX):
            decay = None
            for i in range(8):
                r = pl.ds(j * DAYS + i * 8, 8)
                today = keep * rb[r, :]
                decay = today if i == 0 else decay * today
                dd[r, cols] = decay
            for n, shift in enumerate((1, 2, 4)):
                dk[n, j, :, cols] = jnp.where(sub >= shift, decay, 0.0)
                decay = jnp.where(sub >= shift, decay * pltpu.roll(decay, shift, 0), decay)
            first = jnp.where(sub >= 1, pltpu.roll(decay, 1, 0), 1.0)
            total = jnp.broadcast_to(decay[7:8], (8, LANES))
            dx[j, :, cols] = first
            dt[j, :, cols] = total
            vv[j, :, cols] = first * before
            before = before * total

    def shocks_of(yy):
        return jnp.concatenate([er[j, :, quarter(yy)] for j in range(NX)], axis=0)

    def block(half, w):
        return pl.ds(pl.multiple_of(half[2 * w] * PIECE, 256), 256)

    for n in range(HALF):
        hop(group(4, n), ym, falling[n])
        passed_on(group(8, n), ym, falling[n], c=mate)
        hop(group(5, n), yp, rising[n])
        passed_on(group(9, n), yp, rising[n], c=mate)
    for n in range(HALF):
        hop(group(2, n), y2, rising[n])
        passed_on(group(10, n), y2, rising[n], c=mate)
        hop(group(3, n), y2, falling[n])
        passed_on(group(11, n), y2, falling[n], c=mate)
    pl.semaphore_wait(met.at[2], 2)
    for k in range(1, NX):
        pl.semaphore_signal(met.at[3], inc=1, device_id={"x": lax.rem(x + k, NX)}, device_id_type=MESH_ID)
    for k in FAR_FIRST:
        later(k, lambda k: lr_copy(k).start())
    remote(m_in, mb.at[pl.ds(pl.multiple_of((y * 2 + mate) * 128, 128), 128), :], msend.at[group(12, 0)], mrecv.at[group(12, 0)], c=mate).wait_recv()
    shocks_here(0)
    left = shocks_of(y)
    for w in range(4):
        cols = pl.ds(w * 256, 256)
        acc[:, cols] = jnp.dot(left, mb[quarter(y), cols], preferred_element_type=f32)
    early = ((1, ym, rising, 6), (2, yp, falling, 7))
    for turned, yy, half, g in early:
        shocks_here(turned)
        for n in range(HALF):
            relayed(group(g, n), yy, half[n])
        left = shocks_of(yy)
        for w in range(2):
            cols = block(half, w)
            acc[:, cols] = acc[:, cols] + jnp.dot(left, mb[quarter(yy), cols], preferred_element_type=f32)
    shocks_here(3)
    for n in range(HALF):
        relayed(group(8, n), ym, falling[n])
        relayed(group(9, n), yp, rising[n])
        relayed(group(10, n), y2, rising[n])
        relayed(group(11, n), y2, falling[n])

    far = shocks_of(y2)
    for yy, half in ((ym, falling), (yp, rising)):
        near = shocks_of(yy)
        for w in range(2):
            cols = block(half, w)
            acc[:, cols] = (
                acc[:, cols]
                + jnp.dot(near, mb[quarter(yy), cols], preferred_element_type=f32)
                + jnp.dot(far, mb[quarter(y2), cols], preferred_element_type=f32)
            )
            for k in (half[2 * w], half[2 * w + 1]):
                cols = columns(k)
                log_keep = lpv[:, cols]
                keep = jnp.broadcast_to(jnp.exp(log_keep), (8, LANES))
                double = 2.0 * log_keep
                vol = jnp.broadcast_to(jnp.sqrt(-expm1(double)), (8, LANES))
                carried = jnp.zeros((8, LANES), f32)
                for j in range(NX):
                    state = None
                    for i in range(8):
                        r = pl.ds(j * DAYS + i * 8, 8)
                        shock = vol * acc[r, cols]
                        state = shock if i == 0 else (keep * rb[r, :]) * state + shock
                        acc[r, cols] = state
                    for n, shift in enumerate((1, 2, 4)):
                        state = state + dk[n, j, :, cols] * pltpu.roll(state, shift, 0)
                    first = jnp.where(sub >= 1, pltpu.roll(state, 1, 0), 0.0)
                    uu[j, :, cols] = first + dx[j, :, cols] * carried
                    carried = dt[j, :, cols] * carried + jnp.broadcast_to(state[7:8], (8, LANES))
                ebs[pl.ds(k, 1), :] = carried[0:1]

    for k in FAR_FIRST:
        later(k, lambda k: eb_copy(k).start())

    @pl.loop(0, F // LANES)
    def _(k):
        cols = columns(k)
        paths = lax.broadcasted_iota(jnp.int32, (PATHS, LANES), 0)
        cbs[pl.ds(k, 1), :] = jnp.sum(jnp.where(paths == x, s0v[:, cols], 0.0), axis=0, keepdims=True)
        for j in range(NX):
            u, v = uu[j, :, cols], vv[j, :, cols]
            for i in range(8):
                r = pl.ds(j * DAYS + i * 8, 8)
                decay = dd[r, cols]
                acc[r, cols] = acc[r, cols] + decay * u
                dd[r, cols] = decay * v

    short = scv[...].astype(f32)
    for k in range(F // LANES):
        block = jnp.broadcast_to(short[k : k + 1], (LANES, LANES))
        bm[pl.ds(k * LANES, LANES), pl.ds(K, LANES)] = block.T.astype(bf16)

    span = float(BLOCK) * lpd[...]

    @pl.loop(0, z)
    def _(u):
        remote(lrs, lrr.at[u], lsend.at[0], lrecv.at[u], z=u).wait_recv()
        lrr[pl.ds(u, 1)] = jnp.exp(span + lrr[u])[None]

    def entered(u, carry):
        remote(ebs, ebr.at[u], bsend.at[0], brecv.at[u], z=u).wait_recv()
        return lrr[u] * carry + ebr[u]

    cbs[...] = lax.fori_loop(0, z, entered, cbs[...])

    for w in range(4):
        wide = pl.ds(w * 256, 256)
        now = jnp.concatenate([cbs[k : k + 1, :] for k in (2 * w, 2 * w + 1)], axis=1)
        scenario = (acc[:, wide] + dd[:, wide] * now).astype(bf16)
        term = jnp.dot(scenario, bm[wide, :], preferred_element_type=f32)
        res[...] = term if w == 0 else res[...] + term

    base = jnp.zeros((8, LANES), f32)
    exponent = []
    for j in range(NX):
        run = jnp.zeros((8, LANES), f32)
        sums = []
        for i in range(8):
            run = run + (0.03 + 0.3 * res[pl.ds(j * DAYS + i * 8, 8), pl.ds(K, LANES)])
            sums.append(run)
        total = run
        for shift in (1, 2, 4):
            total = total + jnp.where(sub >= shift, pltpu.roll(total, shift, 0), 0.0)
        start = base + jnp.where(sub >= 1, pltpu.roll(total, 1, 0), 0.0)
        base = base + jnp.broadcast_to(total[7:8], (8, LANES))
        exponent += [(-1.0 / 256.0) * (start + s) for s in sums]
    top = functools.reduce(jnp.maximum, exponent)
    top = jnp.max(top, axis=0, keepdims=True)
    worth = jnp.zeros((8, LANES), f32)
    for n, power in enumerate(exponent):
        worth = worth + jnp.exp(power - top) * res[pl.ds(n * 8, 8), pl.ds(0, K)]
    fs[0:1, :] = jnp.sum(worth, axis=0, keepdims=True)
    low = lax.broadcasted_iota(jnp.int32, (1, LANES), 1) < LANES // 2
    fs[1:2, :] = jnp.where(low, base[0:1], top)
    mine = z * NX + x
    fr[pl.ds(mine, 1)] = fs[...][None]

    pl.semaphore_wait(met.at[3], NX - 1)
    for k in (*FAR_FIRST, 0):
        for n in (2, 1, 3, 0):
            if k or n:
                remote(
                    fs, fr.at[mine], fsend.at[0], frecv.at[0], z=lax.rem(z + k, NZ), x=lax.rem(x + n, NX)
                ).start()

    for copy in (*straight, *onward, *r_copies, *e_copies):
        copy.wait_send()
    for k in FAR_FIRST:
        later(k, lambda k: lr_copy(k).wait_send())
        later(k, lambda k: eb_copy(k).wait_send())
    others = fr.at[pl.ds(0, NZ * NX - 1)]
    everyone = remote(others, others, fsend.at[0], frecv.at[0], z=lax.rem(z + 1, NZ))
    everyone.wait_recv()
    passed = jnp.zeros((NX, LANES), f32)
    value = jnp.zeros((NX, LANES), f32)
    for u in range(NZ):
        part, both = (
            jnp.concatenate([fr[u * NX + j, r : r + 1] for j in range(NX)], axis=0) for r in range(2)
        )
        swapped = pltpu.roll(both, LANES // 2, 1)
        value = value + jnp.exp(jnp.where(low, swapped, both) - (1.0 / 256.0) * passed) * part
        passed = passed + jnp.where(low, both, swapped)
    out[...] = value * (1.0 / 4096.0)
    everyone.wait_send()


def local(e, s0, m, lp, reg, pay, sc):
    vmem, dma = pltpu.VMEM, pltpu.SemaphoreType.DMA
    return pl.pallas_call(
        kernel,
        out_shape=jax.ShapeDtypeStruct((PATHS, K), f32),
        in_specs=[pl.BlockSpec(memory_space=pl.ANY)] * 8,
        out_specs=pl.BlockSpec(memory_space=pltpu.VMEM),
        scratch_shapes=[
            vmem((DAYS, PATHS, F), bf16),
            vmem((PATHS, DAYS, F), bf16),
            vmem((NX, DAYS, F), bf16),
            vmem((F, F), bf16),
            vmem((F, 2 * K), bf16),
            vmem((BLOCK, F), f32),
            vmem((BLOCK, F), f32),
            vmem((BLOCK, 2 * K), f32),
            vmem((NX, 8, LANES), f32),
            vmem((BLOCK, LANES), f32),
            vmem((1, F), f32),
            vmem((8, LANES), f32),
            vmem((PATHS, F), f32),
            vmem((1, DAYS), f32),
            vmem((8, LANES), bf16),
            vmem((3, NX, 8, F), f32),
            vmem((NX, 8, F), f32),
            vmem((NX, 8, F), f32),
            vmem((NX, 8, F), f32),
            vmem((NX, 8, F), f32),
            vmem((8, LANES), f32),
            vmem((NZ, 8, LANES), f32),
            vmem((8, LANES), f32),
            vmem((NZ, 8, LANES), f32),
            vmem((8, LANES), f32),
            vmem((2, LANES), f32),
            vmem((NZ * NX, 2, LANES), f32),
            dma((17,)),
            dma((12 * HALF + 1,)), dma((12 * HALF + 1,)),
            dma((NY, NX)), dma((NY, NX)),
            dma((NX,)), dma((NX,)),
            dma((NZ,)), dma((NZ,)),
            dma((NZ,)), dma((NZ,)),
            dma((1,)), dma((1,)),
            pltpu.SemaphoreType.REGULAR((5,)),
        ],
        compiler_params=pltpu.CompilerParams(collective_id=0, has_side_effects=True, vmem_limit_bytes=32 << 20),
        name="scenarios",
    )(
        *(
            pltpu.with_memory_space_constraint(a, pltpu.HBM)
            for a in (e, s0, m, lp.reshape(1, F), lp.reshape(8, LANES), reg.reshape(1, DAYS), pay, sc.reshape(8, LANES))
        )
    )


def solution(mesh):
    split = Mesh(mesh.devices.reshape(NY, NC, NZ, NX), ("y", "c", "z", "x"))
    paths, days = ("y", "c"), ("z", "x")
    placed = (P(days, paths, None), P(paths, None), P(paths, None), P(), P(days), P(), P())
    return jax.shard_map(local, mesh=split, in_specs=placed, out_specs=P(paths, None), check_vma=False)
```

```python
import functools

import jax
import jax.numpy as jnp
from jax import lax
from jax.experimental import pallas as pl
from jax.experimental.pallas import tpu as pltpu
from jax.sharding import Mesh
from jax.sharding import PartitionSpec as P

MESH_ID = pl.DeviceIdType.MESH
NY, NC, NZ, NX = 4, 2, 16, 4
DAYS, PATHS, F, K = 64, 4, 1024, 128
BLOCK = DAYS * NX
PIECE = 16
HALF = 64 // PIECE
LANES = 128
FAR_FIRST = (8, 7, 9, 6, 10, 5, 11, 4, 12, 3, 13, 2, 14, 1, 15)
f32, bf16 = jnp.float32, jnp.bfloat16


def columns(k):
    return pl.ds(pl.multiple_of(k * LANES, LANES), LANES)


def expm1(v):
    total = jnp.ones_like(v)
    for n in range(10, 1, -1):
        total = 1.0 + total * v * (1.0 / n)
    return v * total


def remote(src, dst, send, recv, **where):
    return pltpu.make_async_remote_copy(
        src_ref=src, dst_ref=dst, send_sem=send, recv_sem=recv, device_id=where, device_id_type=MESH_ID
    )


def kernel(
    e_in, s0_in, m_in, lp_in, lpd_in, reg_in, pay_in, sc_in, out,
    ev, es, er, mb, bm, acc, dd, res, rw, rb, lpv, lpd, s0v, regv, scv,
    dk, dx, dt, uu, vv, lrs, lrr, ebs, ebr, cbs, fs, fr,
    ld, msend, mrecv, esend, erecv, rsend, rrecv, lsend, lrecv, bsend, brecv, fsend, frecv, met,
):
    y, c, z, x = (lax.axis_index(a) for a in ("y", "c", "z", "x"))
    yp, ym, y2 = lax.rem(y + 1, NY), lax.rem(y + NY - 1, NY), lax.rem(y + 2, NY)
    mate = 1 - c

    barrier = pltpu.get_barrier_semaphore()
    beside = [{"x": lax.rem(x + k, NX)} for k in (1, NX - 1)]
    peers = [{"c": mate}, {"y": yp}, {"y": ym}, *beside]
    for peer in peers:
        pl.semaphore_signal(barrier, inc=1, device_id=peer, device_id_type=MESH_ID)

    def along_z(semaphore, distance):
        for k in (distance, NZ - distance):
            pl.semaphore_signal(semaphore, inc=1, device_id={"z": lax.rem(z + k, NZ)}, device_id_type=MESH_ID)

    along_z(barrier, 1)

    def shard(yy, cc, piece):
        return mb.at[pl.ds(pl.multiple_of((yy * 2 + cc) * 128 + piece * PIECE, PIECE), PIECE), :]

    turn = (y, ym, yp, y2)
    width = F // NY

    def quarter(yy):
        return pl.ds(pl.multiple_of(yy * width, width), width)

    shocks = [
        pltpu.make_async_copy(e_in.at[:, :, quarter(yy)], ev.at[:, :, quarter(yy)], ld.at[9 + n])
        for n, yy in enumerate(turn)
    ]
    loads = [
        pltpu.make_async_copy(reg_in, regv, ld.at[1]),
        pltpu.make_async_copy(lp_in, lpv, ld.at[2]),
        pltpu.make_async_copy(lpd_in, lpd, ld.at[3]),
        pltpu.make_async_copy(s0_in, s0v, ld.at[4]),
        pltpu.make_async_copy(sc_in, scv, ld.at[5]),
        pltpu.make_async_copy(pay_in, bm.at[:, pl.ds(0, K)], ld.at[6]),
        pltpu.make_async_copy(m_in, mb.at[pl.ds(pl.multiple_of((y * 2 + c) * 128, 128), 128), :], ld.at[7]),
    ]
    for copy in (*shocks, *loads):
        copy.start()

    pl.semaphore_wait(barrier, len(peers) + 2)
    along_z(met.at[0], 1)

    for peer in beside:
        pl.semaphore_signal(met.at[4], inc=1, device_id=peer, device_id_type=MESH_ID)

    def group(g, n):
        return g * HALF + n

    def m_copy(n, src, dst, **where):
        return remote(src, dst, msend.at[n], mrecv.at[n], **where)

    odd = lax.rem(z, 2)
    rising = [HALF * odd + n for n in range(HALF)]
    falling = [HALF * (1 - odd) + n for n in range(HALF)]

    def own(piece):
        return m_in.at[pl.ds(pl.multiple_of(piece * PIECE, PIECE), PIECE), :]

    straight = []
    for n in range(HALF):
        straight.append(m_copy(group(0, n), own(rising[n]), shard(y, c, rising[n]), y=yp))
        straight.append(m_copy(group(1, n), own(falling[n]), shard(y, c, falling[n]), y=ym))
    straight.append(m_copy(group(12, 0), m_in, mb.at[pl.ds(pl.multiple_of((y * 2 + c) * 128, 128), 128), :], c=mate))
    for copy in straight:
        copy.start()

    loads[0].wait()
    rw[pl.ds(x, 1)] = jnp.ones((1, 8, LANES), f32)
    rw[pl.ds(x, 1), :, pl.ds(0, DAYS)] = jnp.broadcast_to(regv[...][None], (1, 8, DAYS))
    r_copies, e_copies = [], []

    row = lax.broadcasted_iota(jnp.int32, (256, 256), 0)
    col = lax.broadcasted_iota(jnp.int32, (256, 256), 1)
    source = (((row & 7) * 8 + ((row >> 3) & 7)) << 2) + (row >> 6)
    order = (col == source).astype(f32).astype(bf16)
    e_own = []
    for n, yy in enumerate(turn):
        cols = quarter(yy)
        shocks[n].wait()
        flat = ev[:, :, cols].reshape(DAYS * PATHS, width)
        moved = jnp.dot(order, flat, preferred_element_type=f32).astype(bf16)
        for p in range(PATHS):
            es[p, :, cols] = moved[p * DAYS : (p + 1) * DAYS]
        if n == 0:
            pl.semaphore_wait(met.at[0], 2)
            along_z(met.at[1], 2)
            pl.semaphore_wait(met.at[4], 2)
            for k in (2, 1, 3):
                xx = lax.rem(x + k, NX)
                r_copies.append(remote(rw.at[x], rw.at[x], rsend.at[k - 1], rrecv.at[x], x=xx))
                r_copies[-1].start()
        for k in (2, 1, 3):
            xx = lax.rem(x + k, NX)
            e_copies.append(
                remote(es.at[xx, :, cols], er.at[x, :, cols], esend.at[n, k - 1], erecv.at[n, x], x=xx)
            )
            e_copies[-1].start()
        e_own.append(pltpu.make_async_copy(es.at[x, :, cols], er.at[x, :, cols], ld.at[13 + n]))
        e_own[-1].start()

    pl.semaphore_wait(met.at[1], 2)
    along_z(met.at[2], 4)

    def shocks_here(n):
        cols = quarter(turn[n])
        e_own[n].wait()
        for k in range(1, NX):
            xx = lax.rem(x + k, NX)
            remote(
                es.at[xx, :, cols], er.at[xx, :, cols], esend.at[n, k - 1], erecv.at[n, xx], x=xx
            ).wait_recv()

    def hop(n, yy, piece):
        remote(shard(yy, c, piece), shard(yy, c, piece), msend.at[n], mrecv.at[n], y=yp).wait_recv()

    def passed_on(n, yy, piece, **where):
        onward.append(m_copy(n, shard(yy, c, piece), shard(yy, c, piece), **where))
        onward[-1].start()

    def relayed(n, yy, piece):
        remote(shard(yy, mate, piece), shard(yy, mate, piece), msend.at[n], mrecv.at[n], c=mate).wait_recv()

    onward = []
    aside = [{"z": lax.rem(z + 1, NZ)}, {"z": lax.rem(z + NZ - 1, NZ)}]
    for n in range(HALF):
        hop(group(0, n), ym, rising[n])
        passed_on(group(2, n), ym, rising[n], y=yp)
        passed_on(group(4, n), ym, rising[n], **aside[n % 2])
        passed_on(group(6, n), ym, rising[n], c=mate)
        hop(group(1, n), yp, falling[n])
        passed_on(group(3, n), yp, falling[n], y=ym)
        passed_on(group(5, n), yp, falling[n], **aside[n % 2])
        passed_on(group(7, n), yp, falling[n], c=mate)

    for copy in loads[1:]:
        copy.wait()

    def r_wait(k):
        xx = lax.rem(x + k, NX)
        remote(rw.at[x], rw.at[xx], rsend.at[k - 1], rrecv.at[xx], x=xx).wait_recv()

    for k in range(1, NX):
        r_wait(k)
    rows = lax.broadcasted_iota(jnp.int32, (DAYS, LANES), 0)
    lanes = lax.broadcasted_iota(jnp.int32, (DAYS, LANES), 1)
    pick = lanes == (rows & 7) * 8 + (rows >> 3)
    logs = jnp.zeros((8, LANES), f32)
    for j in range(NX):
        logs = logs + jnp.log(rw[j])
        spread = jnp.where(pick, jnp.broadcast_to(rw[j, 0:1], (DAYS, LANES)), 0.0)
        rb[pl.ds(j * DAYS, DAYS), :] = jnp.broadcast_to(jnp.sum(spread, axis=1, keepdims=True), (DAYS, LANES))
    lrs[...] = jnp.broadcast_to(jnp.sum(logs, axis=1, keepdims=True), (8, LANES))

    def later(k, copy):
        @pl.when(z + k < NZ)
        def _():
            copy(k)

    def lr_copy(k):
        return remote(lrs, lrr.at[z], lsend.at[k], lrecv.at[z], z=lax.rem(z + k, NZ))

    def eb_copy(k):
        return remote(ebs, ebr.at[z], bsend.at[k], brecv.at[z], z=lax.rem(z + k, NZ))

    sub = lax.broadcasted_iota(jnp.int32, (8, LANES), 0)

    @pl.loop(0, F // LANES)
    def _(k):
        cols = columns(k)
        keep = jnp.broadcast_to(jnp.exp(lpv[:, cols]), (8, LANES))
        before = jnp.ones((8, LANES), f32)
        for j in range(NX):
            decay = None
            for i in range(8):
                r = pl.ds(j * DAYS + i * 8, 8)
                today = keep * rb[r, :]
                decay = today if i == 0 else decay * today
                dd[r, cols] = decay
            for n, shift in enumerate((1, 2, 4)):
                dk[n, j, :, cols] = jnp.where(sub >= shift, decay, 0.0)
                decay = jnp.where(sub >= shift, decay * pltpu.roll(decay, shift, 0), decay)
            first = jnp.where(sub >= 1, pltpu.roll(decay, 1, 0), 1.0)
            total = jnp.broadcast_to(decay[7:8], (8, LANES))
            dx[j, :, cols] = first
            dt[j, :, cols] = total
            vv[j, :, cols] = first * before
            before = before * total

    def product(row, depth, first=False):
        at = pl.ds(pl.multiple_of(row, depth), depth)
        left = jnp.concatenate([er[j, :, at] for j in range(NX)], axis=0)
        for k in range(4):
            cols = pl.ds(k * 256, 256)
            term = jnp.dot(left, mb[at, cols], preferred_element_type=f32)
            acc[:, cols] = term if first else acc[:, cols] + term

    for n in range(HALF):
        hop(group(4, n), ym, falling[n])
        passed_on(group(8, n), ym, falling[n], c=mate)
        hop(group(5, n), yp, rising[n])
        passed_on(group(9, n), yp, rising[n], c=mate)
    for n in range(HALF):
        hop(group(2, n), y2, rising[n])
        passed_on(group(10, n), y2, rising[n], c=mate)
        hop(group(3, n), y2, falling[n])
        passed_on(group(11, n), y2, falling[n], c=mate)
    pl.semaphore_wait(met.at[2], 2)
    for k in range(1, NX):
        pl.semaphore_signal(met.at[3], inc=1, device_id={"x": lax.rem(x + k, NX)}, device_id_type=MESH_ID)
    for k in FAR_FIRST:
        later(k, lambda k: lr_copy(k).start())
    remote(m_in, mb.at[pl.ds(pl.multiple_of((y * 2 + mate) * 128, 128), 128), :], msend.at[group(12, 0)], mrecv.at[group(12, 0)], c=mate).wait_recv()
    shocks_here(0)
    product(y * 256, 256, True)
    for n in range(HALF):
        relayed(group(6, n), ym, rising[n])
        relayed(group(8, n), ym, falling[n])
    shocks_here(1)
    product(ym * 256, 256)
    for n in range(HALF):
        relayed(group(7, n), yp, falling[n])
        relayed(group(9, n), yp, rising[n])
    shocks_here(2)
    product(yp * 256, 256)
    shocks_here(3)
    for n in range(HALF):
        relayed(group(10, n), y2, rising[n])
        relayed(group(11, n), y2, falling[n])

    last = quarter(y2)
    left = jnp.concatenate([er[j, :, last] for j in range(NX)], axis=0)
    for w in range(4):
        wide = pl.ds(w * 256, 256)
        acc[:, wide] = acc[:, wide] + jnp.dot(left, mb[last, wide], preferred_element_type=f32)
        for k in (2 * w, 2 * w + 1):
            cols = pl.ds(k * LANES, LANES)
            log_keep = lpv[:, cols]
            keep = jnp.broadcast_to(jnp.exp(log_keep), (8, LANES))
            double = 2.0 * log_keep
            vol = jnp.broadcast_to(jnp.sqrt(-expm1(double)), (8, LANES))
            carried = jnp.zeros((8, LANES), f32)
            for j in range(NX):
                state = None
                for i in range(8):
                    r = pl.ds(j * DAYS + i * 8, 8)
                    shock = vol * acc[r, cols]
                    state = shock if i == 0 else (keep * rb[r, :]) * state + shock
                    acc[r, cols] = state
                for n, shift in enumerate((1, 2, 4)):
                    state = state + dk[n, j, :, cols] * pltpu.roll(state, shift, 0)
                first = jnp.where(sub >= 1, pltpu.roll(state, 1, 0), 0.0)
                uu[j, :, cols] = first + dx[j, :, cols] * carried
                carried = dt[j, :, cols] * carried + jnp.broadcast_to(state[7:8], (8, LANES))
            ebs[k : k + 1, :] = carried[0:1]

    for k in FAR_FIRST:
        later(k, lambda k: eb_copy(k).start())

    @pl.loop(0, F // LANES)
    def _(k):
        cols = columns(k)
        paths = lax.broadcasted_iota(jnp.int32, (PATHS, LANES), 0)
        cbs[pl.ds(k, 1), :] = jnp.sum(jnp.where(paths == x, s0v[:, cols], 0.0), axis=0, keepdims=True)
        for j in range(NX):
            u, v = uu[j, :, cols], vv[j, :, cols]
            for i in range(8):
                r = pl.ds(j * DAYS + i * 8, 8)
                decay = dd[r, cols]
                acc[r, cols] = acc[r, cols] + decay * u
                dd[r, cols] = decay * v

    short = scv[...].astype(f32)
    for k in range(F // LANES):
        block = jnp.broadcast_to(short[k : k + 1], (LANES, LANES))
        bm[pl.ds(k * LANES, LANES), pl.ds(K, LANES)] = block.T.astype(bf16)

    span = float(BLOCK) * lpd[...]

    @pl.loop(0, z)
    def _(u):
        remote(lrs, lrr.at[u], lsend.at[0], lrecv.at[u], z=u).wait_recv()
        lrr[pl.ds(u, 1)] = jnp.exp(span + lrr[u])[None]

    def entered(u, carry):
        remote(ebs, ebr.at[u], bsend.at[0], brecv.at[u], z=u).wait_recv()
        return lrr[u] * carry + ebr[u]

    cbs[...] = lax.fori_loop(0, z, entered, cbs[...])

    for w in range(4):
        wide = pl.ds(w * 256, 256)
        now = jnp.concatenate([cbs[k : k + 1, :] for k in (2 * w, 2 * w + 1)], axis=1)
        scenario = (acc[:, wide] + dd[:, wide] * now).astype(bf16)
        term = jnp.dot(scenario, bm[wide, :], preferred_element_type=f32)
        res[...] = term if w == 0 else res[...] + term

    base = jnp.zeros((8, LANES), f32)
    exponent = []
    for j in range(NX):
        run = jnp.zeros((8, LANES), f32)
        sums = []
        for i in range(8):
            run = run + (0.03 + 0.3 * res[pl.ds(j * DAYS + i * 8, 8), pl.ds(K, LANES)])
            sums.append(run)
        total = run
        for shift in (1, 2, 4):
            total = total + jnp.where(sub >= shift, pltpu.roll(total, shift, 0), 0.0)
        start = base + jnp.where(sub >= 1, pltpu.roll(total, 1, 0), 0.0)
        base = base + jnp.broadcast_to(total[7:8], (8, LANES))
        exponent += [(-1.0 / 256.0) * (start + s) for s in sums]
    top = functools.reduce(jnp.maximum, exponent)
    top = jnp.max(top, axis=0, keepdims=True)
    worth = jnp.zeros((8, LANES), f32)
    for n, power in enumerate(exponent):
        worth = worth + jnp.exp(power - top) * res[pl.ds(n * 8, 8), pl.ds(0, K)]
    fs[0:1, :] = jnp.sum(worth, axis=0, keepdims=True)
    low = lax.broadcasted_iota(jnp.int32, (1, LANES), 1) < LANES // 2
    fs[1:2, :] = jnp.where(low, base[0:1], top)
    mine = z * NX + x
    fr[pl.ds(mine, 1)] = fs[...][None]

    pl.semaphore_wait(met.at[3], NX - 1)
    def sums_to(zz, n):
        return remote(fs, fr.at[mine], fsend.at[0], frecv.at[0], z=zz, x=lax.rem(x + n, NX))

    for zz in range(NZ):
        for n in (2, 1, 3):
            sums_to(zz, n).start()

        @pl.when(zz != z)
        def _():
            sums_to(zz, 0).start()

    for copy in (*straight, *onward, *r_copies, *e_copies):
        copy.wait_send()
    for k in FAR_FIRST:
        later(k, lambda k: lr_copy(k).wait_send())
        later(k, lambda k: eb_copy(k).wait_send())
    others = fr.at[pl.ds(0, NZ * NX - 1)]
    everyone = remote(others, others, fsend.at[0], frecv.at[0], z=lax.rem(z + 1, NZ))
    everyone.wait_recv()
    passed = jnp.zeros((NX, LANES), f32)
    value = jnp.zeros((NX, LANES), f32)
    for u in range(NZ):
        part, both = (
            jnp.concatenate([fr[u * NX + j, r : r + 1] for j in range(NX)], axis=0) for r in range(2)
        )
        swapped = pltpu.roll(both, LANES // 2, 1)
        value = value + jnp.exp(jnp.where(low, swapped, both) - (1.0 / 256.0) * passed) * part
        passed = passed + jnp.where(low, both, swapped)
    out[...] = value * (1.0 / 4096.0)
    everyone.wait_send()


def local(e, s0, m, lp, reg, pay, sc):
    vmem, dma = pltpu.VMEM, pltpu.SemaphoreType.DMA
    return pl.pallas_call(
        kernel,
        out_shape=jax.ShapeDtypeStruct((PATHS, K), f32),
        in_specs=[pl.BlockSpec(memory_space=pl.ANY)] * 8,
        out_specs=pl.BlockSpec(memory_space=pltpu.VMEM),
        scratch_shapes=[
            vmem((DAYS, PATHS, F), bf16),
            vmem((PATHS, DAYS, F), bf16),
            vmem((NX, DAYS, F), bf16),
            vmem((F, F), bf16),
            vmem((F, 2 * K), bf16),
            vmem((BLOCK, F), f32),
            vmem((BLOCK, F), f32),
            vmem((BLOCK, 2 * K), f32),
            vmem((NX, 8, LANES), f32),
            vmem((BLOCK, LANES), f32),
            vmem((1, F), f32),
            vmem((8, LANES), f32),
            vmem((PATHS, F), f32),
            vmem((1, DAYS), f32),
            vmem((8, LANES), bf16),
            vmem((3, NX, 8, F), f32),
            vmem((NX, 8, F), f32),
            vmem((NX, 8, F), f32),
            vmem((NX, 8, F), f32),
            vmem((NX, 8, F), f32),
            vmem((8, LANES), f32),
            vmem((NZ, 8, LANES), f32),
            vmem((8, LANES), f32),
            vmem((NZ, 8, LANES), f32),
            vmem((8, LANES), f32),
            vmem((2, LANES), f32),
            vmem((NZ * NX, 2, LANES), f32),
            dma((17,)),
            dma((12 * HALF + 1,)), dma((12 * HALF + 1,)),
            dma((NY, NX)), dma((NY, NX)),
            dma((NX,)), dma((NX,)),
            dma((NZ,)), dma((NZ,)),
            dma((NZ,)), dma((NZ,)),
            dma((1,)), dma((1,)),
            pltpu.SemaphoreType.REGULAR((5,)),
        ],
        compiler_params=pltpu.CompilerParams(collective_id=0, has_side_effects=True, vmem_limit_bytes=32 << 20),
        name="scenarios",
    )(
        *(
            pltpu.with_memory_space_constraint(a, pltpu.HBM)
            for a in (e, s0, m, lp.reshape(1, F), lp.reshape(8, LANES), reg.reshape(1, DAYS), pay, sc.reshape(8, LANES))
        )
    )


def solution(mesh):
    split = Mesh(mesh.devices.reshape(NY, NC, NZ, NX), ("y", "c", "z", "x"))
    paths, days = ("y", "c"), ("z", "x")
    placed = (P(days, paths, None), P(paths, None), P(paths, None), P(), P(days), P(), P())
    return jax.shard_map(local, mesh=split, in_specs=placed, out_specs=P(paths, None), check_vma=False)
```

```python
import functools

import jax
import jax.numpy as jnp
from jax import lax
from jax.experimental import pallas as pl
from jax.experimental.pallas import tpu as pltpu
from jax.sharding import Mesh
from jax.sharding import PartitionSpec as P

MESH_ID = pl.DeviceIdType.MESH
NY, NC, NZ, NX = 4, 2, 16, 4
DAYS, PATHS, F, K = 64, 4, 1024, 128
BLOCK = DAYS * NX
PIECE = 16
HALF = 64 // PIECE
LANES = 128
FAR_FIRST = (8, 7, 9, 6, 10, 5, 11, 4, 12, 3, 13, 2, 14, 1, 15)
f32, bf16 = jnp.float32, jnp.bfloat16


def columns(k):
    return pl.ds(pl.multiple_of(k * LANES, LANES), LANES)


def expm1(v):
    total = jnp.ones_like(v)
    for n in range(10, 1, -1):
        total = 1.0 + total * v * (1.0 / n)
    return v * total


def remote(src, dst, send, recv, **where):
    return pltpu.make_async_remote_copy(
        src_ref=src, dst_ref=dst, send_sem=send, recv_sem=recv, device_id=where, device_id_type=MESH_ID
    )


def kernel(
    e_in, s0_in, m_in, lp_in, lpd_in, reg_in, pay_in, sc_in, out,
    ev, es, er, mb, bm, acc, dd, res, rw, rb, lpv, lpd, s0v, regv, scv,
    dk, dx, dt, uu, vv, lrs, lrr, ebs, ebr, cbs, fs, fr,
    ld, msend, mrecv, esend, erecv, rsend, rrecv, lsend, lrecv, bsend, brecv, fsend, frecv, met,
):
    y, c, z, x = (lax.axis_index(a) for a in ("y", "c", "z", "x"))
    yp, ym, y2 = lax.rem(y + 1, NY), lax.rem(y + NY - 1, NY), lax.rem(y + 2, NY)
    mate = 1 - c

    barrier = pltpu.get_barrier_semaphore()
    beside = [{"x": lax.rem(x + k, NX)} for k in (1, NX - 1)]
    peers = [{"c": mate}, {"y": yp}, {"y": ym}, *beside]
    for peer in peers:
        pl.semaphore_signal(barrier, inc=1, device_id=peer, device_id_type=MESH_ID)

    def along_z(semaphore, distance):
        for k in (distance, NZ - distance):
            pl.semaphore_signal(semaphore, inc=1, device_id={"z": lax.rem(z + k, NZ)}, device_id_type=MESH_ID)

    along_z(barrier, 1)

    def shard(yy, cc, piece):
        return mb.at[pl.ds(pl.multiple_of((yy * 2 + cc) * 128 + piece * PIECE, PIECE), PIECE), :]

    turn = (y, ym, yp, y2)
    width = F // NY

    def quarter(yy):
        return pl.ds(pl.multiple_of(yy * width, width), width)

    own_rows = mb.at[pl.ds(pl.multiple_of((y * 2 + c) * 128, 128), 128), :]
    mixer = pltpu.make_async_copy(m_in, own_rows, ld.at[7])
    shocks = [
        pltpu.make_async_copy(e_in.at[:, :, quarter(yy)], ev.at[:, :, quarter(yy)], ld.at[9 + n])
        for n, yy in enumerate(turn)
    ]
    loads = [
        pltpu.make_async_copy(reg_in, regv, ld.at[1]),
        pltpu.make_async_copy(lp_in, lpv, ld.at[2]),
        pltpu.make_async_copy(lpd_in, lpd, ld.at[3]),
        pltpu.make_async_copy(s0_in, s0v, ld.at[4]),
        pltpu.make_async_copy(sc_in, scv, ld.at[5]),
        pltpu.make_async_copy(pay_in, bm.at[:, pl.ds(0, K)], ld.at[6]),
    ]
    for copy in (mixer, *shocks, *loads):
        copy.start()

    pl.semaphore_wait(barrier, len(peers) + 2)
    def group(g, n):
        return g * HALF + n

    def m_copy(n, src, dst, **where):
        return remote(src, dst, msend.at[n], mrecv.at[n], **where)

    odd = lax.rem(z, 2)
    rising = [HALF * odd + n for n in range(HALF)]
    falling = [HALF * (1 - odd) + n for n in range(HALF)]

    straight = []
    for n in range(HALF):
        straight.append(m_copy(group(0, n), shard(y, c, rising[n]), shard(y, c, rising[n]), y=yp))
        straight.append(m_copy(group(1, n), shard(y, c, falling[n]), shard(y, c, falling[n]), y=ym))
    straight.append(m_copy(group(12, 0), own_rows, own_rows, c=mate))
    mixer.wait()
    for copy in straight:
        copy.start()
    along_z(met.at[0], 1)

    for peer in beside:
        pl.semaphore_signal(met.at[4], inc=1, device_id=peer, device_id_type=MESH_ID)

    loads[0].wait()
    rw[pl.ds(x, 1)] = jnp.ones((1, 8, LANES), f32)
    rw[pl.ds(x, 1), :, pl.ds(0, DAYS)] = jnp.broadcast_to(regv[...][None], (1, 8, DAYS))
    r_copies, e_copies = [], []

    row = lax.broadcasted_iota(jnp.int32, (256, 256), 0)
    col = lax.broadcasted_iota(jnp.int32, (256, 256), 1)
    source = (((row & 7) * 8 + ((row >> 3) & 7)) << 2) + (row >> 6)
    order = (col == source).astype(f32).astype(bf16)
    e_own = []
    for n, yy in enumerate(turn):
        cols = quarter(yy)
        shocks[n].wait()
        flat = ev[:, :, cols].reshape(DAYS * PATHS, width)
        moved = jnp.dot(order, flat, preferred_element_type=f32).astype(bf16)
        for p in range(PATHS):
            es[p, :, cols] = moved[p * DAYS : (p + 1) * DAYS]
        if n == 0:
            pl.semaphore_wait(met.at[0], 2)
            along_z(met.at[1], 2)
            pl.semaphore_wait(met.at[4], 2)
            for k in (2, 1, 3):
                xx = lax.rem(x + k, NX)
                r_copies.append(remote(rw.at[x], rw.at[x], rsend.at[k - 1], rrecv.at[x], x=xx))
                r_copies[-1].start()
        for k in (2, 1, 3):
            xx = lax.rem(x + k, NX)
            e_copies.append(
                remote(es.at[xx, :, cols], er.at[x, :, cols], esend.at[n, k - 1], erecv.at[n, x], x=xx)
            )
            e_copies[-1].start()
        e_own.append(pltpu.make_async_copy(es.at[x, :, cols], er.at[x, :, cols], ld.at[13 + n]))
        e_own[-1].start()

    pl.semaphore_wait(met.at[1], 2)
    along_z(met.at[2], 4)

    def shocks_here(n):
        cols = quarter(turn[n])
        e_own[n].wait()
        for k in range(1, NX):
            xx = lax.rem(x + k, NX)
            remote(
                es.at[xx, :, cols], er.at[xx, :, cols], esend.at[n, k - 1], erecv.at[n, xx], x=xx
            ).wait_recv()

    def hop(n, yy, piece):
        remote(shard(yy, c, piece), shard(yy, c, piece), msend.at[n], mrecv.at[n], y=yp).wait_recv()

    def passed_on(n, yy, piece, **where):
        onward.append(m_copy(n, shard(yy, c, piece), shard(yy, c, piece), **where))
        onward[-1].start()

    def relayed(n, yy, piece):
        remote(shard(yy, mate, piece), shard(yy, mate, piece), msend.at[n], mrecv.at[n], c=mate).wait_recv()

    onward = []
    aside = [{"z": lax.rem(z + 1, NZ)}, {"z": lax.rem(z + NZ - 1, NZ)}]
    for n in range(HALF):
        hop(group(0, n), ym, rising[n])
        passed_on(group(2, n), ym, rising[n], y=yp)
        passed_on(group(4, n), ym, rising[n], **aside[n % 2])
        passed_on(group(6, n), ym, rising[n], c=mate)
        hop(group(1, n), yp, falling[n])
        passed_on(group(3, n), yp, falling[n], y=ym)
        passed_on(group(5, n), yp, falling[n], **aside[n % 2])
        passed_on(group(7, n), yp, falling[n], c=mate)

    for copy in loads[1:]:
        copy.wait()

    def r_wait(k):
        xx = lax.rem(x + k, NX)
        remote(rw.at[x], rw.at[xx], rsend.at[k - 1], rrecv.at[xx], x=xx).wait_recv()

    for k in range(1, NX):
        r_wait(k)
    rows = lax.broadcasted_iota(jnp.int32, (DAYS, LANES), 0)
    lanes = lax.broadcasted_iota(jnp.int32, (DAYS, LANES), 1)
    pick = lanes == (rows & 7) * 8 + (rows >> 3)
    logs = jnp.zeros((8, LANES), f32)
    for j in range(NX):
        logs = logs + jnp.log(rw[j])
        spread = jnp.where(pick, jnp.broadcast_to(rw[j, 0:1], (DAYS, LANES)), 0.0)
        rb[pl.ds(j * DAYS, DAYS), :] = jnp.broadcast_to(jnp.sum(spread, axis=1, keepdims=True), (DAYS, LANES))
    lrs[...] = jnp.broadcast_to(jnp.sum(logs, axis=1, keepdims=True), (8, LANES))

    def later(k, copy):
        @pl.when(z + k < NZ)
        def _():
            copy(k)

    def lr_copy(k):
        return remote(lrs, lrr.at[z], lsend.at[k], lrecv.at[z], z=lax.rem(z + k, NZ))

    def eb_copy(k):
        return remote(ebs, ebr.at[z], bsend.at[k], brecv.at[z], z=lax.rem(z + k, NZ))

    sub = lax.broadcasted_iota(jnp.int32, (8, LANES), 0)

    @pl.loop(0, F // LANES)
    def _(k):
        cols = columns(k)
        keep = jnp.broadcast_to(jnp.exp(lpv[:, cols]), (8, LANES))
        before = jnp.ones((8, LANES), f32)
        for j in range(NX):
            decay = None
            for i in range(8):
                r = pl.ds(j * DAYS + i * 8, 8)
                today = keep * rb[r, :]
                decay = today if i == 0 else decay * today
                dd[r, cols] = decay
            for n, shift in enumerate((1, 2, 4)):
                dk[n, j, :, cols] = jnp.where(sub >= shift, decay, 0.0)
                decay = jnp.where(sub >= shift, decay * pltpu.roll(decay, shift, 0), decay)
            first = jnp.where(sub >= 1, pltpu.roll(decay, 1, 0), 1.0)
            total = jnp.broadcast_to(decay[7:8], (8, LANES))
            dx[j, :, cols] = first
            dt[j, :, cols] = total
            vv[j, :, cols] = first * before
            before = before * total

    def product(row, depth, first=False):
        at = pl.ds(pl.multiple_of(row, depth), depth)
        left = jnp.concatenate([er[j, :, at] for j in range(NX)], axis=0)
        for k in range(4):
            cols = pl.ds(k * 256, 256)
            term = jnp.dot(left, mb[at, cols], preferred_element_type=f32)
            acc[:, cols] = term if first else acc[:, cols] + term

    for n in range(HALF):
        hop(group(4, n), ym, falling[n])
        passed_on(group(8, n), ym, falling[n], c=mate)
        hop(group(5, n), yp, rising[n])
        passed_on(group(9, n), yp, rising[n], c=mate)
    for n in range(HALF):
        hop(group(2, n), y2, rising[n])
        passed_on(group(10, n), y2, rising[n], c=mate)
        hop(group(3, n), y2, falling[n])
        passed_on(group(11, n), y2, falling[n], c=mate)
    pl.semaphore_wait(met.at[2], 2)
    for k in range(1, NX):
        pl.semaphore_signal(met.at[3], inc=1, device_id={"x": lax.rem(x + k, NX)}, device_id_type=MESH_ID)
    for k in FAR_FIRST:
        later(k, lambda k: lr_copy(k).start())
    remote(m_in, mb.at[pl.ds(pl.multiple_of((y * 2 + mate) * 128, 128), 128), :], msend.at[group(12, 0)], mrecv.at[group(12, 0)], c=mate).wait_recv()
    shocks_here(0)
    product(y * 256, 256, True)
    for n in range(HALF):
        relayed(group(6, n), ym, rising[n])
        relayed(group(8, n), ym, falling[n])
    shocks_here(1)
    product(ym * 256, 256)
    for n in range(HALF):
        relayed(group(7, n), yp, falling[n])
        relayed(group(9, n), yp, rising[n])
    shocks_here(2)
    product(yp * 256, 256)
    shocks_here(3)
    for n in range(HALF):
        relayed(group(10, n), y2, rising[n])
        relayed(group(11, n), y2, falling[n])

    last = quarter(y2)
    left = jnp.concatenate([er[j, :, last] for j in range(NX)], axis=0)
    for w in range(4):
        wide = pl.ds(w * 256, 256)
        acc[:, wide] = acc[:, wide] + jnp.dot(left, mb[last, wide], preferred_element_type=f32)
        for k in (2 * w, 2 * w + 1):
            cols = pl.ds(k * LANES, LANES)
            log_keep = lpv[:, cols]
            keep = jnp.broadcast_to(jnp.exp(log_keep), (8, LANES))
            double = 2.0 * log_keep
            vol = jnp.broadcast_to(jnp.sqrt(-expm1(double)), (8, LANES))
            carried = jnp.zeros((8, LANES), f32)
            for j in range(NX):
                state = None
                for i in range(8):
                    r = pl.ds(j * DAYS + i * 8, 8)
                    shock = vol * acc[r, cols]
                    state = shock if i == 0 else (keep * rb[r, :]) * state + shock
                    acc[r, cols] = state
                for n, shift in enumerate((1, 2, 4)):
                    state = state + dk[n, j, :, cols] * pltpu.roll(state, shift, 0)
                first = jnp.where(sub >= 1, pltpu.roll(state, 1, 0), 0.0)
                uu[j, :, cols] = first + dx[j, :, cols] * carried
                carried = dt[j, :, cols] * carried + jnp.broadcast_to(state[7:8], (8, LANES))
            ebs[k : k + 1, :] = carried[0:1]

    for k in FAR_FIRST:
        later(k, lambda k: eb_copy(k).start())

    @pl.loop(0, F // LANES)
    def _(k):
        cols = columns(k)
        paths = lax.broadcasted_iota(jnp.int32, (PATHS, LANES), 0)
        cbs[pl.ds(k, 1), :] = jnp.sum(jnp.where(paths == x, s0v[:, cols], 0.0), axis=0, keepdims=True)
        for j in range(NX):
            u, v = uu[j, :, cols], vv[j, :, cols]
            for i in range(8):
                r = pl.ds(j * DAYS + i * 8, 8)
                decay = dd[r, cols]
                acc[r, cols] = acc[r, cols] + decay * u
                dd[r, cols] = decay * v

    short = scv[...].astype(f32)
    for k in range(F // LANES):
        block = jnp.broadcast_to(short[k : k + 1], (LANES, LANES))
        bm[pl.ds(k * LANES, LANES), pl.ds(K, LANES)] = block.T.astype(bf16)

    span = float(BLOCK) * lpd[...]

    @pl.loop(0, z)
    def _(u):
        remote(lrs, lrr.at[u], lsend.at[0], lrecv.at[u], z=u).wait_recv()
        lrr[pl.ds(u, 1)] = jnp.exp(span + lrr[u])[None]

    def entered(u, carry):
        remote(ebs, ebr.at[u], bsend.at[0], brecv.at[u], z=u).wait_recv()
        return lrr[u] * carry + ebr[u]

    cbs[...] = lax.fori_loop(0, z, entered, cbs[...])

    for w in range(4):
        wide = pl.ds(w * 256, 256)
        now = jnp.concatenate([cbs[k : k + 1, :] for k in (2 * w, 2 * w + 1)], axis=1)
        scenario = (acc[:, wide] + dd[:, wide] * now).astype(bf16)
        term = jnp.dot(scenario, bm[wide, :], preferred_element_type=f32)
        res[...] = term if w == 0 else res[...] + term

    base = jnp.zeros((8, LANES), f32)
    exponent = []
    for j in range(NX):
        run = jnp.zeros((8, LANES), f32)
        sums = []
        for i in range(8):
            run = run + (0.03 + 0.3 * res[pl.ds(j * DAYS + i * 8, 8), pl.ds(K, LANES)])
            sums.append(run)
        total = run
        for shift in (1, 2, 4):
            total = total + jnp.where(sub >= shift, pltpu.roll(total, shift, 0), 0.0)
        start = base + jnp.where(sub >= 1, pltpu.roll(total, 1, 0), 0.0)
        base = base + jnp.broadcast_to(total[7:8], (8, LANES))
        exponent += [(-1.0 / 256.0) * (start + s) for s in sums]
    top = functools.reduce(jnp.maximum, exponent)
    top = jnp.max(top, axis=0, keepdims=True)
    worth = jnp.zeros((8, LANES), f32)
    for n, power in enumerate(exponent):
        worth = worth + jnp.exp(power - top) * res[pl.ds(n * 8, 8), pl.ds(0, K)]
    fs[0:1, :] = jnp.sum(worth, axis=0, keepdims=True)
    low = lax.broadcasted_iota(jnp.int32, (1, LANES), 1) < LANES // 2
    fs[1:2, :] = jnp.where(low, base[0:1], top)
    mine = z * NX + x
    fr[pl.ds(mine, 1)] = fs[...][None]

    pl.semaphore_wait(met.at[3], NX - 1)
    def sums_to(zz, n):
        return remote(fs, fr.at[mine], fsend.at[0], frecv.at[0], z=zz, x=lax.rem(x + n, NX))

    for zz in range(NZ):
        for n in (2, 1, 3):
            sums_to(zz, n).start()

        @pl.when(zz != z)
        def _():
            sums_to(zz, 0).start()

    for copy in (*straight, *onward, *r_copies, *e_copies):
        copy.wait_send()
    for k in FAR_FIRST:
        later(k, lambda k: lr_copy(k).wait_send())
        later(k, lambda k: eb_copy(k).wait_send())
    others = fr.at[pl.ds(0, NZ * NX - 1)]
    everyone = remote(others, others, fsend.at[0], frecv.at[0], z=lax.rem(z + 1, NZ))
    everyone.wait_recv()
    passed = jnp.zeros((NX, LANES), f32)
    value = jnp.zeros((NX, LANES), f32)
    for u in range(NZ):
        part, both = (
            jnp.concatenate([fr[u * NX + j, r : r + 1] for j in range(NX)], axis=0) for r in range(2)
        )
        swapped = pltpu.roll(both, LANES // 2, 1)
        value = value + jnp.exp(jnp.where(low, swapped, both) - (1.0 / 256.0) * passed) * part
        passed = passed + jnp.where(low, both, swapped)
    out[...] = value * (1.0 / 4096.0)
    everyone.wait_send()


def local(e, s0, m, lp, reg, pay, sc):
    vmem, dma = pltpu.VMEM, pltpu.SemaphoreType.DMA
    return pl.pallas_call(
        kernel,
        out_shape=jax.ShapeDtypeStruct((PATHS, K), f32),
        in_specs=[pl.BlockSpec(memory_space=pl.ANY)] * 8,
        out_specs=pl.BlockSpec(memory_space=pltpu.VMEM),
        scratch_shapes=[
            vmem((DAYS, PATHS, F), bf16),
            vmem((PATHS, DAYS, F), bf16),
            vmem((NX, DAYS, F), bf16),
            vmem((F, F), bf16),
            vmem((F, 2 * K), bf16),
            vmem((BLOCK, F), f32),
            vmem((BLOCK, F), f32),
            vmem((BLOCK, 2 * K), f32),
            vmem((NX, 8, LANES), f32),
            vmem((BLOCK, LANES), f32),
            vmem((1, F), f32),
            vmem((8, LANES), f32),
            vmem((PATHS, F), f32),
            vmem((1, DAYS), f32),
            vmem((8, LANES), bf16),
            vmem((3, NX, 8, F), f32),
            vmem((NX, 8, F), f32),
            vmem((NX, 8, F), f32),
            vmem((NX, 8, F), f32),
            vmem((NX, 8, F), f32),
            vmem((8, LANES), f32),
            vmem((NZ, 8, LANES), f32),
            vmem((8, LANES), f32),
            vmem((NZ, 8, LANES), f32),
            vmem((8, LANES), f32),
            vmem((2, LANES), f32),
            vmem((NZ * NX, 2, LANES), f32),
            dma((17,)),
            dma((12 * HALF + 1,)), dma((12 * HALF + 1,)),
            dma((NY, NX)), dma((NY, NX)),
            dma((NX,)), dma((NX,)),
            dma((NZ,)), dma((NZ,)),
            dma((NZ,)), dma((NZ,)),
            dma((1,)), dma((1,)),
            pltpu.SemaphoreType.REGULAR((5,)),
        ],
        compiler_params=pltpu.CompilerParams(collective_id=0, has_side_effects=True, vmem_limit_bytes=32 << 20),
        name="scenarios",
    )(
        *(
            pltpu.with_memory_space_constraint(a, pltpu.HBM)
            for a in (e, s0, m, lp.reshape(1, F), lp.reshape(8, LANES), reg.reshape(1, DAYS), pay, sc.reshape(8, LANES))
        )
    )


def solution(mesh):
    split = Mesh(mesh.devices.reshape(NY, NC, NZ, NX), ("y", "c", "z", "x"))
    paths, days = ("y", "c"), ("z", "x")
    placed = (P(days, paths, None), P(paths, None), P(paths, None), P(), P(days), P(), P())
    return jax.shard_map(local, mesh=split, in_specs=placed, out_specs=P(paths, None), check_vma=False)
```

```python
import functools

import jax
import jax.numpy as jnp
from jax import lax
from jax.experimental import pallas as pl
from jax.experimental.pallas import tpu as pltpu
from jax.sharding import Mesh
from jax.sharding import PartitionSpec as P

MESH_ID = pl.DeviceIdType.MESH
NY, NC, NZ, NX = 4, 2, 16, 4
DAYS, PATHS, F, K = 64, 4, 1024, 128
BLOCK = DAYS * NX
PIECE = 16
HALF = 64 // PIECE
LANES = 128
FAR_FIRST = (8, 7, 9, 6, 10, 5, 11, 4, 12, 3, 13, 2, 14, 1, 15)
f32, bf16 = jnp.float32, jnp.bfloat16


def columns(k):
    return pl.ds(pl.multiple_of(k * LANES, LANES), LANES)


def expm1(v):
    total = jnp.ones_like(v)
    for n in range(10, 1, -1):
        total = 1.0 + total * v * (1.0 / n)
    return v * total


def remote(src, dst, send, recv, **where):
    return pltpu.make_async_remote_copy(
        src_ref=src, dst_ref=dst, send_sem=send, recv_sem=recv, device_id=where, device_id_type=MESH_ID
    )


def kernel(
    e_in, s0_in, m_in, lp_in, lpd_in, reg_in, pay_in, sc_in, out,
    ev, es, er, mb, bm, acc, dd, res, rw, rb, lpv, lpd, s0v, regv, scv,
    dk, dx, dt, uu, vv, lrs, lrr, ebs, ebr, cbs, fs, fr,
    ld, msend, mrecv, esend, erecv, rsend, rrecv, lsend, lrecv, bsend, brecv, fsend, frecv, met,
):
    y, c, z, x = (lax.axis_index(a) for a in ("y", "c", "z", "x"))
    yp, ym, y2 = lax.rem(y + 1, NY), lax.rem(y + NY - 1, NY), lax.rem(y + 2, NY)
    mate = 1 - c

    barrier = pltpu.get_barrier_semaphore()
    beside = [{"x": lax.rem(x + k, NX)} for k in (1, NX - 1)]
    peers = [{"c": mate}, {"y": yp}, {"y": ym}, *beside]
    for peer in peers:
        pl.semaphore_signal(barrier, inc=1, device_id=peer, device_id_type=MESH_ID)

    def along_z(semaphore, distance):
        for k in (distance, NZ - distance):
            pl.semaphore_signal(semaphore, inc=1, device_id={"z": lax.rem(z + k, NZ)}, device_id_type=MESH_ID)

    along_z(barrier, 1)

    def shard(yy, cc, piece):
        return mb.at[pl.ds(pl.multiple_of((yy * 2 + cc) * 128 + piece * PIECE, PIECE), PIECE), :]

    turn = (y, ym, yp, y2)
    width = F // NY

    def quarter(yy):
        return pl.ds(pl.multiple_of(yy * width, width), width)

    own_rows = mb.at[pl.ds(pl.multiple_of((y * 2 + c) * 128, 128), 128), :]
    mixer = pltpu.make_async_copy(m_in, own_rows, ld.at[7])
    shocks = [
        pltpu.make_async_copy(e_in.at[:, :, quarter(yy)], ev.at[:, :, quarter(yy)], ld.at[9 + n])
        for n, yy in enumerate(turn)
    ]
    loads = [
        pltpu.make_async_copy(reg_in, regv, ld.at[1]),
        pltpu.make_async_copy(lp_in, lpv, ld.at[2]),
        pltpu.make_async_copy(lpd_in, lpd, ld.at[3]),
        pltpu.make_async_copy(s0_in, s0v, ld.at[4]),
        pltpu.make_async_copy(sc_in, scv, ld.at[5]),
        pltpu.make_async_copy(pay_in, bm.at[:, pl.ds(0, K)], ld.at[6]),
    ]
    for copy in (mixer, *shocks, *loads):
        copy.start()

    pl.semaphore_wait(barrier, len(peers) + 2)
    def group(g, n):
        return g * HALF + n

    def m_copy(n, src, dst, **where):
        return remote(src, dst, msend.at[n], mrecv.at[n], **where)

    odd = lax.rem(z, 2)
    rising = [HALF * odd + n for n in range(HALF)]
    falling = [HALF * (1 - odd) + n for n in range(HALF)]

    straight = []
    for n in range(HALF):
        straight.append(m_copy(group(0, n), shard(y, c, rising[n]), shard(y, c, rising[n]), y=yp))
        straight.append(m_copy(group(1, n), shard(y, c, falling[n]), shard(y, c, falling[n]), y=ym))
    straight.append(m_copy(group(12, 0), own_rows, own_rows, c=mate))
    mixer.wait()
    for copy in straight:
        copy.start()
    along_z(met.at[0], 1)

    for peer in beside:
        pl.semaphore_signal(met.at[4], inc=1, device_id=peer, device_id_type=MESH_ID)

    loads[0].wait()
    rw[pl.ds(x, 1)] = jnp.ones((1, 8, LANES), f32)
    rw[pl.ds(x, 1), :, pl.ds(0, DAYS)] = jnp.broadcast_to(regv[...][None], (1, 8, DAYS))
    r_copies, e_copies = [], []

    row = lax.broadcasted_iota(jnp.int32, (256, 256), 0)
    col = lax.broadcasted_iota(jnp.int32, (256, 256), 1)
    source = (((row & 7) * 8 + ((row >> 3) & 7)) << 2) + (row >> 6)
    order = (col == source).astype(f32).astype(bf16)
    e_own = []
    for n, yy in enumerate(turn):
        cols = quarter(yy)
        shocks[n].wait()
        flat = ev[:, :, cols].reshape(DAYS * PATHS, width)
        moved = jnp.dot(order, flat, preferred_element_type=f32).astype(bf16)
        for p in range(PATHS):
            es[p, :, cols] = moved[p * DAYS : (p + 1) * DAYS]
        if n == 0:
            pl.semaphore_wait(met.at[0], 2)
            along_z(met.at[1], 2)
            pl.semaphore_wait(met.at[4], 2)
            for k in (2, 1, 3):
                xx = lax.rem(x + k, NX)
                r_copies.append(remote(rw.at[x], rw.at[x], rsend.at[k - 1], rrecv.at[x], x=xx))
                r_copies[-1].start()
        for k in (2, 1, 3):
            xx = lax.rem(x + k, NX)
            e_copies.append(
                remote(es.at[xx, :, cols], er.at[x, :, cols], esend.at[n, k - 1], erecv.at[n, x], x=xx)
            )
            e_copies[-1].start()
        e_own.append(pltpu.make_async_copy(es.at[x, :, cols], er.at[x, :, cols], ld.at[13 + n]))
        e_own[-1].start()

    pl.semaphore_wait(met.at[1], 2)
    along_z(met.at[2], 4)

    def shocks_here(n):
        cols = quarter(turn[n])
        e_own[n].wait()
        for k in range(1, NX):
            xx = lax.rem(x + k, NX)
            remote(
                es.at[xx, :, cols], er.at[xx, :, cols], esend.at[n, k - 1], erecv.at[n, xx], x=xx
            ).wait_recv()

    def half(yy, cc, lower):
        return mb.at[pl.ds(pl.multiple_of((yy * 2 + cc) * 128 + 64 * lower, 64), 64), :]

    def half_relayed(g, yy, lower):
        there = half(yy, mate, lower)
        remote(there, there, msend.at[group(g, 0)], mrecv.at[group(g, 0)], c=mate).wait_recv()

    def hop(n, yy, piece):
        remote(shard(yy, c, piece), shard(yy, c, piece), msend.at[n], mrecv.at[n], y=yp).wait_recv()

    def passed_on(n, yy, piece, **where):
        onward.append(m_copy(n, shard(yy, c, piece), shard(yy, c, piece), **where))
        onward[-1].start()

    def relayed(n, yy, piece):
        remote(shard(yy, mate, piece), shard(yy, mate, piece), msend.at[n], mrecv.at[n], c=mate).wait_recv()

    onward = []
    aside = [{"z": lax.rem(z + 1, NZ)}, {"z": lax.rem(z + NZ - 1, NZ)}]
    for n in range(HALF):
        hop(group(0, n), ym, rising[n])
        passed_on(group(2, n), ym, rising[n], y=yp)
        passed_on(group(4, n), ym, rising[n], **aside[n % 2])
        hop(group(1, n), yp, falling[n])
        passed_on(group(3, n), yp, falling[n], y=ym)
        passed_on(group(5, n), yp, falling[n], **aside[n % 2])
    straight_halves = ((6, ym, odd), (7, yp, 1 - odd))
    for g, yy, lower in straight_halves:
        onward.append(m_copy(group(g, 0), half(yy, c, lower), half(yy, c, lower), c=mate))
        onward[-1].start()

    for copy in loads[1:]:
        copy.wait()

    def r_wait(k):
        xx = lax.rem(x + k, NX)
        remote(rw.at[x], rw.at[xx], rsend.at[k - 1], rrecv.at[xx], x=xx).wait_recv()

    for k in range(1, NX):
        r_wait(k)
    rows = lax.broadcasted_iota(jnp.int32, (DAYS, LANES), 0)
    lanes = lax.broadcasted_iota(jnp.int32, (DAYS, LANES), 1)
    pick = lanes == (rows & 7) * 8 + (rows >> 3)
    logs = jnp.zeros((8, LANES), f32)
    for j in range(NX):
        logs = logs + jnp.log(rw[j])
        spread = jnp.where(pick, jnp.broadcast_to(rw[j, 0:1], (DAYS, LANES)), 0.0)
        rb[pl.ds(j * DAYS, DAYS), :] = jnp.broadcast_to(jnp.sum(spread, axis=1, keepdims=True), (DAYS, LANES))
    lrs[...] = jnp.broadcast_to(jnp.sum(logs, axis=1, keepdims=True), (8, LANES))

    def later(k, copy):
        @pl.when(z + k < NZ)
        def _():
            copy(k)

    def lr_copy(k):
        return remote(lrs, lrr.at[z], lsend.at[k], lrecv.at[z], z=lax.rem(z + k, NZ))

    def eb_copy(k):
        return remote(ebs, ebr.at[z], bsend.at[k], brecv.at[z], z=lax.rem(z + k, NZ))

    sub = lax.broadcasted_iota(jnp.int32, (8, LANES), 0)

    @pl.loop(0, F // LANES)
    def _(k):
        cols = columns(k)
        keep = jnp.broadcast_to(jnp.exp(lpv[:, cols]), (8, LANES))
        before = jnp.ones((8, LANES), f32)
        for j in range(NX):
            decay = None
            for i in range(8):
                r = pl.ds(j * DAYS + i * 8, 8)
                today = keep * rb[r, :]
                decay = today if i == 0 else decay * today
                dd[r, cols] = decay
            for n, shift in enumerate((1, 2, 4)):
                dk[n, j, :, cols] = jnp.where(sub >= shift, decay, 0.0)
                decay = jnp.where(sub >= shift, decay * pltpu.roll(decay, shift, 0), decay)
            first = jnp.where(sub >= 1, pltpu.roll(decay, 1, 0), 1.0)
            total = jnp.broadcast_to(decay[7:8], (8, LANES))
            dx[j, :, cols] = first
            dt[j, :, cols] = total
            vv[j, :, cols] = first * before
            before = before * total

    def product(row, depth, first=False):
        at = pl.ds(pl.multiple_of(row, depth), depth)
        left = jnp.concatenate([er[j, :, at] for j in range(NX)], axis=0)
        for k in range(4):
            cols = pl.ds(k * 256, 256)
            term = jnp.dot(left, mb[at, cols], preferred_element_type=f32)
            acc[:, cols] = term if first else acc[:, cols] + term

    for n in range(HALF):
        hop(group(4, n), ym, falling[n])
        passed_on(group(8, n), ym, falling[n], c=mate)
        hop(group(5, n), yp, rising[n])
        passed_on(group(9, n), yp, rising[n], c=mate)
    for n in range(HALF):
        hop(group(2, n), y2, rising[n])
        passed_on(group(10, n), y2, rising[n], c=mate)
        hop(group(3, n), y2, falling[n])
        passed_on(group(11, n), y2, falling[n], c=mate)
    pl.semaphore_wait(met.at[2], 2)
    for k in range(1, NX):
        pl.semaphore_signal(met.at[3], inc=1, device_id={"x": lax.rem(x + k, NX)}, device_id_type=MESH_ID)
    for k in FAR_FIRST:
        later(k, lambda k: lr_copy(k).start())
    remote(m_in, mb.at[pl.ds(pl.multiple_of((y * 2 + mate) * 128, 128), 128), :], msend.at[group(12, 0)], mrecv.at[group(12, 0)], c=mate).wait_recv()
    shocks_here(0)
    product(y * 256, 256, True)
    half_relayed(*straight_halves[0])
    for n in range(HALF):
        relayed(group(8, n), ym, falling[n])
    shocks_here(1)
    product(ym * 256, 256)
    half_relayed(*straight_halves[1])
    for n in range(HALF):
        relayed(group(9, n), yp, rising[n])
    shocks_here(2)
    product(yp * 256, 256)
    shocks_here(3)
    for n in range(HALF):
        relayed(group(10, n), y2, rising[n])
        relayed(group(11, n), y2, falling[n])

    last = quarter(y2)
    left = jnp.concatenate([er[j, :, last] for j in range(NX)], axis=0)
    for w in range(4):
        wide = pl.ds(w * 256, 256)
        acc[:, wide] = acc[:, wide] + jnp.dot(left, mb[last, wide], preferred_element_type=f32)
        for k in (2 * w, 2 * w + 1):
            cols = pl.ds(k * LANES, LANES)
            log_keep = lpv[:, cols]
            keep = jnp.broadcast_to(jnp.exp(log_keep), (8, LANES))
            double = 2.0 * log_keep
            vol = jnp.broadcast_to(jnp.sqrt(-expm1(double)), (8, LANES))
            carried = jnp.zeros((8, LANES), f32)
            for j in range(NX):
                state = None
                for i in range(8):
                    r = pl.ds(j * DAYS + i * 8, 8)
                    shock = vol * acc[r, cols]
                    state = shock if i == 0 else (keep * rb[r, :]) * state + shock
                    acc[r, cols] = state
                for n, shift in enumerate((1, 2, 4)):
                    state = state + dk[n, j, :, cols] * pltpu.roll(state, shift, 0)
                first = jnp.where(sub >= 1, pltpu.roll(state, 1, 0), 0.0)
                uu[j, :, cols] = first + dx[j, :, cols] * carried
                carried = dt[j, :, cols] * carried + jnp.broadcast_to(state[7:8], (8, LANES))
            ebs[k : k + 1, :] = carried[0:1]

    for k in FAR_FIRST:
        later(k, lambda k: eb_copy(k).start())

    @pl.loop(0, F // LANES)
    def _(k):
        cols = columns(k)
        paths = lax.broadcasted_iota(jnp.int32, (PATHS, LANES), 0)
        cbs[pl.ds(k, 1), :] = jnp.sum(jnp.where(paths == x, s0v[:, cols], 0.0), axis=0, keepdims=True)
        for j in range(NX):
            u, v = uu[j, :, cols], vv[j, :, cols]
            for i in range(8):
                r = pl.ds(j * DAYS + i * 8, 8)
                decay = dd[r, cols]
                acc[r, cols] = acc[r, cols] + decay * u
                dd[r, cols] = decay * v

    short = scv[...].astype(f32)
    for k in range(F // LANES):
        block = jnp.broadcast_to(short[k : k + 1], (LANES, LANES))
        bm[pl.ds(k * LANES, LANES), pl.ds(K, LANES)] = block.T.astype(bf16)

    span = float(BLOCK) * lpd[...]

    @pl.loop(0, z)
    def _(u):
        remote(lrs, lrr.at[u], lsend.at[0], lrecv.at[u], z=u).wait_recv()
        lrr[pl.ds(u, 1)] = jnp.exp(span + lrr[u])[None]

    def entered(u, carry):
        remote(ebs, ebr.at[u], bsend.at[0], brecv.at[u], z=u).wait_recv()
        return lrr[u] * carry + ebr[u]

    cbs[...] = lax.fori_loop(0, z, entered, cbs[...])

    for w in range(4):
        wide = pl.ds(w * 256, 256)
        now = jnp.concatenate([cbs[k : k + 1, :] for k in (2 * w, 2 * w + 1)], axis=1)
        scenario = (acc[:, wide] + dd[:, wide] * now).astype(bf16)
        term = jnp.dot(scenario, bm[wide, :], preferred_element_type=f32)
        res[...] = term if w == 0 else res[...] + term

    base = jnp.zeros((8, LANES), f32)
    exponent = []
    for j in range(NX):
        run = jnp.zeros((8, LANES), f32)
        sums = []
        for i in range(8):
            run = run + (0.03 + 0.3 * res[pl.ds(j * DAYS + i * 8, 8), pl.ds(K, LANES)])
            sums.append(run)
        total = run
        for shift in (1, 2, 4):
            total = total + jnp.where(sub >= shift, pltpu.roll(total, shift, 0), 0.0)
        start = base + jnp.where(sub >= 1, pltpu.roll(total, 1, 0), 0.0)
        base = base + jnp.broadcast_to(total[7:8], (8, LANES))
        exponent += [(-1.0 / 256.0) * (start + s) for s in sums]
    top = functools.reduce(jnp.maximum, exponent)
    top = jnp.max(top, axis=0, keepdims=True)
    worth = jnp.zeros((8, LANES), f32)
    for n, power in enumerate(exponent):
        worth = worth + jnp.exp(power - top) * res[pl.ds(n * 8, 8), pl.ds(0, K)]
    fs[0:1, :] = jnp.sum(worth, axis=0, keepdims=True)
    low = lax.broadcasted_iota(jnp.int32, (1, LANES), 1) < LANES // 2
    fs[1:2, :] = jnp.where(low, base[0:1], top)
    mine = z * NX + x
    fr[pl.ds(mine, 1)] = fs[...][None]

    pl.semaphore_wait(met.at[3], NX - 1)
    def sums_to(zz, n):
        return remote(fs, fr.at[mine], fsend.at[0], frecv.at[0], z=zz, x=lax.rem(x + n, NX))

    for zz in range(NZ):
        for n in (2, 1, 3):
            sums_to(zz, n).start()

        @pl.when(zz != z)
        def _():
            sums_to(zz, 0).start()

    for copy in (*straight, *onward, *r_copies, *e_copies):
        copy.wait_send()
    for k in FAR_FIRST:
        later(k, lambda k: lr_copy(k).wait_send())
        later(k, lambda k: eb_copy(k).wait_send())
    others = fr.at[pl.ds(0, NZ * NX - 1)]
    everyone = remote(others, others, fsend.at[0], frecv.at[0], z=lax.rem(z + 1, NZ))
    everyone.wait_recv()
    passed = jnp.zeros((NX, LANES), f32)
    value = jnp.zeros((NX, LANES), f32)
    for u in range(NZ):
        part, both = (
            jnp.concatenate([fr[u * NX + j, r : r + 1] for j in range(NX)], axis=0) for r in range(2)
        )
        swapped = pltpu.roll(both, LANES // 2, 1)
        value = value + jnp.exp(jnp.where(low, swapped, both) - (1.0 / 256.0) * passed) * part
        passed = passed + jnp.where(low, both, swapped)
    out[...] = value * (1.0 / 4096.0)
    everyone.wait_send()


def local(e, s0, m, lp, reg, pay, sc):
    vmem, dma = pltpu.VMEM, pltpu.SemaphoreType.DMA
    return pl.pallas_call(
        kernel,
        out_shape=jax.ShapeDtypeStruct((PATHS, K), f32),
        in_specs=[pl.BlockSpec(memory_space=pl.ANY)] * 8,
        out_specs=pl.BlockSpec(memory_space=pltpu.VMEM),
        scratch_shapes=[
            vmem((DAYS, PATHS, F), bf16),
            vmem((PATHS, DAYS, F), bf16),
            vmem((NX, DAYS, F), bf16),
            vmem((F, F), bf16),
            vmem((F, 2 * K), bf16),
            vmem((BLOCK, F), f32),
            vmem((BLOCK, F), f32),
            vmem((BLOCK, 2 * K), f32),
            vmem((NX, 8, LANES), f32),
            vmem((BLOCK, LANES), f32),
            vmem((1, F), f32),
            vmem((8, LANES), f32),
            vmem((PATHS, F), f32),
            vmem((1, DAYS), f32),
            vmem((8, LANES), bf16),
            vmem((3, NX, 8, F), f32),
            vmem((NX, 8, F), f32),
            vmem((NX, 8, F), f32),
            vmem((NX, 8, F), f32),
            vmem((NX, 8, F), f32),
            vmem((8, LANES), f32),
            vmem((NZ, 8, LANES), f32),
            vmem((8, LANES), f32),
            vmem((NZ, 8, LANES), f32),
            vmem((8, LANES), f32),
            vmem((2, LANES), f32),
            vmem((NZ * NX, 2, LANES), f32),
            dma((17,)),
            dma((12 * HALF + 1,)), dma((12 * HALF + 1,)),
            dma((NY, NX)), dma((NY, NX)),
            dma((NX,)), dma((NX,)),
            dma((NZ,)), dma((NZ,)),
            dma((NZ,)), dma((NZ,)),
            dma((1,)), dma((1,)),
            pltpu.SemaphoreType.REGULAR((5,)),
        ],
        compiler_params=pltpu.CompilerParams(collective_id=0, has_side_effects=True, vmem_limit_bytes=32 << 20),
        name="scenarios",
    )(
        *(
            pltpu.with_memory_space_constraint(a, pltpu.HBM)
            for a in (e, s0, m, lp.reshape(1, F), lp.reshape(8, LANES), reg.reshape(1, DAYS), pay, sc.reshape(8, LANES))
        )
    )


def solution(mesh):
    split = Mesh(mesh.devices.reshape(NY, NC, NZ, NX), ("y", "c", "z", "x"))
    paths, days = ("y", "c"), ("z", "x")
    placed = (P(days, paths, None), P(paths, None), P(paths, None), P(), P(days), P(), P())
    return jax.shard_map(local, mesh=split, in_specs=placed, out_specs=P(paths, None), check_vma=False)
```

```python
import functools

import jax
import jax.numpy as jnp
from jax import lax
from jax.experimental import pallas as pl
from jax.experimental.pallas import tpu as pltpu
from jax.sharding import Mesh
from jax.sharding import PartitionSpec as P

MESH_ID = pl.DeviceIdType.MESH
NY, NC, NZ, NX = 4, 2, 16, 4
DAYS, PATHS, F, K = 64, 4, 1024, 128
BLOCK = DAYS * NX
PIECE = 16
HALF = 64 // PIECE
LANES = 128
FAR_FIRST = (8, 7, 9, 6, 10, 5, 11, 4, 12, 3, 13, 2, 14, 1, 15)
f32, bf16 = jnp.float32, jnp.bfloat16


def columns(k):
    return pl.ds(pl.multiple_of(k * LANES, LANES), LANES)


def expm1(v):
    total = jnp.ones_like(v)
    for n in range(10, 1, -1):
        total = 1.0 + total * v * (1.0 / n)
    return v * total


def remote(src, dst, send, recv, **where):
    return pltpu.make_async_remote_copy(
        src_ref=src, dst_ref=dst, send_sem=send, recv_sem=recv, device_id=where, device_id_type=MESH_ID
    )


def kernel(
    e_in, s0_in, m_in, lp_in, lpd_in, reg_in, pay_in, sc_in, out,
    ev, es, er, mb, bm, acc, dd, res, rw, rb, lpv, lpd, s0v, regv, scv,
    dk, dx, dt, uu, vv, lrs, lrr, ebs, ebr, cbs, fs, fr,
    ld, msend, mrecv, esend, erecv, rsend, rrecv, lsend, lrecv, bsend, brecv, fsend, frecv, met,
):
    y, c, z, x = (lax.axis_index(a) for a in ("y", "c", "z", "x"))
    yp, ym, y2 = lax.rem(y + 1, NY), lax.rem(y + NY - 1, NY), lax.rem(y + 2, NY)
    mate = 1 - c

    barrier = pltpu.get_barrier_semaphore()
    beside = [{"x": lax.rem(x + k, NX)} for k in (1, NX - 1)]
    peers = [{"c": mate}, {"y": yp}, {"y": ym}, *beside]
    for peer in peers:
        pl.semaphore_signal(barrier, inc=1, device_id=peer, device_id_type=MESH_ID)

    def along_z(semaphore, distance):
        for k in (distance, NZ - distance):
            pl.semaphore_signal(semaphore, inc=1, device_id={"z": lax.rem(z + k, NZ)}, device_id_type=MESH_ID)

    along_z(barrier, 1)

    def shard(yy, cc, piece):
        return mb.at[pl.ds(pl.multiple_of((yy * 2 + cc) * 128 + piece * PIECE, PIECE), PIECE), :]

    turn = (y, ym, yp, y2)
    width = F // NY

    def quarter(yy):
        return pl.ds(pl.multiple_of(yy * width, width), width)

    own_rows = mb.at[pl.ds(pl.multiple_of((y * 2 + c) * 128, 128), 128), :]
    mixer = pltpu.make_async_copy(m_in, own_rows, ld.at[7])
    shocks = [
        pltpu.make_async_copy(e_in.at[:, :, quarter(yy)], ev.at[:, :, quarter(yy)], ld.at[9 + n])
        for n, yy in enumerate(turn)
    ]
    loads = [
        pltpu.make_async_copy(reg_in, regv, ld.at[1]),
        pltpu.make_async_copy(lp_in, lpv, ld.at[2]),
        pltpu.make_async_copy(lpd_in, lpd, ld.at[3]),
        pltpu.make_async_copy(s0_in, s0v, ld.at[4]),
        pltpu.make_async_copy(sc_in, scv, ld.at[5]),
        pltpu.make_async_copy(pay_in, bm.at[:, pl.ds(0, K)], ld.at[6]),
    ]
    for copy in (mixer, *shocks, *loads):
        copy.start()

    pl.semaphore_wait(barrier, len(peers) + 2)
    def group(g, n):
        return g * HALF + n

    def m_copy(n, src, dst, **where):
        return remote(src, dst, msend.at[n], mrecv.at[n], **where)

    odd = lax.rem(z, 2)
    rising = [HALF * odd + n for n in range(HALF)]
    falling = [HALF * (1 - odd) + n for n in range(HALF)]

    straight = []
    for n in range(HALF):
        straight.append(m_copy(group(0, n), shard(y, c, rising[n]), shard(y, c, rising[n]), y=yp))
        straight.append(m_copy(group(1, n), shard(y, c, falling[n]), shard(y, c, falling[n]), y=ym))
    straight.append(m_copy(group(12, 0), own_rows, own_rows, c=mate))
    mixer.wait()
    for copy in straight:
        copy.start()
    along_z(met.at[0], 1)

    for peer in beside:
        pl.semaphore_signal(met.at[4], inc=1, device_id=peer, device_id_type=MESH_ID)

    loads[0].wait()
    rw[pl.ds(x, 1)] = jnp.ones((1, 8, LANES), f32)
    rw[pl.ds(x, 1), :, pl.ds(0, DAYS)] = jnp.broadcast_to(regv[...][None], (1, 8, DAYS))
    r_copies, e_copies = [], []

    row = lax.broadcasted_iota(jnp.int32, (256, 256), 0)
    col = lax.broadcasted_iota(jnp.int32, (256, 256), 1)
    source = (((row & 7) * 8 + ((row >> 3) & 7)) << 2) + (row >> 6)
    order = (col == source).astype(f32).astype(bf16)
    e_own = []
    for n, yy in enumerate(turn):
        cols = quarter(yy)
        shocks[n].wait()
        flat = ev[:, :, cols].reshape(DAYS * PATHS, width)
        moved = jnp.dot(order, flat, preferred_element_type=f32).astype(bf16)
        for p in range(PATHS):
            es[p, :, cols] = moved[p * DAYS : (p + 1) * DAYS]
        if n == 0:
            pl.semaphore_wait(met.at[0], 2)
            along_z(met.at[1], 2)
            pl.semaphore_wait(met.at[4], 2)
            for k in (2, 1, 3):
                xx = lax.rem(x + k, NX)
                r_copies.append(remote(rw.at[x], rw.at[x], rsend.at[k - 1], rrecv.at[x], x=xx))
                r_copies[-1].start()
        for k in (2, 1, 3):
            xx = lax.rem(x + k, NX)
            e_copies.append(
                remote(es.at[xx, :, cols], er.at[x, :, cols], esend.at[n, k - 1], erecv.at[n, x], x=xx)
            )
            e_copies[-1].start()
        e_own.append(pltpu.make_async_copy(es.at[x, :, cols], er.at[x, :, cols], ld.at[13 + n]))

    pl.semaphore_wait(met.at[1], 2)
    along_z(met.at[2], 4)

    def shocks_here(n):
        cols = quarter(turn[n])
        e_own[n].wait()
        for k in range(1, NX):
            xx = lax.rem(x + k, NX)
            remote(
                es.at[xx, :, cols], er.at[xx, :, cols], esend.at[n, k - 1], erecv.at[n, xx], x=xx
            ).wait_recv()

    def half(yy, cc, lower):
        return mb.at[pl.ds(pl.multiple_of((yy * 2 + cc) * 128 + 64 * lower, 64), 64), :]

    def half_relayed(g, yy, lower):
        there = half(yy, mate, lower)
        remote(there, there, msend.at[group(g, 0)], mrecv.at[group(g, 0)], c=mate).wait_recv()

    def hop(n, yy, piece):
        remote(shard(yy, c, piece), shard(yy, c, piece), msend.at[n], mrecv.at[n], y=yp).wait_recv()

    def passed_on(n, yy, piece, **where):
        onward.append(m_copy(n, shard(yy, c, piece), shard(yy, c, piece), **where))
        onward[-1].start()

    def relayed(n, yy, piece):
        remote(shard(yy, mate, piece), shard(yy, mate, piece), msend.at[n], mrecv.at[n], c=mate).wait_recv()

    onward = []
    aside = [{"z": lax.rem(z + 1, NZ)}, {"z": lax.rem(z + NZ - 1, NZ)}]
    for n in range(HALF):
        hop(group(0, n), ym, rising[n])
        passed_on(group(2, n), ym, rising[n], y=yp)
        passed_on(group(4, n), ym, rising[n], **aside[n % 2])
        hop(group(1, n), yp, falling[n])
        passed_on(group(3, n), yp, falling[n], y=ym)
        passed_on(group(5, n), yp, falling[n], **aside[n % 2])
    straight_halves = ((6, ym, odd), (7, yp, 1 - odd))
    for g, yy, lower in straight_halves:
        onward.append(m_copy(group(g, 0), half(yy, c, lower), half(yy, c, lower), c=mate))
        onward[-1].start()

    for copy in e_own:
        copy.start()
    for copy in loads[1:]:
        copy.wait()

    def r_wait(k):
        xx = lax.rem(x + k, NX)
        remote(rw.at[x], rw.at[xx], rsend.at[k - 1], rrecv.at[xx], x=xx).wait_recv()

    for k in range(1, NX):
        r_wait(k)
    rows = lax.broadcasted_iota(jnp.int32, (DAYS, LANES), 0)
    lanes = lax.broadcasted_iota(jnp.int32, (DAYS, LANES), 1)
    pick = lanes == (rows & 7) * 8 + (rows >> 3)
    logs = jnp.zeros((8, LANES), f32)
    for j in range(NX):
        logs = logs + jnp.log(rw[j])
        spread = jnp.where(pick, jnp.broadcast_to(rw[j, 0:1], (DAYS, LANES)), 0.0)
        rb[pl.ds(j * DAYS, DAYS), :] = jnp.broadcast_to(jnp.sum(spread, axis=1, keepdims=True), (DAYS, LANES))
    lrs[...] = jnp.broadcast_to(jnp.sum(logs, axis=1, keepdims=True), (8, LANES))

    def later(k, copy):
        @pl.when(z + k < NZ)
        def _():
            copy(k)

    def lr_copy(k):
        return remote(lrs, lrr.at[z], lsend.at[k], lrecv.at[z], z=lax.rem(z + k, NZ))

    def eb_copy(k):
        return remote(ebs, ebr.at[z], bsend.at[k], brecv.at[z], z=lax.rem(z + k, NZ))

    sub = lax.broadcasted_iota(jnp.int32, (8, LANES), 0)

    @pl.loop(0, F // LANES)
    def _(k):
        cols = columns(k)
        keep = jnp.broadcast_to(jnp.exp(lpv[:, cols]), (8, LANES))
        before = jnp.ones((8, LANES), f32)
        for j in range(NX):
            decay = None
            for i in range(8):
                r = pl.ds(j * DAYS + i * 8, 8)
                today = keep * rb[r, :]
                decay = today if i == 0 else decay * today
                dd[r, cols] = decay
            for n, shift in enumerate((1, 2, 4)):
                dk[n, j, :, cols] = jnp.where(sub >= shift, decay, 0.0)
                decay = jnp.where(sub >= shift, decay * pltpu.roll(decay, shift, 0), decay)
            first = jnp.where(sub >= 1, pltpu.roll(decay, 1, 0), 1.0)
            total = jnp.broadcast_to(decay[7:8], (8, LANES))
            dx[j, :, cols] = first
            dt[j, :, cols] = total
            vv[j, :, cols] = first * before
            before = before * total

    def product(row, depth, first=False):
        at = pl.ds(pl.multiple_of(row, depth), depth)
        left = jnp.concatenate([er[j, :, at] for j in range(NX)], axis=0)
        for k in range(4):
            cols = pl.ds(k * 256, 256)
            term = jnp.dot(left, mb[at, cols], preferred_element_type=f32)
            acc[:, cols] = term if first else acc[:, cols] + term

    for n in range(HALF):
        hop(group(4, n), ym, falling[n])
        passed_on(group(8, n), ym, falling[n], c=mate)
        hop(group(5, n), yp, rising[n])
        passed_on(group(9, n), yp, rising[n], c=mate)
    for n in range(HALF):
        hop(group(2, n), y2, rising[n])
        passed_on(group(10, n), y2, rising[n], c=mate)
        hop(group(3, n), y2, falling[n])
        passed_on(group(11, n), y2, falling[n], c=mate)
    pl.semaphore_wait(met.at[2], 2)
    for k in range(1, NX):
        pl.semaphore_signal(met.at[3], inc=1, device_id={"x": lax.rem(x + k, NX)}, device_id_type=MESH_ID)
    for k in FAR_FIRST:
        later(k, lambda k: lr_copy(k).start())
    remote(m_in, mb.at[pl.ds(pl.multiple_of((y * 2 + mate) * 128, 128), 128), :], msend.at[group(12, 0)], mrecv.at[group(12, 0)], c=mate).wait_recv()
    shocks_here(0)
    product(y * 256, 256, True)
    half_relayed(*straight_halves[0])
    for n in range(HALF):
        relayed(group(8, n), ym, falling[n])
    shocks_here(1)
    product(ym * 256, 256)
    half_relayed(*straight_halves[1])
    for n in range(HALF):
        relayed(group(9, n), yp, rising[n])
    shocks_here(2)
    product(yp * 256, 256)
    shocks_here(3)
    for n in range(HALF):
        relayed(group(10, n), y2, rising[n])
        relayed(group(11, n), y2, falling[n])

    last = quarter(y2)
    left = jnp.concatenate([er[j, :, last] for j in range(NX)], axis=0)
    for w in range(4):
        wide = pl.ds(w * 256, 256)
        acc[:, wide] = acc[:, wide] + jnp.dot(left, mb[last, wide], preferred_element_type=f32)
        for k in (2 * w, 2 * w + 1):
            cols = pl.ds(k * LANES, LANES)
            log_keep = lpv[:, cols]
            keep = jnp.broadcast_to(jnp.exp(log_keep), (8, LANES))
            double = 2.0 * log_keep
            vol = jnp.broadcast_to(jnp.sqrt(-expm1(double)), (8, LANES))
            carried = jnp.zeros((8, LANES), f32)
            for j in range(NX):
                state = None
                for i in range(8):
                    r = pl.ds(j * DAYS + i * 8, 8)
                    shock = vol * acc[r, cols]
                    state = shock if i == 0 else (keep * rb[r, :]) * state + shock
                    acc[r, cols] = state
                for n, shift in enumerate((1, 2, 4)):
                    state = state + dk[n, j, :, cols] * pltpu.roll(state, shift, 0)
                first = jnp.where(sub >= 1, pltpu.roll(state, 1, 0), 0.0)
                uu[j, :, cols] = first + dx[j, :, cols] * carried
                carried = dt[j, :, cols] * carried + jnp.broadcast_to(state[7:8], (8, LANES))
            ebs[k : k + 1, :] = carried[0:1]

    for k in FAR_FIRST:
        later(k, lambda k: eb_copy(k).start())

    @pl.loop(0, F // LANES)
    def _(k):
        cols = columns(k)
        paths = lax.broadcasted_iota(jnp.int32, (PATHS, LANES), 0)
        cbs[pl.ds(k, 1), :] = jnp.sum(jnp.where(paths == x, s0v[:, cols], 0.0), axis=0, keepdims=True)
        for j in range(NX):
            u, v = uu[j, :, cols], vv[j, :, cols]
            for i in range(8):
                r = pl.ds(j * DAYS + i * 8, 8)
                decay = dd[r, cols]
                acc[r, cols] = acc[r, cols] + decay * u
                dd[r, cols] = decay * v

    short = scv[...].astype(f32)
    for k in range(F // LANES):
        block = jnp.broadcast_to(short[k : k + 1], (LANES, LANES))
        bm[pl.ds(k * LANES, LANES), pl.ds(K, LANES)] = block.T.astype(bf16)

    span = float(BLOCK) * lpd[...]

    @pl.loop(0, z)
    def _(u):
        remote(lrs, lrr.at[u], lsend.at[0], lrecv.at[u], z=u).wait_recv()
        lrr[pl.ds(u, 1)] = jnp.exp(span + lrr[u])[None]

    def entered(u, carry):
        remote(ebs, ebr.at[u], bsend.at[0], brecv.at[u], z=u).wait_recv()
        return lrr[u] * carry + ebr[u]

    cbs[...] = lax.fori_loop(0, z, entered, cbs[...])

    for w in range(4):
        wide = pl.ds(w * 256, 256)
        now = jnp.concatenate([cbs[k : k + 1, :] for k in (2 * w, 2 * w + 1)], axis=1)
        scenario = (acc[:, wide] + dd[:, wide] * now).astype(bf16)
        term = jnp.dot(scenario, bm[wide, :], preferred_element_type=f32)
        res[...] = term if w == 0 else res[...] + term

    base = jnp.zeros((8, LANES), f32)
    exponent = []
    for j in range(NX):
        run = jnp.zeros((8, LANES), f32)
        sums = []
        for i in range(8):
            run = run + (0.03 + 0.3 * res[pl.ds(j * DAYS + i * 8, 8), pl.ds(K, LANES)])
            sums.append(run)
        total = run
        for shift in (1, 2, 4):
            total = total + jnp.where(sub >= shift, pltpu.roll(total, shift, 0), 0.0)
        start = base + jnp.where(sub >= 1, pltpu.roll(total, 1, 0), 0.0)
        base = base + jnp.broadcast_to(total[7:8], (8, LANES))
        exponent += [(-1.0 / 256.0) * (start + s) for s in sums]
    top = functools.reduce(jnp.maximum, exponent)
    top = jnp.max(top, axis=0, keepdims=True)
    worth = jnp.zeros((8, LANES), f32)
    for n, power in enumerate(exponent):
        worth = worth + jnp.exp(power - top) * res[pl.ds(n * 8, 8), pl.ds(0, K)]
    fs[0:1, :] = jnp.sum(worth, axis=0, keepdims=True)
    low = lax.broadcasted_iota(jnp.int32, (1, LANES), 1) < LANES // 2
    fs[1:2, :] = jnp.where(low, base[0:1], top)
    mine = z * NX + x
    fr[pl.ds(mine, 1)] = fs[...][None]

    pl.semaphore_wait(met.at[3], NX - 1)
    def sums_to(zz, n):
        return remote(fs, fr.at[mine], fsend.at[0], frecv.at[0], z=zz, x=lax.rem(x + n, NX))

    for zz in range(NZ):
        for n in (2, 1, 3):
            sums_to(zz, n).start()

        @pl.when(zz != z)
        def _():
            sums_to(zz, 0).start()

    for copy in (*straight, *onward, *r_copies, *e_copies):
        copy.wait_send()
    for k in FAR_FIRST:
        later(k, lambda k: lr_copy(k).wait_send())
        later(k, lambda k: eb_copy(k).wait_send())
    others = fr.at[pl.ds(0, NZ * NX - 1)]
    everyone = remote(others, others, fsend.at[0], frecv.at[0], z=lax.rem(z + 1, NZ))
    everyone.wait_recv()
    passed = jnp.zeros((NX, LANES), f32)
    value = jnp.zeros((NX, LANES), f32)
    for u in range(NZ):
        part, both = (
            jnp.concatenate([fr[u * NX + j, r : r + 1] for j in range(NX)], axis=0) for r in range(2)
        )
        swapped = pltpu.roll(both, LANES // 2, 1)
        value = value + jnp.exp(jnp.where(low, swapped, both) - (1.0 / 256.0) * passed) * part
        passed = passed + jnp.where(low, both, swapped)
    out[...] = value * (1.0 / 4096.0)
    everyone.wait_send()


def local(e, s0, m, lp, reg, pay, sc):
    vmem, dma = pltpu.VMEM, pltpu.SemaphoreType.DMA
    return pl.pallas_call(
        kernel,
        out_shape=jax.ShapeDtypeStruct((PATHS, K), f32),
        in_specs=[pl.BlockSpec(memory_space=pl.ANY)] * 8,
        out_specs=pl.BlockSpec(memory_space=pltpu.VMEM),
        scratch_shapes=[
            vmem((DAYS, PATHS, F), bf16),
            vmem((PATHS, DAYS, F), bf16),
            vmem((NX, DAYS, F), bf16),
            vmem((F, F), bf16),
            vmem((F, 2 * K), bf16),
            vmem((BLOCK, F), f32),
            vmem((BLOCK, F), f32),
            vmem((BLOCK, 2 * K), f32),
            vmem((NX, 8, LANES), f32),
            vmem((BLOCK, LANES), f32),
            vmem((1, F), f32),
            vmem((8, LANES), f32),
            vmem((PATHS, F), f32),
            vmem((1, DAYS), f32),
            vmem((8, LANES), bf16),
            vmem((3, NX, 8, F), f32),
            vmem((NX, 8, F), f32),
            vmem((NX, 8, F), f32),
            vmem((NX, 8, F), f32),
            vmem((NX, 8, F), f32),
            vmem((8, LANES), f32),
            vmem((NZ, 8, LANES), f32),
            vmem((8, LANES), f32),
            vmem((NZ, 8, LANES), f32),
            vmem((8, LANES), f32),
            vmem((2, LANES), f32),
            vmem((NZ * NX, 2, LANES), f32),
            dma((17,)),
            dma((12 * HALF + 1,)), dma((12 * HALF + 1,)),
            dma((NY, NX)), dma((NY, NX)),
            dma((NX,)), dma((NX,)),
            dma((NZ,)), dma((NZ,)),
            dma((NZ,)), dma((NZ,)),
            dma((1,)), dma((1,)),
            pltpu.SemaphoreType.REGULAR((5,)),
        ],
        compiler_params=pltpu.CompilerParams(collective_id=0, has_side_effects=True, vmem_limit_bytes=32 << 20),
        name="scenarios",
    )(
        *(
            pltpu.with_memory_space_constraint(a, pltpu.HBM)
            for a in (e, s0, m, lp.reshape(1, F), lp.reshape(8, LANES), reg.reshape(1, DAYS), pay, sc.reshape(8, LANES))
        )
    )


def solution(mesh):
    split = Mesh(mesh.devices.reshape(NY, NC, NZ, NX), ("y", "c", "z", "x"))
    paths, days = ("y", "c"), ("z", "x")
    placed = (P(days, paths, None), P(paths, None), P(paths, None), P(), P(days), P(), P())
    return jax.shard_map(local, mesh=split, in_specs=placed, out_specs=P(paths, None), check_vma=False)
```
